32 devices in a mesh: seq: 8 (over y, x, core), head: 4 (over z).
Axes of the slice: x: 2, y: 2, z: 4, core: 2. Of those that a mesh axis runs over, the one named last changes fastest.
Arguments:
- queries: bfloat16 [6144, 5120], P('seq', 'head'), may hold values from -8000 to 8000
- keys: bfloat16 [6144, 5120], P('seq', 'head'), may hold values from -8000 to 8000
- values: bfloat16 [6144, 5120], P('seq', 'head'), may hold values from -6 to 6
- query_gain: float32 [5120], P('head'), may hold values from 0.1 to 1.9
- key_gain: float32 [5120], P('head'), may hold values from 0.1 to 1.9
- head_kind: int32 [40], P('head'), may hold values from 0 to 1, as said below
Outputs:
- attended: bfloat16 [6144, 5120], P('seq', 'head')
The draws below stay inside these ranges and needn't reach their ends.
Inputs may be any that keep to these rules, and one draw needn't show every extreme that they name: `head_kind`: among the heads h * 10 to (h + 1) * 10 - 1, for each h, exactly 2 are temporal.
All inputs are finite; a program needn't handle non-finite values.
Results may differ from the reference program's by a relative error of at most 0.011.
Values may be sent and summed in bfloat16 or wider, within the bound.
No kernel may reach another device: no remote copies, remote signals or barrier semaphores. Data moves between devices by JAX's collectives and lax.ppermute only.
A program may use at most 128 MiB of HBM per device.

```python
import math
import jax
import jax.numpy as jnp
from jax import lax

HEADS = 40
HEAD_DIM = 128
D = 5120
FRAME = 1024
OFFSET = 512
TOKENS = 6144
FRAMES = 6
HEADS_DEV = 10
TEMP_DEV = 2


def scale_table(key, row_top):
    row_key, col_key = jax.random.split(key)
    rows = jnp.exp(jax.random.uniform(row_key, (TOKENS, 1), jnp.float32, 0.0, math.log(row_top)))
    head = (jnp.arange(D) // HEAD_DIM).astype(jnp.float32)
    cols = 10.0 ** (0.75 * head / (HEADS - 1)) * jax.random.uniform(col_key, (D,), jnp.float32, 0.7, 1.4)
    return rows * cols[None, :]


def entries(key):
    first = jax.random.fold_in(key, 0)
    third = jax.random.fold_in(key, 2)
    base = jax.random.truncated_normal(first, -4.0, 4.0, (TOKENS, D), jnp.float32)
    return base * scale_table(third, 10.0)


def draw_keys(key, part):
    return entries(jax.random.fold_in(key, 2)).astype(jnp.bfloat16)


def draw_queries(key, part):
    base = entries(jax.random.fold_in(key, 1))
    return base.astype(jnp.bfloat16)


def draw_head_kind(key, part):
    scores = jax.random.randint(key, (HEADS,), 0, 2 ** 20) * HEADS + jnp.arange(HEADS)
    groups = scores.reshape(HEADS // HEADS_DEV, HEADS_DEV)
    ranks = jnp.argsort(jnp.argsort(groups, axis=1), axis=1)
    return (ranks < TEMP_DEV).astype(jnp.int32).reshape(HEADS)


def levels(stream_key, extent, cuts, least, high):
    factor_of, own = 1.0, jax.random.fold_in(stream_key, 6)
    for axis_at, parts in cuts:
        steps = jnp.exp(jax.random.uniform(jax.random.fold_in(own, axis_at), (parts,), jnp.float32, least / len(cuts), high / len(cuts)))
        factor_of = factor_of * jnp.repeat(steps, extent[axis_at] // parts).reshape([-1 if axis == axis_at else 1 for axis in range(len(extent))])
    return factor_of


def gaussian(key, shape, deviation, reach, cuts=(), held_as=jnp.bfloat16):
    factor_of = levels(key, shape, cuts, -0.22, 0.18) if cuts else 1.0
    array = jax.random.normal(key, shape, jnp.float32) * deviation * factor_of
    return jnp.minimum(jnp.maximum(array, -reach), reach).astype(held_as)


def setup_inputs(seed: int = 0) -> dict:
    splits = jax.random.split(jax.random.key(seed), 7)
    queries = draw_queries(jax.random.fold_in(splits[6], 71), 0)
    keys = draw_keys(jax.random.fold_in(splits[6], 71), 0)
    values = gaussian(splits[2], (TOKENS, D), 1.0, 6.0, ((0, 8), (1, 4)))
    query_gain = jnp.clip(1.0 + 0.18 * jax.random.normal(splits[3], (D,), jnp.float32), 0.1, 1.9)
    key_gain = jnp.clip(1.0 + 0.18 * jax.random.normal(splits[4], (D,), jnp.float32), 0.1, 1.9)
    head_kind = draw_head_kind(jax.random.fold_in(splits[6], 71), 0)
    return {"queries": queries, "keys": keys, "values": values, "query_gain": query_gain, "key_gain": key_gain, "head_kind": head_kind}


def normalize(rows, gain):
    wide = rows.astype(jnp.float32)
    sums = lax.optimization_barrier(jnp.sum(wide * wide, axis=1, keepdims=True))
    return (wide * lax.rsqrt(sums / D + 1e-06) * gain[None, :]).astype(jnp.bfloat16)

def softmax_rows(scores):
    top = lax.optimization_barrier(jnp.max(scores, axis=-1, keepdims=True))
    expo = jnp.exp(scores - top)
    return expo / lax.optimization_barrier(jnp.sum(expo, axis=-1, keepdims=True))

def reference(queries, keys, values, query_gain, key_gain, head_kind):
    factor = HEAD_DIM ** (-0.5)
    q_norm = jnp.roll(normalize(queries, query_gain), OFFSET, axis=0).reshape(FRAMES, FRAME, HEADS, HEAD_DIM)
    k_norm = jnp.roll(normalize(keys, key_gain), OFFSET, axis=0).reshape(FRAMES, FRAME, HEADS, HEAD_DIM)
    v_all = jnp.roll(values, OFFSET, axis=0).reshape(FRAMES, FRAME, HEADS, HEAD_DIM)

    def one_frame(items):
        q_frame, k_frame, v_frame = items
        scores = jnp.einsum('qhd,khd->hqk', q_frame.astype(jnp.float32), k_frame.astype(jnp.float32)) * factor
        weights = softmax_rows(scores).astype(jnp.bfloat16)
        return jnp.einsum('hqk,khd->qhd', weights.astype(jnp.float32), v_frame.astype(jnp.float32)).astype(jnp.bfloat16)
    spatial = lax.map(one_frame, (q_norm, k_norm, v_all))
    scores = jnp.einsum('fphd,gphd->phfg', q_norm.astype(jnp.float32), k_norm.astype(jnp.float32)) * factor
    weights = softmax_rows(scores)
    temporal = jnp.einsum('phfg,gphd->fphd', weights, v_all.astype(jnp.float32)).astype(jnp.bfloat16)
    chosen = (head_kind == 1)[None, None, :, None]
    video = jnp.where(chosen, temporal, spatial).reshape(TOKENS, D)
    return jnp.roll(video, -OFFSET, axis=0)
```

```python
import functools
import math

import jax
import jax.numpy as jnp
from jax import lax
from jax.experimental import pallas as pl
from jax.experimental.pallas import tpu as pltpu
from jax.sharding import PartitionSpec as P

HEAD_DIM = 128
D = 5120
FRAME = 1024
OFFSET = 512
CHUNKS = 2
VMEM = 48 * 1024 * 1024
LOW = -1e30
FACTOR = math.log2(math.e) / math.sqrt(HEAD_DIM)
F32 = jnp.float32
BF16 = jnp.bfloat16


def cost(flops, moved, exps=0):
    return pl.CostEstimate(flops=flops, bytes_accessed=moved, transcendentals=exps)


def params():
    return pltpu.CompilerParams(vmem_limit_bytes=VMEM)


def permuted(block, axis, route):
    return lax.ppermute(block, axis, route)


def shape(dims, dtype=BF16):
    return jax.ShapeDtypeStruct(dims, dtype)


def meta_of(head_kind, index, heads, spatial, temporal):
    is_temporal = head_kind == 1
    place = jnp.arange(heads, dtype=jnp.int32)
    before = jnp.sum(
        jnp.where((place[None, :] < place[:, None]) & is_temporal[None, :], 1, 0), axis=1
    ).astype(jnp.int32)
    turn = index % 2 if temporal == 2 else 0
    rank = jnp.where(is_temporal, spatial + (before ^ turn), place - before)
    order = jnp.sum(jnp.where(rank[None, :] == place[:, None], place[None, :], 0), axis=1)
    own = jnp.stack([index % 4, index % 2, index // 2])
    return jnp.concatenate([order, own]).astype(jnp.int32)


def cross_start(meta, heads, block):
    return pl.multiple_of(jnp.where(meta[heads] == 0, 0, block), block)


def sums_kernel(heads, spatial, block, meta, q_ref, k_ref, v_ref, sums_ref, vs_ref, vx_ref, sq_q, sq_k):
    h = pl.program_id(0)
    q = q_ref[...].astype(F32)
    k = k_ref[...].astype(F32)

    @pl.when(h == 0)
    def _():
        sq_q[...] = q * q
        sq_k[...] = k * k

    @pl.when(h > 0)
    def _():
        sq_q[...] += q * q
        sq_k[...] += k * k

    @pl.when(h < spatial)
    def _():
        vs_ref[0] = v_ref[...]
        vx_ref[0] = v_ref[pl.ds(cross_start(meta, heads, block), 2 * block), :]

    @pl.when(h == heads - 1)
    def _():
        ones = jnp.ones((8, HEAD_DIM), F32)
        for i, acc in enumerate((sq_q, sq_k)):
            total = lax.dot_general(
                ones,
                acc[...],
                (((1,), (1,)), ((), ())),
                precision=lax.Precision.HIGHEST,
                preferred_element_type=F32,
            )
            sums_ref[i : i + 1, :] = total[0:1, :]


def sums_call(meta, queries, keys, values, heads, spatial, block):
    rows = queries.shape[0]
    last = spatial - 1
    column = lambda h, m: (0, m[h])
    column_v = lambda h, m: (0, m[jnp.minimum(h, last)])
    by_head = lambda h, m: (jnp.minimum(h, last), 0, 0)
    one = (rows, HEAD_DIM)
    return pl.pallas_call(
        functools.partial(sums_kernel, heads, spatial, block),
        grid_spec=pltpu.PrefetchScalarGridSpec(
            num_scalar_prefetch=1,
            grid=(heads,),
            in_specs=[pl.BlockSpec(one, column), pl.BlockSpec(one, column), pl.BlockSpec(one, column_v)],
            out_specs=[
                pl.BlockSpec((2, rows), lambda h, m: (0, 0)),
                pl.BlockSpec((1,) + one, by_head),
                pl.BlockSpec((1, 2 * block, HEAD_DIM), by_head),
            ],
            scratch_shapes=[pltpu.VMEM(one, F32), pltpu.VMEM(one, F32)],
        ),
        out_shape=[
            shape((2, rows), F32),
            shape((spatial, rows, HEAD_DIM)),
            shape((spatial, 2 * block, HEAD_DIM)),
        ],
        compiler_params=params(),
        cost_estimate=cost(6 * queries.size, 10 * queries.size),
        name="sums",
    )(meta, queries, keys, values)


def norm_kernel(heads, spatial, block, parts, meta, q_ref, k_ref, v_ref, gq_ref, gk_ref, *refs):
    sums, refs = refs[:parts], refs[parts:]
    qs_ref, ks_ref = refs[:2]
    kx_refs = refs[2 : 2 + CHUNKS]
    t_refs = refs[2 + CHUNKS : -2]
    scale_q, scale_k = refs[-2:]
    h = pl.program_id(0)
    rows = q_ref.shape[0]

    @pl.when(h == 0)
    def _():
        total = sums[0][...]
        for other in sums[1:]:
            total = total + other[...]
        inverse = lax.rsqrt(total / D + 1e-06)
        for i, into in enumerate((scale_q, scale_k)):
            into[...] = jnp.transpose(jnp.broadcast_to(inverse[i : i + 1, :], (HEAD_DIM, rows)))

    q = (q_ref[...].astype(F32) * scale_q[...] * (gq_ref[...] * FACTOR)).astype(BF16)
    k = (k_ref[...].astype(F32) * scale_k[...] * gk_ref[...]).astype(BF16)

    @pl.when(h < spatial)
    def _():
        qs_ref[0] = q
        ks_ref[0] = k

    each = spatial // CHUNKS
    for c in range(CHUNKS):

        @pl.when((h >= c * each) & (h < (c + 1) * each))
        def _():
            kx_refs[c][0] = ks_ref[0, pl.ds(cross_start(meta, heads, block), 2 * block), :]

    for j, t_ref in enumerate(t_refs):

        @pl.when(h == spatial + j)
        def _():
            t_ref[0] = q
            t_ref[1] = k
            t_ref[2] = v_ref[...]


def norm_call(meta, queries, keys, values, query_gain, key_gain, sums, heads, spatial, block):
    rows = queries.shape[0]
    last = spatial - 1
    each = spatial // CHUNKS
    temporal = heads - spatial
    one = (rows, HEAD_DIM)
    column = lambda h, m: (0, m[h])
    column_v = lambda h, m: (0, m[jnp.maximum(h, spatial)])
    by_head = lambda h, m: (jnp.minimum(h, last), 0, 0)
    whole = lambda h, m: (0, 0)

    def by_chunk(c):
        return lambda h, m: (jnp.clip(h - c * each, 0, each - 1), 0, 0)

    return pl.pallas_call(
        functools.partial(norm_kernel, heads, spatial, block, len(sums)),
        grid_spec=pltpu.PrefetchScalarGridSpec(
            num_scalar_prefetch=1,
            grid=(heads,),
            in_specs=[
                pl.BlockSpec(one, column),
                pl.BlockSpec(one, column),
                pl.BlockSpec(one, column_v),
                pl.BlockSpec((1, HEAD_DIM), column),
                pl.BlockSpec((1, HEAD_DIM), column),
            ]
            + [pl.BlockSpec((2, rows), whole)] * len(sums),
            out_specs=[pl.BlockSpec((1,) + one, by_head)] * 2
            + [pl.BlockSpec((1, 2 * block, HEAD_DIM), by_chunk(c)) for c in range(CHUNKS)]
            + [pl.BlockSpec((3,) + one, lambda h, m: (0, 0, 0))] * temporal,
            scratch_shapes=[pltpu.VMEM(one, F32), pltpu.VMEM(one, F32)],
        ),
        out_shape=[shape((spatial,) + one)] * 2
        + [shape((each, 2 * block, HEAD_DIM))] * CHUNKS
        + [shape((3,) + one)] * temporal,
        compiler_params=params(),
        cost_estimate=cost(10 * queries.size, 12 * queries.size),
        name="norms",
    )(meta, queries, keys, values, query_gain.reshape(1, -1), key_gain.reshape(1, -1), *sums)


def attend(query, parts):
    scores = [
        lax.dot_general(query, k, (((1,), (1,)), ((), ())), preferred_element_type=F32)
        for k, _ in parts
    ]
    top = functools.reduce(jnp.maximum, [jnp.max(s, axis=1, keepdims=True) for s in scores])
    total = None
    for s, (_, v) in zip(scores, parts):
        wide = jnp.concatenate([v, jnp.ones_like(v)], axis=1)
        part = jnp.dot(jnp.exp2(s - top).astype(BF16), wide, preferred_element_type=F32)
        total = part if total is None else total + part
    return (total[:, :HEAD_DIM] / total[:, HEAD_DIM:]).astype(BF16)


def near_kernel(heads, block, meta, q_ref, k_ref, v_ref, kp_ref, vp_ref, o_ref):
    kind = meta[heads]
    apart = pl.multiple_of(jnp.where((kind == 0) | (kind == 1), 2 * block, 0), block)
    one = pl.ds(apart, block)

    @pl.when((kind == 1) | (kind == 2))
    def _():
        for part in range(3):
            rows = pl.ds(part * block, block)
            o_ref[rows, :] = attend(
                q_ref[0, rows, :],
                [(k_ref[0], v_ref[0]), (kp_ref[0, one, :], vp_ref[0, one, :])],
            )

    @pl.when((kind == 0) | (kind == 3))
    def _():
        o_ref[one, :] = attend(
            q_ref[0, one, :],
            [(kp_ref[0], vp_ref[0]), (k_ref[0, one, :], v_ref[0, one, :])],
        )


def near_call(meta, q, k, v, k_pair, v_pair, heads, block):
    spatial, rows, _ = q.shape
    by_head = pl.BlockSpec((1, rows, HEAD_DIM), lambda h, m: (h, 0, 0))
    pairs = spatial * rows * 4 * block
    return pl.pallas_call(
        functools.partial(near_kernel, heads, block),
        grid_spec=pltpu.PrefetchScalarGridSpec(
            num_scalar_prefetch=1,
            grid=(spatial,),
            in_specs=[by_head] * 5,
            out_specs=pl.BlockSpec((rows, HEAD_DIM), lambda h, m: (0, m[h])),
        ),
        out_shape=shape((rows, heads * HEAD_DIM)),
        compiler_params=params(),
        cost_estimate=cost(4 * pairs * HEAD_DIM, 12 * q.size, pairs),
        name="near",
    )(meta, q, k, v, k_pair, v_pair)


def far_kernel(heads, block, meta, q_ref, k_ref, v_ref, kx_ref, vx_ref, have_ref, o_ref):
    kind = meta[heads]
    start = cross_start(meta, heads, block)
    o_ref[...] = have_ref[...]

    @pl.when((kind == 0) | (kind == 3))
    def _():
        own = pl.ds(start, 2 * block)
        for part in range(2):
            rows = pl.ds(pl.multiple_of(start + part * block, block), block)
            o_ref[rows, :] = attend(
                q_ref[0, rows, :],
                [(k_ref[0, own, :], v_ref[0, own, :]), (kx_ref[0], vx_ref[0])],
            )


def far_call(meta, q, k, v, k_cross, v_cross, have, first, heads, block):
    rows = q.shape[1]
    count = k_cross.shape[0]
    by_head = pl.BlockSpec((1, rows, HEAD_DIM), lambda h, m: (h + first, 0, 0))
    column = pl.BlockSpec((rows, HEAD_DIM), lambda h, m: (0, m[h + first]))
    pairs = count * 2 * block * 4 * block
    return pl.pallas_call(
        functools.partial(far_kernel, heads, block),
        grid_spec=pltpu.PrefetchScalarGridSpec(
            num_scalar_prefetch=1,
            grid=(count,),
            in_specs=[
                by_head,
                by_head,
                by_head,
                pl.BlockSpec((1, 2 * block, HEAD_DIM), lambda h, m: (h, 0, 0)),
                pl.BlockSpec((1, 2 * block, HEAD_DIM), lambda h, m: (h + first, 0, 0)),
                column,
            ],
            out_specs=column,
        ),
        out_shape=shape(have.shape),
        input_output_aliases={6: 0},
        compiler_params=params(),
        cost_estimate=cost(4 * pairs * HEAD_DIM, 14 * count * rows * HEAD_DIM, pairs),
        name="far",
    )(meta, q, k, v, k_cross, v_cross, have)


def place_kernel(meta, *refs):
    parts, o_ref = refs[:-2], refs[-1]
    j = pl.program_id(0)
    for i, part in enumerate(parts):

        @pl.when(j == i)
        def _():
            o_ref[...] = part[...]


def place_call(meta, parts, have, spatial):
    rows = have.shape[0]
    count = len(parts)
    return pl.pallas_call(
        place_kernel,
        grid_spec=pltpu.PrefetchScalarGridSpec(
            num_scalar_prefetch=1,
            grid=(count,),
            in_specs=[pl.BlockSpec((rows, HEAD_DIM), lambda j, m: (0, 0))] * count
            + [pl.BlockSpec(memory_space=pl.ANY)],
            out_specs=pl.BlockSpec((rows, HEAD_DIM), lambda j, m: (0, m[spatial + j])),
        ),
        out_shape=shape(have.shape),
        input_output_aliases={1 + count: 0},
        compiler_params=params(),
        cost_estimate=cost(0, 4 * count * rows * HEAD_DIM),
        name="place",
    )(meta, *parts, have)


PIECE = 128
CHIPS = 4
TURNS = 3


def deal_kernel(heads, meta, keep_ref, got_ref, *refs):
    outs, held, sems = refs[:CHIPS], refs[CHIPS], refs[CHIPS + 1]
    core = meta[heads + 1]
    chip = meta[heads + 2]
    rows = keep_ref.shape[1]
    ins = [
        pltpu.make_async_copy(
            ref, held.at[:, pl.ds(pl.multiple_of(at * rows, rows), rows), :], sems.at[i]
        )
        for i, (ref, at) in enumerate(((keep_ref, core), (got_ref, 1 - core)))
    ]
    for copy in ins:
        copy.start()
    for copy in ins:
        copy.wait()
    copies = []
    for turn in range(CHIPS):
        owner = chip ^ turn
        for g in range(TURNS):
            at = pl.multiple_of((owner + CHIPS * g) * PIECE, PIECE)
            copies.append(
                pltpu.make_async_copy(
                    held.at[:, pl.ds(at, PIECE), :],
                    outs[turn].at[:, g],
                    sems.at[2 + turn * TURNS + g],
                )
            )
    for copy in copies:
        copy.start()
    for copy in copies:
        copy.wait()


def deal_call(meta, keep, got, heads):
    return pl.pallas_call(
        functools.partial(deal_kernel, heads),
        in_specs=[pl.BlockSpec(memory_space=pltpu.SMEM)] + [pl.BlockSpec(memory_space=pl.ANY)] * 2,
        out_specs=[pl.BlockSpec(memory_space=pl.ANY)] * CHIPS,
        out_shape=[shape((3, TURNS, PIECE, HEAD_DIM))] * CHIPS,
        scratch_shapes=[
            pltpu.VMEM((3, 2 * keep.shape[1], HEAD_DIM), BF16),
            pltpu.SemaphoreType.DMA((2 + CHIPS * TURNS,)),
        ],
        compiler_params=params(),
        cost_estimate=cost(0, 8 * keep.size),
        name="deal",
    )(meta, keep, got)


def gather_kernel(heads, meta, *refs):
    ins, (keep_ref, send_ref, held, sems) = refs[:CHIPS], refs[CHIPS:]
    core = meta[heads + 1]
    chip = meta[heads + 2]
    pieces = CHIPS * TURNS // 2
    copies = []
    for turn in range(CHIPS):
        owner = chip ^ turn
        for g in range(TURNS):
            copies.append(
                pltpu.make_async_copy(
                    ins[turn].at[g], held.at[owner + CHIPS * g], sems.at[turn * TURNS + g]
                )
            )
    for copy in copies:
        copy.start()
    for copy in copies:
        copy.wait()
    outs = [
        pltpu.make_async_copy(held.at[pl.ds(at * pieces, pieces)], ref, sems.at[i])
        for i, (ref, at) in enumerate(((keep_ref, core), (send_ref, 1 - core)))
    ]
    for copy in outs:
        copy.start()
    for copy in outs:
        copy.wait()


def gather_call(meta, parts, heads):
    pieces = CHIPS * TURNS // 2
    return pl.pallas_call(
        functools.partial(gather_kernel, heads),
        in_specs=[pl.BlockSpec(memory_space=pltpu.SMEM)]
        + [pl.BlockSpec(memory_space=pl.ANY)] * CHIPS,
        out_specs=[pl.BlockSpec(memory_space=pl.ANY)] * 2,
        out_shape=[shape((pieces, PIECE, HEAD_DIM))] * 2,
        scratch_shapes=[
            pltpu.VMEM((2 * pieces, PIECE, HEAD_DIM), BF16),
            pltpu.SemaphoreType.DMA((CHIPS * TURNS,)),
        ],
        compiler_params=params(),
        cost_estimate=cost(0, 8 * pieces * PIECE * HEAD_DIM),
        name="gather",
    )(meta, *parts)


GROUPS = (
    ((0, 1), (2, 1), (1, 0), (1, 2), (3, 0), (3, 2)),
    ((0, 0), (0, 2), (2, 0), (2, 2), (1, 1), (3, 1)),
)


def frames_kernel(*refs):
    ins, outs = refs[:CHIPS], refs[CHIPS:]
    row = lax.broadcasted_iota(jnp.int32, (PIECE, PIECE), 0)
    col = lax.broadcasted_iota(jnp.int32, (PIECE, PIECE), 1)
    off = jnp.where(row == col, 0.0, LOW)
    for group in GROUPS:
        key = jnp.concatenate([ins[s][1, g] for s, g in group], axis=0)
        value = jnp.concatenate([ins[s][2, g] for s, g in group], axis=0)
        wide = jnp.concatenate([value, jnp.ones_like(value)], axis=1)
        mask = jnp.concatenate([off] * len(group), axis=1)
        for s, g in group:
            scores = (
                lax.dot_general(
                    ins[s][0, g], key, (((1,), (1,)), ((), ())), preferred_element_type=F32
                )
            )
            scores = jnp.where(mask == 0.0, scores, LOW)
            top = jnp.max(scores, axis=1, keepdims=True)
            weights = jnp.exp2(scores - top).astype(BF16)
            total = jnp.dot(weights, wide, preferred_element_type=F32)
            outs[s][g] = (total[:, :HEAD_DIM] / total[:, HEAD_DIM:]).astype(BF16)


def frames_call(parts):
    size = TURNS * PIECE * HEAD_DIM
    return pl.pallas_call(
        frames_kernel,
        in_specs=[pl.BlockSpec(memory_space=pltpu.VMEM)] * CHIPS,
        out_specs=[pl.BlockSpec(memory_space=pltpu.VMEM)] * CHIPS,
        out_shape=[shape((TURNS, PIECE, HEAD_DIM))] * CHIPS,
        compiler_params=params(),
        cost_estimate=cost(4 * 12 * PIECE * 6 * PIECE * HEAD_DIM, 32 * size, 72 * PIECE * PIECE),
        name="frames",
    )(*parts)


def temporal_dealt(meta, keep, send, heads, devices):
    pair = [(i, i ^ 1) for i in range(devices)]
    routes = [[(i, i ^ (2 * turn)) for i in range(devices)] for turn in range(1, CHIPS)]
    got = permuted(send, "seq", pair)
    dealt = deal_call(meta, keep, got, heads)
    arrived = [dealt[0]] + [permuted(p, "seq", r) for p, r in zip(dealt[1:], routes)]
    results = frames_call(arrived)
    back = [results[0]] + [permuted(p, "seq", r) for p, r in zip(results[1:], routes)]
    own, other = gather_call(meta, back, heads)
    other = permuted(other, "seq", pair)
    return [own.reshape(-1, HEAD_DIM), other.reshape(-1, HEAD_DIM)]


def temporal_folded(parts, first):
    rows = parts[0].shape[1]
    stacked = jnp.stack(parts, axis=2).astype(F32)
    query = stacked[0]
    flat = jnp.stack(parts, axis=2).astype(BF16)
    count = len(parts)
    key_all = lax.all_gather(flat[1].reshape(rows, -1), "seq", axis=0, tiled=True)
    value_all = lax.all_gather(flat[2].reshape(rows, -1), "seq", axis=0, tiled=True)
    place = (first + jnp.arange(rows, dtype=jnp.int32)) % FRAME
    running = jnp.full((rows, count), LOW, F32)
    total = jnp.zeros((rows, count), F32)
    summed = jnp.zeros((rows, count, HEAD_DIM), F32)
    for step in range(key_all.shape[0] // FRAME):
        at = place + step * FRAME
        key = jnp.take(key_all, at, axis=0).reshape(rows, count, HEAD_DIM).astype(F32)
        value = jnp.take(value_all, at, axis=0).reshape(rows, count, HEAD_DIM).astype(F32)
        scores = jnp.sum(query * key, axis=2)
        newest = jnp.maximum(running, scores)
        shrink = jnp.exp2(running - newest)
        weight = jnp.exp2(scores - newest)
        total = total * shrink + weight
        summed = summed * shrink[:, :, None] + weight[:, :, None] * value
        running = newest
    done = (summed / total[:, :, None]).astype(BF16)
    return [done[:, j] for j in range(count)]


def per_device(queries, keys, values, query_gain, key_gain, head_kind):
    rows = queries.shape[0]
    heads = head_kind.shape[0]
    temporal = heads // 5
    spatial = heads - temporal
    block = rows // 3
    devices = lax.axis_size("seq")
    parts = lax.axis_size("head")
    index = lax.axis_index("seq").astype(jnp.int32)
    pair = [(i, i ^ 1) for i in range(devices)]
    cross = []
    for i in range(3, devices, 4):
        after = (i + 1) % devices
        cross += [(i, after), (after, i)]

    meta = meta_of(head_kind, index, heads, spatial, temporal)
    sums, v, v_near = sums_call(meta, queries, keys, values, heads, spatial, block)
    all_sums = [sums] + [
        permuted(sums, "head", [(i, (i + d) % parts) for i in range(parts)])
        for d in range(1, parts)
    ]
    v_cross = permuted(v_near, "seq", cross)
    v_pair = permuted(v, "seq", pair)
    q, k, *rest = norm_call(
        meta, queries, keys, values, query_gain, key_gain, all_sums, heads, spatial, block
    )
    k_near, t_parts = rest[:CHUNKS], rest[CHUNKS:]
    k_pair = permuted(k, "seq", pair)
    k_cross = [permuted(part, "seq", cross) for part in k_near]
    if temporal == 2 and devices == 2 * CHIPS and rows == 6 * PIECE:
        t_out = temporal_dealt(meta, t_parts[0], t_parts[1], heads, devices)
    else:
        t_out = temporal_folded(t_parts, index * rows)
    out = near_call(meta, q, k, v, k_pair, v_pair, heads, block)
    for c, part in enumerate(k_cross):
        first = c * part.shape[0]
        out = far_call(meta, q, k, v, part, v_cross, out, first, heads, block)
    return place_call(meta, t_out, out, spatial)


def solution(mesh):
    placed = (P("seq", "head"), P("seq", "head"), P("seq", "head"), P("head"), P("head"), P("head"))
    return jax.shard_map(
        per_device, mesh=mesh, in_specs=placed, out_specs=P("seq", "head"), check_vma=False
    )
```

```python
import functools
import math

import jax
import jax.numpy as jnp
from jax import lax
from jax.experimental import pallas as pl
from jax.experimental.pallas import tpu as pltpu
from jax.sharding import PartitionSpec as P

HEAD_DIM = 128
D = 5120
FRAME = 1024
OFFSET = 512
CHUNKS = 2
UNROLL = 4
VMEM = 64 * 1024 * 1024
LOW = -1e30
FACTOR = math.log2(math.e) / math.sqrt(HEAD_DIM)
F32 = jnp.float32
BF16 = jnp.bfloat16
ANY = pl.BlockSpec(memory_space=pl.ANY)
IN_SMEM = pl.BlockSpec(memory_space=pltpu.SMEM)
IN_VMEM = pl.BlockSpec(memory_space=pltpu.VMEM)


def shape(dims, dtype=BF16):
    return jax.ShapeDtypeStruct(dims, dtype)


def call(kernel, name, out_shape, in_specs, out_specs, scratch, operands, aliases=None):
    return pl.pallas_call(
        kernel,
        out_shape=out_shape,
        in_specs=in_specs,
        out_specs=out_specs,
        scratch_shapes=scratch,
        input_output_aliases=aliases or {},
        compiler_params=pltpu.CompilerParams(vmem_limit_bytes=VMEM),
        cost_estimate=pl.CostEstimate(flops=1000, bytes_accessed=1000, transcendentals=0),
        name=name,
    )(*operands)


def column(ref, head, rows=None):
    lanes = pl.ds(pl.multiple_of(head * HEAD_DIM, HEAD_DIM), HEAD_DIM)
    return ref.at[:, lanes] if rows is None else ref.at[rows, lanes]


def put_order(kind_ref, order_ref, spatial):
    heads = kind_ref.shape[0]

    def step(h, count):
        s, t = count
        temporal = kind_ref[h] == 1
        order_ref[jnp.where(temporal, spatial + t, s)] = h
        return jnp.where(temporal, s, s + 1), jnp.where(temporal, t + 1, t)

    lax.fori_loop(0, heads, step, (jnp.int32(0), jnp.int32(0)))


def order_scratch(heads):
    return pltpu.SMEM((heads,), jnp.int32)


class Place:
    def __init__(self, block):
        index = lax.axis_index("seq").astype(jnp.int32)
        self.kind = index % 4
        self.core = index % 2
        self.chip = index // 2
        self.inner = (self.kind == 1) | (self.kind == 2)
        self.apart = jnp.where((self.kind == 0) | (self.kind == 1), 2 * block, 0)
        self.near = jnp.where(self.kind == 0, 2 * block, 0)
        self.far = jnp.where(self.kind == 0, 0, block)
        self.cross = jnp.where(self.kind == 0, 0, block)


def start_all(copies):
    for copy in copies:
        copy.start()


def wait_all(copies):
    for copy in copies:
        copy.wait()


def first_kernel(spatial, block, dealt, kind_ref, q_ref, k_ref, v_ref, sums_ref, vx_ref, *refs):
    order, held, squares, v_buf, t_buf, sums, sems, v_sems, t_sems = refs[-9:]
    put_order(kind_ref, order, spatial)
    place = Place(block)
    rows, width = q_ref.shape
    steps = held.shape[1]
    size = rows // steps
    across = pl.ds(pl.multiple_of(place.cross, block), 2 * block)
    v_in = [
        pltpu.make_async_copy(column(v_ref, order[h], across), v_buf.at[h], v_sems.at[0, h])
        for h in range(spatial)
    ]
    v_out = [
        pltpu.make_async_copy(v_buf.at[h], vx_ref.at[h], v_sems.at[1, h]) for h in range(spatial)
    ]
    t_in = []
    t_out = []
    if dealt:
        head = order[spatial + 1 - place.core]
        t_in = [
            pltpu.make_async_copy(column(ref, head), t_buf.at[i], t_sems.at[i])
            for i, ref in enumerate((q_ref, k_ref, v_ref))
        ]
        t_out = [pltpu.make_async_copy(t_buf, refs[0], t_sems.at[3])]
    copies = [
        [
            pltpu.make_async_copy(ref.at[pl.ds(s * size, size), :], held.at[i, s], sems.at[i, s])
            for s in range(steps)
        ]
        for i, ref in enumerate((q_ref, k_ref))
    ]
    start_all(t_in)
    start_all(v_in)
    for line in copies:
        start_all(line)
    wait_all(t_in)
    start_all(t_out)
    for h in range(spatial):
        v_in[h].wait()
        v_out[h].start()
    for i in range(2):
        for s in range(steps):
            copies[i][s].wait()
            total = None
            for c in range(width // HEAD_DIM):
                x = held[i, s, :, c * HEAD_DIM : (c + 1) * HEAD_DIM].astype(F32)
                total = x * x if total is None else total + x * x
            squares[s * size : (s + 1) * size, :] = total
        row = lax.dot_general(
            jnp.ones((8, HEAD_DIM), F32),
            squares[...],
            (((1,), (1,)), ((), ())),
            precision=lax.Precision.HIGHEST,
            preferred_element_type=F32,
        )
        sums[i : i + 1, :] = row[0:1, :]
    out = pltpu.make_async_copy(sums, sums_ref, t_sems.at[4])
    out.start()
    wait_all(t_out + v_out + [out])


def first_call(head_kind, queries, keys, values, spatial, block, dealt):
    rows, width = queries.shape
    steps = 6
    outs = [shape((2, rows), F32), shape((spatial, 2 * block, HEAD_DIM))]
    if dealt:
        outs.append(shape((3, rows, HEAD_DIM)))
    return call(
        functools.partial(first_kernel, spatial, block, dealt),
        "first",
        outs,
        [IN_SMEM, ANY, ANY, ANY],
        [ANY] * len(outs),
        [
            order_scratch(head_kind.shape[0]),
            pltpu.VMEM((2, steps, rows // steps, width), BF16),
            pltpu.VMEM((rows, HEAD_DIM), F32),
            pltpu.VMEM((spatial, 2 * block, HEAD_DIM), BF16),
            pltpu.VMEM((3, rows, HEAD_DIM), BF16),
            pltpu.VMEM((2, rows), F32),
            pltpu.SemaphoreType.DMA((2, steps)),
            pltpu.SemaphoreType.DMA((2, spatial)),
            pltpu.SemaphoreType.DMA((5,)),
        ],
        (head_kind, queries, keys, values),
    )


def small_scratch(*operands):
    return [pltpu.VMEM(x.shape, F32) for x in operands] + [
        pltpu.SemaphoreType.DMA((len(operands),))
    ]


def small_copies(sources, scratch):
    return [
        pltpu.make_async_copy(ref, buf, scratch[-1].at[i])
        for i, (ref, buf) in enumerate(zip(sources, scratch[:-1]))
    ]


def row_factors(total_ref, which, start, size):
    sums = total_ref[which : which + 1, pl.ds(start, size)]
    inverse = lax.rsqrt(sums / D + 1e-06)
    return jnp.transpose(jnp.broadcast_to(inverse, (HEAD_DIM, size)))


def gain_of(gain_ref, head):
    gain = gain_ref[pl.ds(pl.multiple_of(head * HEAD_DIM, HEAD_DIM), HEAD_DIM)]
    return jnp.broadcast_to(gain[None, :], (8, HEAD_DIM))[0:1, :]


def keys_kernel(spatial, block, kind_ref, k_ref, gain_any, total_any, after_ref, after_too, *refs):
    ks_ref, kx_refs = refs[0], refs[1 : 1 + CHUNKS]
    order, held, done, factors, sems, *small = refs[1 + CHUNKS :]
    gain_ref, total_ref = small[:2]
    smalls = small_copies((gain_any, total_any), small)
    start_all(smalls)
    put_order(kind_ref, order, spatial)
    place = Place(block)
    rows = k_ref.shape[0]
    ins = [
        pltpu.make_async_copy(column(k_ref, order[h]), held.at[h], sems.at[0, h])
        for h in range(spatial)
    ]
    start_all(ins)
    wait_all(smalls)
    factors[...] = row_factors(total_ref, 1, 0, rows)
    each = spatial // CHUNKS
    own = pl.ds(pl.multiple_of(place.cross, block), 2 * block)
    outs = []
    for h in range(spatial):
        ins[h].wait()
        done[h] = (held[h].astype(F32) * factors[...] * gain_of(gain_ref, order[h])).astype(BF16)
        outs.append(pltpu.make_async_copy(done.at[h], ks_ref.at[h], sems.at[1, h]))
        outs.append(
            pltpu.make_async_copy(
                done.at[h, own], kx_refs[h // each].at[h % each], sems.at[2, h]
            )
        )
        start_all(outs[-2:])
    wait_all(outs)


def keys_call(head_kind, keys, gain, total, after, after_too, spatial, block):
    rows = keys.shape[0]
    each = spatial // CHUNKS
    one = (spatial, rows, HEAD_DIM)
    return call(
        functools.partial(keys_kernel, spatial, block),
        "keys",
        [shape(one)] + [shape((each, 2 * block, HEAD_DIM))] * CHUNKS,
        [IN_SMEM] + [ANY] * 5,
        [ANY] * (1 + CHUNKS),
        [
            order_scratch(head_kind.shape[0]),
            pltpu.VMEM(one, BF16),
            pltpu.VMEM(one, BF16),
            pltpu.VMEM((rows, HEAD_DIM), F32),
            pltpu.SemaphoreType.DMA((3, spatial)),
            *small_scratch(gain, total),
        ],
        (head_kind, keys, gain, total, after, after_too),
    )


def attend(query, key, value):
    scores = lax.dot_general(query, key, (((1,), (1,)), ((), ())), preferred_element_type=F32)
    top = jnp.max(scores, axis=1, keepdims=True)
    weights = jnp.exp2(scores - top).astype(BF16)
    wide = jnp.concatenate([value, jnp.ones_like(value)], axis=1)
    total = jnp.dot(weights, wide, preferred_element_type=F32)
    return (total[:, :HEAD_DIM] / total[:, HEAD_DIM:]).astype(BF16)


def attention(count, first, blocks, block, starts, load, refs):
    q_ref, gain_any, total_any, out_ref, order, q_buf, k_buf, v_buf, o_buf, factors, sems, *small = refs
    gain_ref, total_ref = small[:2]
    smalls = small_copies((gain_any, total_any), small)
    start_all(smalls)
    size = blocks * block
    start = pl.multiple_of(starts, block)

    def q_copy(h):
        return pltpu.make_async_copy(
            column(q_ref, order[first + h], pl.ds(start, size)), q_buf.at[h], sems.at[0, h]
        )

    def o_copy(h):
        return pltpu.make_async_copy(
            o_buf.at[h], column(out_ref, order[first + h], pl.ds(start, size)), sems.at[3, h]
        )

    for h in range(count):
        q_copy(h).start()
        load(h)
    wait_all(smalls)
    factors[...] = row_factors(total_ref, 0, start, size)
    together = min(UNROLL // blocks, count)

    def step(g, _):
        for n in range(together):
            h = g * together + n
            q_copy(h).wait()
            for i, buf in ((1, k_buf), (2, v_buf)):
                pltpu.make_async_copy(buf.at[h], buf.at[h], sems.at[i, h]).wait()
        for n in range(together):
            h = g * together + n
            gain = gain_of(gain_ref, order[first + h]) * FACTOR
            for part in range(blocks):
                rows = slice(part * block, (part + 1) * block)
                query = (q_buf[h, rows, :].astype(F32) * factors[rows, :] * gain).astype(BF16)
                o_buf[h, rows, :] = attend(query, k_buf[h], v_buf[h])
        for n in range(together):
            o_copy(g * together + n).start()
        return 0

    lax.fori_loop(0, count // together, step, 0)
    for h in range(count):
        o_copy(h).wait()


def attention_scratch(heads, count, blocks, block, gain, total):
    return [
        order_scratch(heads),
        pltpu.VMEM((count, blocks * block, HEAD_DIM), BF16),
        pltpu.VMEM((count, 4 * block, HEAD_DIM), BF16),
        pltpu.VMEM((count, 4 * block, HEAD_DIM), BF16),
        pltpu.VMEM((count, blocks * block, HEAD_DIM), BF16),
        pltpu.VMEM((blocks * block, HEAD_DIM), F32),
        pltpu.SemaphoreType.DMA((4, count)),
        *small_scratch(gain, total),
    ]


def fill(buf, sem, parts):
    at = 0
    for part in parts:
        size = part.shape[0]
        pltpu.make_async_copy(part, buf.at[pl.ds(at, size)], sem).start()
        at += size


def near_kernel(spatial, block, kind_ref, q_ref, k_ref, v_ref, kp_ref, vp_ref, gain_ref, total_ref, after_ref, out_ref, *scratch):
    order, q_buf, k_buf, v_buf, o_buf, factors, sems = scratch[:7]
    put_order(kind_ref, order, spatial)
    place = Place(block)
    one = pl.ds(pl.multiple_of(place.apart, block), block)

    def load(h):
        head = order[h]

        @pl.when(place.inner)
        def _():
            fill(k_buf.at[h], sems.at[1, h], (k_ref.at[h], kp_ref.at[h, one]))
            fill(v_buf.at[h], sems.at[2, h], (column(v_ref, head), column(vp_ref, head, one)))

        @pl.when(jnp.logical_not(place.inner))
        def _():
            fill(k_buf.at[h], sems.at[1, h], (kp_ref.at[h], k_ref.at[h, one]))
            fill(v_buf.at[h], sems.at[2, h], (column(vp_ref, head), column(v_ref, head, one)))

    refs = (q_ref, gain_ref, total_ref, out_ref) + scratch
    attention(spatial, 0, 1, block, place.near, load, refs)


def near_call(head_kind, q, k, v, k_pair, v_pair, gain, total, after, spatial, block):
    heads = head_kind.shape[0]
    return call(
        functools.partial(near_kernel, spatial, block),
        "near",
        shape(q.shape),
        [IN_SMEM] + [ANY] * 8,
        ANY,
        attention_scratch(heads, spatial, 1, block, gain, total),
        (head_kind, q, k, v, k_pair, v_pair, gain, total, after),
    )


def far_kernel(spatial, first, count, block, kind_ref, q_ref, k_ref, v_ref, kp_ref, vp_ref, kx_ref, vx_ref, gain_ref, total_ref, after_ref, have_ref, out_ref, *scratch):
    order, q_buf, k_buf, v_buf, o_buf, factors, sems = scratch[:7]
    put_order(kind_ref, order, spatial)
    place = Place(block)
    one = pl.ds(pl.multiple_of(place.apart, block), block)
    two = pl.ds(pl.multiple_of(place.far, block), 2 * block)

    def load(h):
        n = first + h
        head = order[n]

        @pl.when(place.inner)
        def _():
            fill(k_buf.at[h], sems.at[1, h], (k_ref.at[n], kp_ref.at[n, one]))
            fill(v_buf.at[h], sems.at[2, h], (column(v_ref, head), column(vp_ref, head, one)))

        @pl.when(jnp.logical_not(place.inner))
        def _():
            fill(k_buf.at[h], sems.at[1, h], (k_ref.at[n, two], kx_ref.at[h]))
            fill(v_buf.at[h], sems.at[2, h], (column(v_ref, head, two), vx_ref.at[n]))

    refs = (q_ref, gain_ref, total_ref, out_ref) + scratch
    attention(count, first, 2, block, place.far, load, refs)


def far_call(head_kind, q, k, v, k_pair, v_pair, k_cross, v_cross, gain, total, after, have, first, spatial, block):
    heads = head_kind.shape[0]
    count = k_cross.shape[0]
    return call(
        functools.partial(far_kernel, spatial, first, count, block),
        "far",
        shape(q.shape),
        [IN_SMEM] + [ANY] * 11,
        ANY,
        attention_scratch(heads, count, 2, block, gain, total),
        (head_kind, q, k, v, k_pair, v_pair, k_cross, v_cross, gain, total, after, have),
        aliases={11: 0},
    )


def place_kernel(spatial, firsts, kind_ref, *refs):
    count = len(firsts)
    parts, (out_ref, order, held, sems) = refs[:count], refs[-4:]
    copies = [pltpu.make_async_copy(x, held.at[i], sems.at[0, i]) for i, x in enumerate(parts)]
    start_all(copies)
    put_order(kind_ref, order, spatial)
    core = lax.axis_index("seq").astype(jnp.int32) % 2
    wait_all(copies)
    copies = [
        pltpu.make_async_copy(
            held.at[i],
            column(out_ref, order[spatial + (1 - core if at is None else at)]),
            sems.at[1, i],
        )
        for i, at in enumerate(firsts)
    ]
    start_all(copies)
    wait_all(copies)


def place_call(head_kind, parts, firsts, have, spatial):
    count = len(parts)
    return call(
        functools.partial(place_kernel, spatial, firsts),
        "place",
        shape(have.shape),
        [IN_SMEM] + [ANY] * (count + 1),
        ANY,
        [
            order_scratch(head_kind.shape[0]),
            pltpu.VMEM((count,) + parts[0].shape, BF16),
            pltpu.SemaphoreType.DMA((2, count)),
        ],
        (head_kind, *parts, have),
        aliases={1 + count: 0},
    )


PIECE = 128
CHIPS = 4
TURNS = 3


def deal_kernel(spatial, block, kind_ref, q_ref, k_ref, v_ref, got_ref, *refs):
    small_any, outs = refs[:4], refs[5 : 5 + CHIPS]
    order, held, sems, *small = refs[5 + CHIPS :]
    gq_ref, gk_ref, total_ref, pair_ref = small[:4]
    smalls = small_copies(small_any, small)
    start_all(smalls)
    put_order(kind_ref, order, spatial)
    place = Place(block)
    rows = q_ref.shape[0]
    head = order[spatial + place.core]
    own = pl.ds(pl.multiple_of(place.core * rows, rows), rows)
    other = pl.ds(pl.multiple_of((1 - place.core) * rows, rows), rows)
    ins = [
        pltpu.make_async_copy(column(ref, head), held.at[i, own], sems.at[i])
        for i, ref in enumerate((q_ref, k_ref, v_ref))
    ]
    ins.append(pltpu.make_async_copy(got_ref, held.at[:, other], sems.at[3]))
    start_all(ins)
    wait_all(smalls)
    gains = (gain_of(gq_ref, head) * FACTOR, gain_of(gk_ref, head))
    factors = [
        [row_factors(ref, i, 0, rows) for i in range(2)] for ref in (total_ref, pair_ref)
    ]
    wait_all(ins)
    for half, factor in zip((own, other), factors):
        for i in range(2):
            held[i, half, :] = (held[i, half, :].astype(F32) * factor[i] * gains[i]).astype(BF16)
    copies = []
    for turn in (1, 2, 3, 0):
        owner = place.chip ^ turn
        for g in range(TURNS):
            at = pl.multiple_of((owner + CHIPS * g) * PIECE, PIECE)
            copies.append(
                pltpu.make_async_copy(
                    held.at[:, pl.ds(at, PIECE), :],
                    outs[turn].at[:, g],
                    sems.at[4 + turn * TURNS + g],
                )
            )
    start_all(copies)
    wait_all(copies)


def deal_call(head_kind, queries, keys, values, got, query_gain, key_gain, total, pair, after, spatial, block):
    return call(
        functools.partial(deal_kernel, spatial, block),
        "deal",
        [shape((3, TURNS, PIECE, HEAD_DIM))] * CHIPS,
        [IN_SMEM] + [ANY] * 9,
        [ANY] * CHIPS,
        [
            order_scratch(head_kind.shape[0]),
            pltpu.VMEM((3, 2 * queries.shape[0], HEAD_DIM), BF16),
            pltpu.SemaphoreType.DMA((4 + CHIPS * TURNS,)),
            *small_scratch(query_gain, key_gain, total, pair),
        ],
        (head_kind, queries, keys, values, got, query_gain, key_gain, total, pair, after),
    )


def gather_kernel(spatial, kind_ref, *refs):
    ins = refs[:CHIPS]
    out_ref, send_ref, order, held, sems = refs[-5:]
    put_order(kind_ref, order, spatial)
    index = lax.axis_index("seq").astype(jnp.int32)
    core, chip = index % 2, index // 2
    rows = send_ref.shape[0]
    copies = []
    for turn in range(CHIPS):
        owner = chip ^ turn
        for g in range(TURNS):
            at = pl.multiple_of((owner + CHIPS * g) * PIECE, PIECE)
            copies.append(
                pltpu.make_async_copy(
                    ins[turn].at[g], held.at[pl.ds(at, PIECE)], sems.at[turn * TURNS + g]
                )
            )
    start_all(copies)
    wait_all(copies)
    own = held.at[pl.ds(pl.multiple_of(core * rows, rows), rows)]
    other = held.at[pl.ds(pl.multiple_of((1 - core) * rows, rows), rows)]
    outs = [
        pltpu.make_async_copy(other, send_ref, sems.at[0]),
        pltpu.make_async_copy(own, column(out_ref, order[spatial + core]), sems.at[1]),
    ]
    start_all(outs)
    wait_all(outs)


def gather_call(head_kind, parts, have, spatial):
    rows = have.shape[0]
    return call(
        functools.partial(gather_kernel, spatial),
        "gather",
        [shape(have.shape), shape((rows, HEAD_DIM))],
        [IN_SMEM] + [ANY] * (CHIPS + 1),
        [ANY] * 2,
        [
            order_scratch(head_kind.shape[0]),
            pltpu.VMEM((2 * rows, HEAD_DIM), BF16),
            pltpu.SemaphoreType.DMA((CHIPS * TURNS,)),
        ],
        (head_kind, *parts, have),
        aliases={1 + CHIPS: 0},
    )


GROUPS = (
    ((0, 1), (2, 1), (1, 0), (1, 2), (3, 0), (3, 2)),
    ((0, 0), (0, 2), (2, 0), (2, 2), (1, 1), (3, 1)),
)


def frames_kernel(*refs):
    anys, outs, ins, sems = refs[:CHIPS], refs[CHIPS + 1 : 2 * CHIPS + 1], refs[2 * CHIPS + 1 : -1], refs[-1]
    copies = [pltpu.make_async_copy(a, b, sems.at[i]) for i, (a, b) in enumerate(zip(anys, ins))]
    start_all(copies)
    wait_all(copies)
    row = lax.broadcasted_iota(jnp.int32, (PIECE, PIECE), 0)
    col = lax.broadcasted_iota(jnp.int32, (PIECE, PIECE), 1)
    for group in GROUPS:
        key = jnp.concatenate([ins[s][1, g] for s, g in group], axis=0)
        value = jnp.concatenate([ins[s][2, g] for s, g in group], axis=0)
        wide = jnp.concatenate([value, jnp.ones_like(value)], axis=1)
        same = jnp.concatenate([row == col] * len(group), axis=1)
        for s, g in group:
            scores = lax.dot_general(
                ins[s][0, g], key, (((1,), (1,)), ((), ())), preferred_element_type=F32
            )
            scores = jnp.where(same, scores, LOW)
            top = jnp.max(scores, axis=1, keepdims=True)
            weights = jnp.exp2(scores - top).astype(BF16)
            total = jnp.dot(weights, wide, preferred_element_type=F32)
            outs[s][g] = (total[:, :HEAD_DIM] / total[:, HEAD_DIM:]).astype(BF16)


def frames_call(parts, after):
    return call(
        frames_kernel,
        "frames",
        [shape((TURNS, PIECE, HEAD_DIM))] * CHIPS,
        [ANY] * (CHIPS + 1),
        [IN_VMEM] * CHIPS,
        [pltpu.VMEM(parts[0].shape, BF16) for _ in parts] + [pltpu.SemaphoreType.DMA((CHIPS,))],
        (*parts, after),
    )


def temporal_folded(queries, keys, values, query_gain, key_gain, head_kind, total, spatial, first):
    rows = queries.shape[0]
    heads = head_kind.shape[0]
    count = heads - spatial
    ids = jnp.argsort(head_kind, stable=True)[spatial:]
    take = lambda x: jnp.take(x.reshape(-1, heads, HEAD_DIM), ids, axis=1)
    inverse = lax.rsqrt(total / D + 1e-06)[:, :, None, None]
    norm = lambda x, i, gain: (take(x).astype(F32) * inverse[i] * take(gain)).astype(BF16)
    query = norm(queries, 0, query_gain * FACTOR).astype(F32)
    flat = lambda x: lax.all_gather(x.reshape(rows, -1), "seq", axis=0, tiled=True)
    key_all = flat(norm(keys, 1, key_gain))
    value_all = flat(take(values))
    place = (first + jnp.arange(rows, dtype=jnp.int32)) % FRAME
    running = jnp.full((rows, count), LOW, F32)
    summed = jnp.zeros((rows, count), F32)
    result = jnp.zeros((rows, count, HEAD_DIM), F32)
    for step in range(key_all.shape[0] // FRAME):
        at = place + step * FRAME
        key = jnp.take(key_all, at, axis=0).reshape(rows, count, HEAD_DIM).astype(F32)
        value = jnp.take(value_all, at, axis=0).reshape(rows, count, HEAD_DIM).astype(F32)
        scores = jnp.sum(query * key, axis=2)
        newest = jnp.maximum(running, scores)
        shrink = jnp.exp2(running - newest)
        weight = jnp.exp2(scores - newest)
        summed = summed * shrink + weight
        result = result * shrink[:, :, None] + weight[:, :, None] * value
        running = newest
    done = (result / summed[:, :, None]).astype(BF16)
    return [done[:, j] for j in range(count)]


def per_device(queries, keys, values, query_gain, key_gain, head_kind):
    rows = queries.shape[0]
    heads = head_kind.shape[0]
    temporal = heads // 5
    spatial = heads - temporal
    block = rows // 3
    devices = lax.axis_size("seq")
    parts = lax.axis_size("head")
    dealt = temporal == 2 and devices == 2 * CHIPS and rows == 6 * PIECE
    pair = [(i, i ^ 1) for i in range(devices)]
    cross = []
    for i in range(3, devices, 4):
        after = (i + 1) % devices
        cross += [(i, after), (after, i)]
    turned = [[(i, i ^ (2 * turn)) for i in range(devices)] for turn in range(1, CHIPS)]
    send = lambda x, route: lax.ppermute(x, "seq", route)
    gq, gk = query_gain, key_gain

    v_pair = send(values, pair)
    sums, v_near, *t_send = first_call(head_kind, queries, keys, values, spatial, block, dealt)
    v_cross = send(v_near, cross)
    total = sums
    for d in range(1, parts):
        total = total + lax.ppermute(sums, "head", [(i, (i + d) % parts) for i in range(parts)])
    last = total
    if dealt:
        t_got = send(t_send[0], pair)
        pair_total = send(total, pair)
        pieces = deal_call(
            head_kind, queries, keys, values, t_got, gq, gk, total, pair_total, v_pair,
            spatial, block,
        )
        arrived = [pieces[0]] + [send(p, r) for p, r in zip(pieces[1:], turned)]
        last = pieces[0]
    k, *k_near = keys_call(head_kind, keys, gk, total, last, v_cross, spatial, block)
    k_pair = send(k, pair)
    k_cross = [send(part, cross) for part in k_near]
    out = near_call(head_kind, queries, k, values, k_pair, v_pair, gq, total, total, spatial, block)
    last = total
    if dealt:
        results = frames_call(arrived, out)
        back = [results[0]] + [send(p, r) for p, r in zip(results[1:], turned)]
        last = results[0]
    each = spatial // CHUNKS
    for c, part in enumerate(k_cross):
        out = far_call(
            head_kind, queries, k, values, k_pair, v_pair, part, v_cross, gq, total, last, out,
            c * each, spatial, block,
        )
        if dealt and c == 0:
            out, t_other = gather_call(head_kind, back, out, spatial)
            t_other = send(t_other, pair)
    if dealt:
        return place_call(head_kind, [t_other], [None], out, spatial)
    index = lax.axis_index("seq").astype(jnp.int32)
    t_out = temporal_folded(
        queries, keys, values, query_gain, key_gain, head_kind, total, spatial, index * rows
    )
    return place_call(head_kind, t_out, list(range(temporal)), out, spatial)


def solution(mesh):
    placed = (P("seq", "head"), P("seq", "head"), P("seq", "head"), P("head"), P("head"), P("head"))
    return jax.shard_map(
        per_device, mesh=mesh, in_specs=placed, out_specs=P("seq", "head"), check_vma=False
    )
```

```python
import functools
import math

import jax
import jax.numpy as jnp
from jax import lax
from jax.experimental import pallas as pl
from jax.experimental.pallas import tpu as pltpu
from jax.sharding import PartitionSpec as P

HEAD_DIM = 128
D = 5120
FRAME = 1024
OFFSET = 512
VMEM = 24 * 1024 * 1024
VMEM_FIRST = 61 * 1024 * 1024
LOW = -1e30
FACTOR = math.log2(math.e) / math.sqrt(HEAD_DIM)
F32 = jnp.float32
BF16 = jnp.bfloat16
CHUNKS = 4
ANY = pl.BlockSpec(memory_space=pltpu.HBM)
LOOSE = pl.BlockSpec(memory_space=pl.ANY)
IN_SMEM = pl.BlockSpec(memory_space=pltpu.SMEM)
IN_VMEM = pl.BlockSpec(memory_space=pltpu.VMEM)


def shape(dims, dtype=BF16):
    return jax.ShapeDtypeStruct(dims, dtype)


def call(kernel, name, out_shape, in_specs, out_specs, scratch, operands, aliases=None, cycles=1000, vmem=VMEM):
    return pl.pallas_call(
        kernel,
        out_shape=out_shape,
        in_specs=in_specs,
        out_specs=out_specs,
        scratch_shapes=scratch,
        input_output_aliases=aliases or {},
        compiler_params=pltpu.CompilerParams(vmem_limit_bytes=vmem),
        cost_estimate=pl.CostEstimate(flops=1000 * cycles, bytes_accessed=1000, transcendentals=0),
        name=name,
    )(*operands)


def column(ref, head, rows=None):
    lanes = pl.ds(pl.multiple_of(head * HEAD_DIM, HEAD_DIM), HEAD_DIM)
    return ref.at[:, lanes] if rows is None else ref.at[rows, lanes]


def put_order(kind_ref, order_ref, spatial):
    heads = kind_ref.shape[0]

    def step(h, count):
        s, t = count
        temporal = kind_ref[h] == 1
        order_ref[jnp.where(temporal, spatial + t, s)] = h
        return jnp.where(temporal, s, s + 1), jnp.where(temporal, t + 1, t)

    lax.fori_loop(0, heads, step, (jnp.int32(0), jnp.int32(0)))


def order_scratch(heads):
    return pltpu.SMEM((heads,), jnp.int32)


class Place:
    def __init__(self, block=1):
        index = lax.axis_index("seq").astype(jnp.int32)
        self.kind = index % 4
        self.core = index % 2
        self.chip = index // 2
        self.inner = (self.kind == 1) | (self.kind == 2)
        self.apart = jnp.where((self.kind == 0) | (self.kind == 1), 2 * block, 0)
        self.near = jnp.where(self.kind == 0, 2 * block, 0)
        self.far = jnp.where(self.kind == 0, 0, block)
        self.cross = jnp.where(self.kind == 0, 0, block)


def lanes(head):
    return pl.ds(pl.multiple_of(head * HEAD_DIM, HEAD_DIM), HEAD_DIM)


def start_all(copies):
    for copy in copies:
        copy.start()


def wait_all(copies):
    for copy in copies:
        copy.wait()


def first_kernel(spatial, block, dealt, kind_ref, q_any, k_any, v_any, sums_ref, vx_ref, *refs):
    order, held, squares, sems = refs[-4:]
    rows, width = q_any.shape
    steps = (sems.shape[0] - 1) // 2
    size = rows // steps
    copies = [
        [
            pltpu.make_async_copy(
                source.at[pl.ds(s * size, size), :],
                held.at[i, pl.ds(s * size, size), :],
                sems.at[i * steps + s],
            )
            for s in range(steps)
        ]
        for i, source in enumerate((q_any, k_any))
    ]
    v_copy = pltpu.make_async_copy(v_any, held.at[2], sems.at[2 * steps])
    start_all(copies[0] + copies[1] + [v_copy])
    put_order(kind_ref, order, spatial)
    place = Place(block)
    across = pl.ds(pl.multiple_of(place.cross, block), 2 * block)
    for i in range(2):
        for s in range(steps):
            copies[i][s].wait()
            total = None
            for c in range(width // HEAD_DIM):
                x = held[i, s * size : (s + 1) * size, c * HEAD_DIM : (c + 1) * HEAD_DIM].astype(F32)
                total = x * x if total is None else total + x * x
            squares[s * size : (s + 1) * size, :] = total
        sums_ref[i : i + 1, :] = jnp.sum(jnp.transpose(squares[...]), axis=0, keepdims=True)
    v_copy.wait()
    for h in range(spatial):
        vx_ref[h] = held[2, across, lanes(order[h])]
    if dealt:
        for j, ref in enumerate(refs[:2]):
            one = lanes(order[spatial + (1 - place.core if j == 0 else place.core)])
            for i in range(3):
                ref[i] = held[i, :, one]


def first_call(head_kind, queries, keys, values, spatial, block, dealt):
    rows, width = queries.shape
    steps = 6
    outs = [
        shape((2, rows), F32),
        shape((spatial, 2 * block, HEAD_DIM)),
    ]
    if dealt:
        outs += [shape((3, rows, HEAD_DIM))] * 2
    return call(
        functools.partial(first_kernel, spatial, block, dealt),
        "first",
        outs,
        [IN_SMEM] + [ANY] * 3,
        [IN_VMEM] * len(outs),
        [
            order_scratch(head_kind.shape[0]),
            pltpu.VMEM((3, rows, width), BF16),
            pltpu.VMEM((rows, HEAD_DIM), F32),
            pltpu.SemaphoreType.DMA((2 * steps + 1,)),
        ],
        (head_kind, queries, keys, values),
        vmem=VMEM_FIRST,
    )


def row_factors(sums, which, start, size):
    total = None
    for part in sums:
        row = part[which : which + 1, pl.ds(start, size)]
        total = row if total is None else total + row
    inverse = lax.rsqrt(total / D + 1e-06)
    return jnp.transpose(jnp.broadcast_to(inverse, (HEAD_DIM, size)))


def gain_of(gain_ref, head):
    gain = gain_ref[lanes(head)]
    return jnp.broadcast_to(gain[None, :], (8, HEAD_DIM))[0:1, :]


def keys_kernel(spatial, block, kind_ref, k_ref, k_pair_ref, gain_ref, total_ref, pair_ref, after_ref, ks_ref, kp_ref, *refs):
    kx_refs, (order, factors) = refs[:-2], refs[-2:]
    each = kx_refs[0].shape[0]
    rows = k_ref.shape[0]
    put_order(kind_ref, order, spatial)
    place = Place(block)
    factors[0] = row_factors([total_ref], 1, 0, rows)
    factors[1] = row_factors([pair_ref], 1, 0, rows)
    across = pl.ds(pl.multiple_of(place.cross, block), 2 * block)
    for h in range(spatial):
        gain = gain_of(gain_ref, order[h])
        one = lanes(order[h])
        ks_ref[h] = (k_ref[:, one].astype(F32) * factors[0] * gain).astype(BF16)
        kp_ref[h] = (k_pair_ref[:, one].astype(F32) * factors[1] * gain).astype(BF16)
        kx_refs[h // each][h % each] = ks_ref[h, across, :]


def keys_call(head_kind, keys, k_pair, gain, total, pair, after, spatial, block):
    rows = keys.shape[0]
    each = spatial // CHUNKS
    return call(
        functools.partial(keys_kernel, spatial, block),
        "keys",
        [shape((spatial, rows, HEAD_DIM))] * 2
        + [shape((each, 2 * block, HEAD_DIM))] * CHUNKS,
        [IN_SMEM] + [IN_VMEM] * 5 + [LOOSE],
        [IN_VMEM] * (2 + CHUNKS),
        [order_scratch(head_kind.shape[0]), pltpu.VMEM((2, rows, HEAD_DIM), F32)],
        (head_kind, keys, k_pair, gain, total, pair, after),
    )


def attend_all(work, query_of, keys_of, values_of, put):
    def scores_of(item):
        parts = [
            lax.dot_general(query_of(*item), k, (((1,), (1,)), ((), ())), preferred_element_type=F32)
            for k in keys_of(*item)
        ]
        return jnp.concatenate(parts, axis=1)

    scores = scores_of(work[0])
    for n, item in enumerate(work):
        ahead = scores_of(work[n + 1]) if n + 1 < len(work) else None
        top = jnp.max(scores, axis=1, keepdims=True)
        weights = jnp.exp2(scores - top).astype(BF16)
        value = jnp.concatenate(values_of(*item), axis=0)
        wide = jnp.concatenate([value, jnp.ones_like(value)], axis=1)
        total = jnp.dot(weights, wide, preferred_element_type=F32)
        put(item, (total[:, :HEAD_DIM] / total[:, HEAD_DIM:]).astype(BF16))
        scores = ahead


def query_part(q_ref, gain_ref, factors, head, start, size, part):
    rows = pl.ds(pl.multiple_of(start + part * size, size), size)
    gain = gain_of(gain_ref, head) * FACTOR
    scale = factors[part * size : (part + 1) * size, :]
    return (q_ref[rows, lanes(head)].astype(F32) * scale * gain).astype(BF16)


def near_kernel(spatial, block, kind_ref, q_ref, k_ref, v_ref, kp_ref, v_pair_ref, gain_ref, total_ref, after_ref, out_ref, order, factors):
    put_order(kind_ref, order, spatial)
    place = Place(block)
    one = pl.ds(pl.multiple_of(place.apart, block), block)
    factors[...] = row_factors([total_ref], 0, pl.multiple_of(place.near, block), block)

    def both(own_ref, pair_ref):
        return (
            jnp.where(place.inner, own_ref[...], pair_ref[...]),
            jnp.where(place.inner, pair_ref[one, :], own_ref[one, :]),
        )

    def values_of(h):
        head = lanes(order[h])
        return both(v_ref.at[:, head], v_pair_ref.at[:, head])

    def put(item, result):
        out_ref[item[0]] = result

    attend_all(
        [(h,) for h in range(spatial)],
        lambda h: query_part(q_ref, gain_ref, factors, order[h], place.near, block, 0),
        lambda h: both(k_ref.at[h], kp_ref.at[h]),
        values_of,
        put,
    )


def near_call(head_kind, q, k, v, k_pair, v_pair, gain, total, after, spatial, block):
    return call(
        functools.partial(near_kernel, spatial, block),
        "near",
        shape((spatial, block, HEAD_DIM)),
        [IN_SMEM] + [IN_VMEM] * 7 + [LOOSE],
        IN_VMEM,
        [order_scratch(head_kind.shape[0]), pltpu.VMEM((block, HEAD_DIM), F32)],
        (head_kind, q, k, v, k_pair, v_pair, gain, total, after),
    )


def far_attention(first, count, block, place, order, refs, put):
    q_ref, k_ref, v_ref, kp_ref, v_pair_ref, vx_ref, gain_ref, total_ref, factors, *kx_refs = refs
    each = kx_refs[0].shape[0]
    one = pl.ds(pl.multiple_of(place.apart, block), block)
    start = jnp.where(place.inner, 0, place.far)
    two = pl.ds(pl.multiple_of(start, block), 2 * block)
    factors[...] = row_factors([total_ref], 0, pl.multiple_of(place.far, block), 2 * block)

    def three(own_ref, pair_ref, cross_ref):
        return (
            own_ref[two, :],
            jnp.where(place.inner, own_ref[2 * block :, :], cross_ref[:block, :]),
            jnp.where(place.inner, pair_ref[one, :], cross_ref[block:, :]),
        )

    def values_of(h, part):
        head = lanes(order[first + h])
        return three(v_ref.at[:, head], v_pair_ref.at[:, head], vx_ref.at[first + h])

    attend_all(
        [(h, part) for h in range(count) for part in range(2)],
        lambda h, part: query_part(q_ref, gain_ref, factors, order[first + h], place.far, block, part),
        lambda h, part: three(k_ref.at[first + h], kp_ref.at[first + h], kx_refs[h // each].at[h % each]),
        values_of,
        put,
    )


def far_kernel(spatial, first, count, block, chunks, kind_ref, *refs):
    operands, kx_refs, (out_ref, order, factors) = refs[:8], refs[8 : 8 + chunks], refs[-3:]
    put_order(kind_ref, order, spatial)
    place = Place(block)

    def put(item, result):
        h, part = item
        out_ref[h, part * block : (part + 1) * block, :] = result

    far_attention(first, count, block, place, order, operands + (factors,) + kx_refs, put)


def far_call(head_kind, operands, k_cross, after, first, count, spatial, block):
    return call(
        functools.partial(far_kernel, spatial, first, count, block, len(k_cross)),
        "far",
        shape((count, 2 * block, HEAD_DIM)),
        [IN_SMEM] + [IN_VMEM] * (len(operands) + len(k_cross)) + [LOOSE],
        IN_VMEM,
        [order_scratch(head_kind.shape[0]), pltpu.VMEM((2 * block, HEAD_DIM), F32)],
        (head_kind, *operands, *k_cross, after),
    )


def last_kernel(spatial, first, count, block, parts, chunks, kind_ref, *refs):
    operands, kx_refs, refs = refs[:8], refs[8 : 8 + chunks], refs[8 + chunks :]
    near_ref, far_ref, t_refs = refs[0], refs[1], refs[2 : 2 + parts]
    out_ref, order, factors, done, held, sems = refs[2 + parts :]
    put_order(kind_ref, order, spatial)
    place = Place(block)
    near_rows = pl.ds(pl.multiple_of(place.near, block), block)
    far_rows = pl.ds(pl.multiple_of(place.far, block), 2 * block)
    copies = []

    def send(source, head, rows):
        copies.append(
            pltpu.make_async_copy(source, column(out_ref, head, rows), sems.at[len(copies)])
        )
        copies[-1].start()

    for h in range(spatial):
        send(near_ref.at[h], order[h], near_rows)
    for h in range(first):
        send(far_ref.at[h], order[h], far_rows)
    rows = 3 * block
    if parts == 2 * CHIPS:
        for j in range(2):
            for turn in range(CHIPS):
                for g in range(TURNS):
                    piece = (place.chip ^ turn) + CHIPS * g
                    into = pl.ds(pl.multiple_of(piece * PIECE, PIECE), PIECE)
                    held[j, into, :] = t_refs[j * CHIPS + turn][g]
            own = pl.ds(pl.multiple_of(place.core * rows, block), rows)
            send(held.at[j, own], order[spatial + (place.core ^ j)], pl.ds(0, rows))
    else:
        for j in range(parts):
            send(t_refs[j], order[spatial + j], pl.ds(0, rows))

    def put(item, result):
        h, part = item
        done[h, part * block : (part + 1) * block, :] = result
        if part == 1:
            send(done.at[h], order[first + h], far_rows)

    far_attention(first, count, block, place, order, operands + (factors,) + kx_refs, put)
    wait_all(copies)


def last_call(head_kind, operands, k_cross, near, far, parts, first, count, spatial, block):
    rows, width = operands[0].shape
    heads = head_kind.shape[0]
    return call(
        functools.partial(last_kernel, spatial, first, count, block, len(parts), len(k_cross)),
        "last",
        shape((rows, width)),
        [IN_SMEM] + [IN_VMEM] * (len(operands) + len(k_cross) + 2 + len(parts)),
        ANY,
        [
            order_scratch(heads),
            pltpu.VMEM((2 * block, HEAD_DIM), F32),
            pltpu.VMEM((count, 2 * block, HEAD_DIM), BF16),
            pltpu.VMEM((2, 2 * rows, HEAD_DIM), BF16),
            pltpu.SemaphoreType.DMA((2 * spatial + heads - spatial,)),
        ],
        (head_kind, *operands, *k_cross, near, far, *parts),
    )


PIECE = 128
CHIPS = 4
TURNS = 3


def deal_kernel(spatial, block, kind_ref, own_ref, got_ref, gq_ref, gk_ref, total_ref, pair_ref, *refs):
    outs, (order, held) = refs[:CHIPS], refs[CHIPS:]
    put_order(kind_ref, order, spatial)
    place = Place(block)
    rows = own_ref.shape[1]
    head = order[spatial + place.core]
    own = pl.ds(pl.multiple_of(place.core * rows, rows), rows)
    other = pl.ds(pl.multiple_of((1 - place.core) * rows, rows), rows)
    gains = (gain_of(gq_ref, head) * FACTOR, gain_of(gk_ref, head))
    for half, source, sums in ((own, own_ref, total_ref), (other, got_ref, pair_ref)):
        for i in range(2):
            factors = row_factors([sums], i, 0, rows)
            held[i, half, :] = (source[i].astype(F32) * factors * gains[i]).astype(BF16)
        held[2, half, :] = source[2]
    for turn in range(CHIPS):
        owner = place.chip ^ turn
        for g in range(TURNS):
            at = pl.multiple_of((owner + CHIPS * g) * PIECE, PIECE)
            for i in range(3):
                outs[turn][i, g] = held[i, pl.ds(at, PIECE), :]


def deal_call(head_kind, own, got, query_gain, key_gain, total, pair, spatial, block):
    return call(
        functools.partial(deal_kernel, spatial, block),
        "deal",
        [shape((3, TURNS, PIECE, HEAD_DIM))] * CHIPS,
        [IN_SMEM] + [IN_VMEM] * 6,
        [IN_VMEM] * CHIPS,
        [
            order_scratch(head_kind.shape[0]),
            pltpu.VMEM((3, 2 * own.shape[1], HEAD_DIM), BF16),
        ],
        (head_kind, own, got, query_gain, key_gain, total, pair),
    )


GROUPS = (
    ((0, 1), (2, 1), (1, 0), (1, 2), (3, 0), (3, 2)),
    ((0, 0), (0, 2), (2, 0), (2, 2), (1, 1), (3, 1)),
)


def frames_kernel(*refs):
    ins, outs = refs[:CHIPS], refs[-CHIPS:]
    side = len(GROUPS[0]) * PIECE
    row = lax.broadcasted_iota(jnp.int32, (PIECE, PIECE), 0)
    col = lax.broadcasted_iota(jnp.int32, (PIECE, PIECE), 1)
    same = jnp.tile(row == col, (1, len(GROUPS[0])))
    half = side // 2
    work = [(n, part) for n in range(len(GROUPS)) for part in range(2)]
    query, key, value = (
        [jnp.concatenate([ins[s][i, g] for s, g in group], axis=0) for group in GROUPS]
        for i in range(3)
    )
    same = jnp.concatenate([same] * (half // PIECE), axis=0)

    def scores_of(n, part):
        return lax.dot_general(
            query[n][part * half : (part + 1) * half],
            key[n],
            (((1,), (1,)), ((), ())),
            preferred_element_type=F32,
        )

    scores = scores_of(*work[0])
    for at, (n, part) in enumerate(work):
        ahead = scores_of(*work[at + 1]) if at + 1 < len(work) else None
        scores = jnp.where(same, scores, LOW)
        top = jnp.max(scores, axis=1, keepdims=True)
        weights = jnp.exp2(scores - top).astype(BF16)
        wide = jnp.concatenate([value[n], jnp.ones_like(value[n])], axis=1)
        total = jnp.dot(weights, wide, preferred_element_type=F32)
        done = (total[:, :HEAD_DIM] / total[:, HEAD_DIM:]).astype(BF16)
        for i in range(half // PIECE):
            s, g = GROUPS[n][part * (half // PIECE) + i]
            outs[s][g] = done[i * PIECE : (i + 1) * PIECE]
        scores = ahead


def frames_call(parts, after):
    return call(
        frames_kernel,
        "frames",
        [shape((TURNS, PIECE, HEAD_DIM))] * CHIPS,
        [IN_VMEM] * CHIPS + [LOOSE],
        [IN_VMEM] * CHIPS,
        [],
        (*parts, after),
    )


def temporal_folded(queries, keys, values, query_gain, key_gain, head_kind, total, spatial, first):
    rows = queries.shape[0]
    heads = head_kind.shape[0]
    count = heads - spatial
    ids = jnp.argsort(head_kind, stable=True)[spatial:]
    take = lambda x: jnp.take(x.reshape(-1, heads, HEAD_DIM), ids, axis=1)
    inverse = lax.rsqrt(total / D + 1e-06)[:, :, None, None]
    norm = lambda x, i, gain: (take(x).astype(F32) * inverse[i] * take(gain)).astype(BF16)
    query = norm(queries, 0, query_gain * FACTOR).astype(F32)
    flat = lambda x: lax.all_gather(x.reshape(rows, -1), "seq", axis=0, tiled=True)
    key_all = flat(norm(keys, 1, key_gain))
    value_all = flat(take(values))
    place = (first + jnp.arange(rows, dtype=jnp.int32)) % FRAME
    running = jnp.full((rows, count), LOW, F32)
    summed = jnp.zeros((rows, count), F32)
    result = jnp.zeros((rows, count, HEAD_DIM), F32)
    for step in range(key_all.shape[0] // FRAME):
        at = place + step * FRAME
        key = jnp.take(key_all, at, axis=0).reshape(rows, count, HEAD_DIM).astype(F32)
        value = jnp.take(value_all, at, axis=0).reshape(rows, count, HEAD_DIM).astype(F32)
        scores = jnp.sum(query * key, axis=2)
        newest = jnp.maximum(running, scores)
        shrink = jnp.exp2(running - newest)
        weight = jnp.exp2(scores - newest)
        summed = summed * shrink + weight
        result = result * shrink[:, :, None] + weight[:, :, None] * value
        running = newest
    done = (result / summed[:, :, None]).astype(BF16)
    return [done[:, j] for j in range(count)]


def per_device(queries, keys, values, query_gain, key_gain, head_kind):
    rows = queries.shape[0]
    heads = head_kind.shape[0]
    temporal = heads // 5
    spatial = heads - temporal
    block = rows // 3
    devices = lax.axis_size("seq")
    planes = lax.axis_size("head")
    dealt = temporal == 2 and devices == 2 * CHIPS and rows == 6 * PIECE
    pair = [(i, i ^ 1) for i in range(devices)]
    cross = []
    for i in range(3, devices, 4):
        after = (i + 1) % devices
        cross += [(i, after), (after, i)]
    turned = [[(i, i ^ (2 * turn)) for i in range(devices)] for turn in range(1, CHIPS)]
    send = lambda x, route: lax.ppermute(x, "seq", route)

    sums, v_near, *t_parts = first_call(
        head_kind, queries, keys, values, spatial, block, dealt
    )
    k_pair = send(lax.optimization_barrier((keys, sums))[0], pair)
    v_pair = send(lax.optimization_barrier((values, sums))[0], pair)
    v_cross = send(v_near, cross)
    total = sums
    if planes & (planes - 1) == 0:
        for d in [1 << n for n in range(planes.bit_length() - 1)]:
            total = total + lax.ppermute(total, "head", [(i, i ^ d) for i in range(planes)])
    else:
        total = lax.psum(sums, "head")
    pair_total = send(total, pair)
    last = total
    if dealt:
        t_got = send(t_parts[0], pair)
        pieces = deal_call(
            head_kind, t_parts[1], t_got, query_gain, key_gain, total, pair_total, spatial, block
        )
        arrived = [pieces[0]] + [send(p, r) for p, r in zip(pieces[1:], turned)]
        last = pieces[0]
    k, kp, *k_near = keys_call(
        head_kind, keys, k_pair, key_gain, total, pair_total, last, spatial, block
    )
    near = near_call(
        head_kind, queries, k, values, kp, v_pair, query_gain, total, v_cross, spatial, block
    )
    k_cross = [send(lax.optimization_barrier((part, near))[0], cross) for part in k_near]
    last = near
    if dealt:
        results = frames_call(arrived, near)
        own = [results[0]] + [send(p, r) for p, r in zip(results[1:], turned)]
        last = results[0]
    else:
        index = lax.axis_index("seq").astype(jnp.int32)
        parts = temporal_folded(
            queries, keys, values, query_gain, key_gain, head_kind, total, spatial, index * rows
        )
    operands = (queries, k, values, kp, v_pair, v_cross, query_gain, total)
    half = spatial // 2
    far = far_call(
        head_kind, operands, k_cross[: CHUNKS // 2], last, 0, half, spatial, block
    )
    if dealt:
        parts = own + [send(lax.optimization_barrier((p, far))[0], pair) for p in own]
    return last_call(
        head_kind, operands, k_cross[CHUNKS // 2 :], near, far, parts, half, spatial - half,
        spatial, block,
    )


def solution(mesh):
    placed = (P("seq", "head"), P("seq", "head"), P("seq", "head"), P("head"), P("head"), P("head"))
    return jax.shard_map(
        per_device, mesh=mesh, in_specs=placed, out_specs=P("seq", "head"), check_vma=False
    )
```

```python
import functools
import math

import jax
import jax.numpy as jnp
from jax import lax
from jax.experimental import pallas as pl
from jax.experimental.pallas import tpu as pltpu
from jax.sharding import PartitionSpec as P

HEAD_DIM = 128
D = 5120
FRAME = 1024
OFFSET = 512
VMEM = 24 * 1024 * 1024
VMEM_PACK = 57 * 1024 * 1024
VMEM_SUMS = 53 * 1024 * 1024
LOW = -1e30
FACTOR = math.log2(math.e) / math.sqrt(HEAD_DIM)
F32 = jnp.float32
BF16 = jnp.bfloat16
ANY = pl.BlockSpec(memory_space=pltpu.HBM)
LOOSE = pl.BlockSpec(memory_space=pl.ANY)
IN_SMEM = pl.BlockSpec(memory_space=pltpu.SMEM)
IN_VMEM = pl.BlockSpec(memory_space=pltpu.VMEM)


def shape(dims, dtype=BF16):
    return jax.ShapeDtypeStruct(dims, dtype)


def call(kernel, name, out_shape, in_specs, out_specs, scratch, operands, aliases=None, cycles=1000, vmem=VMEM):
    return pl.pallas_call(
        kernel,
        out_shape=out_shape,
        in_specs=in_specs,
        out_specs=out_specs,
        scratch_shapes=scratch,
        input_output_aliases=aliases or {},
        compiler_params=pltpu.CompilerParams(vmem_limit_bytes=vmem),
        cost_estimate=pl.CostEstimate(flops=cycles, bytes_accessed=1000, transcendentals=0),
        name=name,
    )(*operands)


def column(ref, head, rows=None):
    lanes = pl.ds(pl.multiple_of(head * HEAD_DIM, HEAD_DIM), HEAD_DIM)
    return ref.at[:, lanes] if rows is None else ref.at[rows, lanes]


def put_order(kind_ref, order_ref, spatial):
    heads = kind_ref.shape[0]

    def step(h, count):
        s, t = count
        temporal = kind_ref[h] == 1
        order_ref[jnp.where(temporal, spatial + t, s)] = h
        return jnp.where(temporal, s, s + 1), jnp.where(temporal, t + 1, t)

    lax.fori_loop(0, heads, step, (jnp.int32(0), jnp.int32(0)))


def order_scratch(heads):
    return pltpu.SMEM((heads,), jnp.int32)


class Place:
    def __init__(self, block=1):
        index = lax.axis_index("seq").astype(jnp.int32)
        self.kind = index % 4
        self.core = index % 2
        self.chip = index // 2
        self.inner = (self.kind == 1) | (self.kind == 2)
        self.apart = jnp.where((self.kind == 0) | (self.kind == 1), 2 * block, 0)
        self.near = jnp.where(self.kind == 0, 2 * block, 0)
        self.far = jnp.where(self.kind == 0, 0, block)
        self.cross = jnp.where(self.kind == 0, 0, block)


def lanes(head):
    return pl.ds(pl.multiple_of(head * HEAD_DIM, HEAD_DIM), HEAD_DIM)


def start_all(copies):
    for copy in copies:
        copy.start()


def wait_all(copies):
    for copy in copies:
        copy.wait()


def pack_kernel(spatial, block, dealt, kind_ref, q_any, k_any, v_any, *refs):
    outs, (order, packed, t_buf, sems) = refs[:-4], refs[-4:]
    put_order(kind_ref, order, spatial)
    place = Place(block)
    across = pl.ds(pl.multiple_of(place.cross, block), 2 * block)
    moves = []

    def move(source, held, into):
        n = len(moves)
        moves.append(
            (
                pltpu.make_async_copy(source, held, sems.at[0, n]),
                pltpu.make_async_copy(held, into, sems.at[1, n]),
            )
        )
        moves[-1][0].start()

    for h in range(spatial):
        for i, ref in enumerate((k_any, v_any)):
            move(column(ref, order[h], across), packed.at[i, h], outs[0].at[i, h])
    if dealt:
        head = order[spatial + 1 - place.core]
        for i, ref in enumerate((q_any, k_any, v_any)):
            move(column(ref, head), t_buf.at[i], outs[1].at[i])
    for came, goes in moves:
        came.wait()
        goes.start()
    for _, goes in moves:
        goes.wait()


def pack_call(head_kind, queries, keys, values, spatial, block, dealt):
    rows = queries.shape[0]
    both = (2, spatial, 2 * block, HEAD_DIM)
    outs = [shape(both)]
    if dealt:
        outs.append(shape((3, rows, HEAD_DIM)))
    return call(
        functools.partial(pack_kernel, spatial, block, dealt),
        "pack",
        outs,
        [IN_SMEM] + [ANY] * 3,
        [ANY] * len(outs),
        [
            order_scratch(head_kind.shape[0]),
            pltpu.VMEM(both, BF16),
            pltpu.VMEM((3, rows, HEAD_DIM), BF16),
            pltpu.SemaphoreType.DMA((2, 2 * spatial + 3)),
        ],
        (head_kind, queries, keys, values),
        vmem=VMEM_PACK,
    )


def sums_kernel(q_any, k_any, after_ref, sums_any, held, squares, sums, sems):
    rows, width = q_any.shape
    steps = (sems.shape[0] - 1) // 2
    size = rows // steps
    copies = [
        [
            pltpu.make_async_copy(
                source.at[pl.ds(s * size, size), :],
                held.at[i, pl.ds(s * size, size), :],
                sems.at[i * steps + s],
            )
            for s in range(steps)
        ]
        for i, source in enumerate((q_any, k_any))
    ]
    start_all(copies[0] + copies[1])
    for i in range(2):
        for s in range(steps):
            copies[i][s].wait()
            total = None
            for c in range(width // HEAD_DIM):
                x = held[i, s * size : (s + 1) * size, c * HEAD_DIM : (c + 1) * HEAD_DIM].astype(F32)
                total = x * x if total is None else total + x * x
            squares[s * size : (s + 1) * size, :] = total
        sums[i : i + 1, :] = jnp.sum(jnp.transpose(squares[...]), axis=0, keepdims=True)
    out = pltpu.make_async_copy(sums, sums_any, sems.at[2 * steps])
    out.start()
    out.wait()


def sums_call(queries, keys, after):
    rows, width = queries.shape
    steps = 4
    return call(
        sums_kernel,
        "sums",
        shape((2, rows), F32),
        [ANY] * 2 + [LOOSE],
        ANY,
        [
            pltpu.VMEM((2, rows, width), BF16),
            pltpu.VMEM((rows, HEAD_DIM), F32),
            pltpu.VMEM((2, rows), F32),
            pltpu.SemaphoreType.DMA((2 * steps + 1,)),
        ],
        (queries, keys, after),
        vmem=VMEM_SUMS,
    )


def row_factors(sums, which, start, size):
    total = None
    for part in sums:
        row = part[which : which + 1, pl.ds(start, size)]
        total = row if total is None else total + row
    inverse = lax.rsqrt(total / D + 1e-06)
    return jnp.transpose(jnp.broadcast_to(inverse, (HEAD_DIM, size)))


def gain_of(gain_ref, head):
    gain = gain_ref[lanes(head)]
    return jnp.broadcast_to(gain[None, :], (8, HEAD_DIM))[0:1, :]


def own_kernel(spatial, dealt, afters, kind_ref, q_ref, k_ref, v_ref, gq_ref, gk_ref, total_ref, *refs):
    ks_ref, (order, factors) = refs[afters], refs[-2:]
    rows = k_ref.shape[0]
    put_order(kind_ref, order, spatial)
    place = Place()
    factors[...] = row_factors([total_ref], 1, 0, rows)
    for h in range(spatial):
        gain = gain_of(gk_ref, order[h])
        ks_ref[h] = (k_ref[:, lanes(order[h])].astype(F32) * factors[...] * gain).astype(BF16)
    if dealt:
        t_ref = refs[afters + 1]
        head = order[spatial + place.core]
        one = lanes(head)
        scale = row_factors([total_ref], 0, 0, rows)
        t_ref[0] = (q_ref[:, one].astype(F32) * scale * (gain_of(gq_ref, head) * FACTOR)).astype(BF16)
        t_ref[1] = (k_ref[:, one].astype(F32) * factors[...] * gain_of(gk_ref, head)).astype(BF16)
        t_ref[2] = v_ref[:, one]


def own_call(head_kind, queries, keys, values, query_gain, key_gain, total, afters, spatial, dealt):
    rows = keys.shape[0]
    outs = [shape((spatial, rows, HEAD_DIM))]
    if dealt:
        outs.append(shape((3, rows, HEAD_DIM)))
    return call(
        functools.partial(own_kernel, spatial, dealt, len(afters)),
        "own",
        outs,
        [IN_SMEM] + [IN_VMEM] * 6 + [LOOSE] * len(afters),
        [IN_VMEM] * len(outs),
        [order_scratch(head_kind.shape[0]), pltpu.VMEM((rows, HEAD_DIM), F32)],
        (head_kind, queries, keys, values, query_gain, key_gain, total, *afters),
    )


def pair_kernel(spatial, kind_ref, k_ref, gain_ref, sums_ref, after_ref, kp_ref, order, factors):
    put_order(kind_ref, order, spatial)
    factors[...] = row_factors([sums_ref], 1, 0, k_ref.shape[0])
    for h in range(spatial):
        gain = gain_of(gain_ref, order[h])
        kp_ref[h] = (k_ref[:, lanes(order[h])].astype(F32) * factors[...] * gain).astype(BF16)


def pair_call(head_kind, keys, gain, sums, after, spatial):
    rows = keys.shape[0]
    return call(
        functools.partial(pair_kernel, spatial),
        "pair",
        shape((spatial, rows, HEAD_DIM)),
        [IN_SMEM] + [IN_VMEM] * 3 + [LOOSE],
        IN_VMEM,
        [order_scratch(head_kind.shape[0]), pltpu.VMEM((rows, HEAD_DIM), F32)],
        (head_kind, keys, gain, sums, after),
    )


def attend_all(work, query_of, keys_of, values_of, put):
    def scores_of(item):
        parts = [
            lax.dot_general(query_of(*item), k, (((1,), (1,)), ((), ())), preferred_element_type=F32)
            for k in keys_of(*item)
        ]
        return jnp.concatenate(parts, axis=1)

    scores = scores_of(work[0])
    for n, item in enumerate(work):
        ahead = scores_of(work[n + 1]) if n + 1 < len(work) else None
        top = jnp.max(scores, axis=1, keepdims=True)
        weights = jnp.exp2(scores - top).astype(BF16)
        value = jnp.concatenate(values_of(*item), axis=0)
        wide = jnp.concatenate([value, jnp.ones_like(value)], axis=1)
        total = jnp.dot(weights, wide, preferred_element_type=F32)
        put(item, (total[:, :HEAD_DIM] / total[:, HEAD_DIM:]).astype(BF16))
        scores = ahead


def query_part(q_ref, gain_ref, factors, head, start, size, part):
    rows = pl.ds(pl.multiple_of(start + part * size, size), size)
    gain = gain_of(gain_ref, head) * FACTOR
    scale = factors[part * size : (part + 1) * size, :]
    return (q_ref[rows, lanes(head)].astype(F32) * scale * gain).astype(BF16)


def near_kernel(spatial, block, kind_ref, q_ref, k_ref, v_ref, kp_ref, v_pair_ref, gain_ref, total_ref, out_ref, order, factors):
    put_order(kind_ref, order, spatial)
    place = Place(block)
    one = pl.ds(pl.multiple_of(place.apart, block), block)
    factors[...] = row_factors([total_ref], 0, pl.multiple_of(place.near, block), block)

    def both(own_ref, pair_ref):
        return (
            jnp.where(place.inner, own_ref[...], pair_ref[...]),
            jnp.where(place.inner, pair_ref[one, :], own_ref[one, :]),
        )

    def values_of(h):
        head = lanes(order[h])
        return both(v_ref.at[:, head], v_pair_ref.at[:, head])

    def put(item, result):
        out_ref[item[0]] = result

    attend_all(
        [(h,) for h in range(spatial)],
        lambda h: query_part(q_ref, gain_ref, factors, order[h], place.near, block, 0),
        lambda h: both(k_ref.at[h], kp_ref.at[h]),
        values_of,
        put,
    )


def near_call(head_kind, q, k, v, k_pair, v_pair, gain, total, spatial, block):
    return call(
        functools.partial(near_kernel, spatial, block),
        "near",
        shape((spatial, block, HEAD_DIM)),
        [IN_SMEM] + [IN_VMEM] * 7,
        IN_VMEM,
        [order_scratch(head_kind.shape[0]), pltpu.VMEM((block, HEAD_DIM), F32)],
        (head_kind, q, k, v, k_pair, v_pair, gain, total),
    )


def far_attention(first, count, block, place, order, refs, put):
    q_ref, k_ref, v_ref, kp_ref, v_pair_ref, kvx_ref, gq_ref, gk_ref, total_ref, cross_ref, factors, x_factors, x_keys = refs
    one = pl.ds(pl.multiple_of(place.apart, block), block)
    start = jnp.where(place.inner, 0, place.far)
    two = pl.ds(pl.multiple_of(start, block), 2 * block)
    factors[...] = row_factors([total_ref], 0, pl.multiple_of(place.far, block), 2 * block)
    sent = pl.multiple_of(jnp.where(place.kind == 0, block, 0), block)
    x_factors[...] = row_factors([cross_ref], 1, sent, 2 * block)

    def three(own_ref, pair_ref, cross):
        return (
            own_ref[two, :],
            jnp.where(place.inner, own_ref[2 * block :, :], cross[:block]),
            jnp.where(place.inner, pair_ref[one, :], cross[block:]),
        )

    def keys_of(h, part):
        n = first + h
        if part == 0:
            gain = gain_of(gk_ref, order[n])
            x_keys[h % 2] = (kvx_ref[0, n].astype(F32) * x_factors[...] * gain).astype(BF16)
        return three(k_ref.at[n], kp_ref.at[n], x_keys[h % 2])

    def values_of(h, part):
        head = lanes(order[first + h])
        return three(v_ref.at[:, head], v_pair_ref.at[:, head], kvx_ref[1, first + h])

    attend_all(
        [(h, part) for h in range(count) for part in range(2)],
        lambda h, part: query_part(q_ref, gq_ref, factors, order[first + h], place.far, block, part),
        keys_of,
        values_of,
        put,
    )


def far_kernel(spatial, first, count, block, kind_ref, *refs):
    operands, (out_ref, order, factors, x_factors, x_keys) = refs[:10], refs[-5:]
    put_order(kind_ref, order, spatial)
    place = Place(block)

    def put(item, result):
        h, part = item
        out_ref[h, part * block : (part + 1) * block, :] = result

    far_attention(first, count, block, place, order, operands + (factors, x_factors, x_keys), put)


def far_call(head_kind, operands, after, first, count, spatial, block):
    return call(
        functools.partial(far_kernel, spatial, first, count, block),
        "far",
        shape((count, 2 * block, HEAD_DIM)),
        [IN_SMEM] + [IN_VMEM] * len(operands) + [LOOSE],
        IN_VMEM,
        [order_scratch(head_kind.shape[0])]
        + [pltpu.VMEM((2 * block, HEAD_DIM), F32)] * 2
        + [pltpu.VMEM((2, 2 * block, HEAD_DIM), BF16)],
        (head_kind, *operands, after),
    )


def rest_kernel(spatial, first, count, block, kind_ref, *refs):
    operands, refs = refs[:10], refs[10:]
    near_ref, far_ref, _, out_ref, token_ref, order, factors, x_factors, x_keys, done, sems = refs
    token_ref[...] = jnp.zeros_like(token_ref)
    put_order(kind_ref, order, spatial)
    place = Place(block)
    near_rows = pl.ds(pl.multiple_of(place.near, block), block)
    far_rows = pl.ds(pl.multiple_of(place.far, block), 2 * block)
    copies = []

    def send(source, head, rows):
        copies.append(
            pltpu.make_async_copy(source, column(out_ref, head, rows), sems.at[len(copies)])
        )
        copies[-1].start()

    for h in range(spatial):
        send(near_ref.at[h], order[h], near_rows)
    for h in range(first):
        send(far_ref.at[h], order[h], far_rows)

    def put(item, result):
        h, part = item
        done[h, part * block : (part + 1) * block, :] = result
        if part == 1:
            send(done.at[h], order[first + h], far_rows)

    far_attention(first, count, block, place, order, operands + (factors, x_factors, x_keys), put)
    wait_all(copies)


def rest_call(head_kind, operands, near, far, after, first, count, spatial, block):
    rows, width = operands[0].shape
    heads = head_kind.shape[0]
    return call(
        functools.partial(rest_kernel, spatial, first, count, block),
        "rest",
        [shape((rows, width)), shape((8, HEAD_DIM), F32)],
        [IN_SMEM] + [IN_VMEM] * (len(operands) + 2) + [LOOSE],
        [ANY, IN_VMEM],
        [
            order_scratch(heads),
            pltpu.VMEM((2 * block, HEAD_DIM), F32),
            pltpu.VMEM((2 * block, HEAD_DIM), F32),
            pltpu.VMEM((2, 2 * block, HEAD_DIM), BF16),
            pltpu.VMEM((count, 2 * block, HEAD_DIM), BF16),
            pltpu.SemaphoreType.DMA((2 * spatial,)),
        ],
        (head_kind, *operands, near, far, after),
    )


def place_kernel(spatial, block, parts, kind_ref, *refs):
    t_refs, (_, out_ref, order, held, sems) = refs[:parts], refs[parts:]
    put_order(kind_ref, order, spatial)
    place = Place(block)
    rows = 3 * block
    copies = []

    def send(source, head):
        copies.append(
            pltpu.make_async_copy(source, column(out_ref, head), sems.at[len(copies)])
        )
        copies[-1].start()

    if parts == 2 * CHIPS:
        for j in range(2):
            for turn in range(CHIPS):
                for g in range(TURNS):
                    piece = (place.chip ^ turn) + CHIPS * g
                    into = pl.ds(pl.multiple_of(piece * PIECE, PIECE), PIECE)
                    held[j, into, :] = t_refs[j * CHIPS + turn][g]
            own = pl.ds(pl.multiple_of(place.core * rows, block), rows)
            send(held.at[j, own], order[spatial + (place.core ^ j)])
    else:
        for j in range(parts):
            send(t_refs[j], order[spatial + j])
    wait_all(copies)


def place_call(head_kind, parts, have, spatial, block):
    heads = head_kind.shape[0]
    return call(
        functools.partial(place_kernel, spatial, block, len(parts)),
        "place",
        shape(have.shape),
        [IN_SMEM] + [IN_VMEM] * len(parts) + [ANY],
        ANY,
        [
            order_scratch(heads),
            pltpu.VMEM((2, 2 * have.shape[0], HEAD_DIM), BF16),
            pltpu.SemaphoreType.DMA((heads - spatial,)),
        ],
        (head_kind, *parts, have),
        aliases={1 + len(parts): 0},
    )


PIECE = 128
CHIPS = 4
TURNS = 3


def deal_kernel(spatial, block, kind_ref, own_ref, got_ref, gq_ref, gk_ref, sums_ref, *refs):
    outs, (order, held) = refs[:CHIPS], refs[CHIPS:]
    put_order(kind_ref, order, spatial)
    place = Place(block)
    rows = own_ref.shape[1]
    head = order[spatial + place.core]
    own = pl.ds(pl.multiple_of(place.core * rows, rows), rows)
    other = pl.ds(pl.multiple_of((1 - place.core) * rows, rows), rows)
    gains = (gain_of(gq_ref, head) * FACTOR, gain_of(gk_ref, head))
    for i in range(2):
        factors = row_factors([sums_ref], i, 0, rows)
        held[i, other, :] = (got_ref[i].astype(F32) * factors * gains[i]).astype(BF16)
    held[2, other, :] = got_ref[2]
    for i in range(3):
        held[i, own, :] = own_ref[i]
    for turn in range(CHIPS):
        owner = place.chip ^ turn
        for g in range(TURNS):
            at = pl.multiple_of((owner + CHIPS * g) * PIECE, PIECE)
            for i in range(3):
                outs[turn][i, g] = held[i, pl.ds(at, PIECE), :]


def deal_call(head_kind, own, got, query_gain, key_gain, sums, spatial, block):
    return call(
        functools.partial(deal_kernel, spatial, block),
        "deal",
        [shape((3, TURNS, PIECE, HEAD_DIM))] * CHIPS,
        [IN_SMEM] + [IN_VMEM] * 5,
        [IN_VMEM] * CHIPS,
        [
            order_scratch(head_kind.shape[0]),
            pltpu.VMEM((3, 2 * own.shape[1], HEAD_DIM), BF16),
        ],
        (head_kind, own, got, query_gain, key_gain, sums),
    )


GROUPS = (
    ((0, 1), (2, 1), (1, 0), (1, 2), (3, 0), (3, 2)),
    ((0, 0), (0, 2), (2, 0), (2, 2), (1, 1), (3, 1)),
)


def frames_kernel(*refs):
    ins, outs = refs[:CHIPS], refs[-CHIPS:]
    side = len(GROUPS[0]) * PIECE
    row = lax.broadcasted_iota(jnp.int32, (PIECE, PIECE), 0)
    col = lax.broadcasted_iota(jnp.int32, (PIECE, PIECE), 1)
    same = jnp.tile(row == col, (1, len(GROUPS[0])))
    half = side // 2
    work = [(n, part) for n in range(len(GROUPS)) for part in range(2)]
    query, key, value = (
        [jnp.concatenate([ins[s][i, g] for s, g in group], axis=0) for group in GROUPS]
        for i in range(3)
    )
    same = jnp.concatenate([same] * (half // PIECE), axis=0)

    def scores_of(n, part):
        return lax.dot_general(
            query[n][part * half : (part + 1) * half],
            key[n],
            (((1,), (1,)), ((), ())),
            preferred_element_type=F32,
        )

    scores = scores_of(*work[0])
    for at, (n, part) in enumerate(work):
        ahead = scores_of(*work[at + 1]) if at + 1 < len(work) else None
        scores = jnp.where(same, scores, LOW)
        top = jnp.max(scores, axis=1, keepdims=True)
        weights = jnp.exp2(scores - top).astype(BF16)
        wide = jnp.concatenate([value[n], jnp.ones_like(value[n])], axis=1)
        total = jnp.dot(weights, wide, preferred_element_type=F32)
        done = (total[:, :HEAD_DIM] / total[:, HEAD_DIM:]).astype(BF16)
        for i in range(half // PIECE):
            s, g = GROUPS[n][part * (half // PIECE) + i]
            outs[s][g] = done[i * PIECE : (i + 1) * PIECE]
        scores = ahead


def frames_call(parts, after):
    return call(
        frames_kernel,
        "frames",
        [shape((TURNS, PIECE, HEAD_DIM))] * CHIPS,
        [IN_VMEM] * CHIPS + [LOOSE],
        [IN_VMEM] * CHIPS,
        [],
        (*parts, after),
    )


def temporal_folded(queries, keys, values, query_gain, key_gain, head_kind, total, spatial, first):
    rows = queries.shape[0]
    heads = head_kind.shape[0]
    count = heads - spatial
    ids = jnp.argsort(head_kind, stable=True)[spatial:]
    take = lambda x: jnp.take(x.reshape(-1, heads, HEAD_DIM), ids, axis=1)
    inverse = lax.rsqrt(total / D + 1e-06)[:, :, None, None]
    norm = lambda x, i, gain: (take(x).astype(F32) * inverse[i] * take(gain)).astype(BF16)
    query = norm(queries, 0, query_gain * FACTOR).astype(F32)
    flat = lambda x: lax.all_gather(x.reshape(rows, -1), "seq", axis=0, tiled=True)
    key_all = flat(norm(keys, 1, key_gain))
    value_all = flat(take(values))
    place = (first + jnp.arange(rows, dtype=jnp.int32)) % FRAME
    running = jnp.full((rows, count), LOW, F32)
    summed = jnp.zeros((rows, count), F32)
    result = jnp.zeros((rows, count, HEAD_DIM), F32)
    for step in range(key_all.shape[0] // FRAME):
        at = place + step * FRAME
        key = jnp.take(key_all, at, axis=0).reshape(rows, count, HEAD_DIM).astype(F32)
        value = jnp.take(value_all, at, axis=0).reshape(rows, count, HEAD_DIM).astype(F32)
        scores = jnp.sum(query * key, axis=2)
        newest = jnp.maximum(running, scores)
        shrink = jnp.exp2(running - newest)
        weight = jnp.exp2(scores - newest)
        summed = summed * shrink + weight
        result = result * shrink[:, :, None] + weight[:, :, None] * value
        running = newest
    done = (result / summed[:, :, None]).astype(BF16)
    return [done[:, j] for j in range(count)]


def per_device(queries, keys, values, query_gain, key_gain, head_kind):
    rows = queries.shape[0]
    heads = head_kind.shape[0]
    temporal = heads // 5
    spatial = heads - temporal
    block = rows // 3
    devices = lax.axis_size("seq")
    planes = lax.axis_size("head")
    dealt = temporal == 2 and devices == 2 * CHIPS and rows == 6 * PIECE
    pair = [(i, i ^ 1) for i in range(devices)]
    cross = []
    for i in range(3, devices, 4):
        after = (i + 1) % devices
        cross += [(i, after), (after, i)]
    turned = [[(i, i ^ (2 * turn)) for i in range(devices)] for turn in range(1, CHIPS)]
    send = lambda x, route: lax.ppermute(x, "seq", route)

    kv_near, *t_send = pack_call(head_kind, queries, keys, values, spatial, block, dealt)
    kv_cross = send(kv_near, cross)
    sums = sums_call(queries, keys, t_send[0] if t_send else kv_near)
    k_pair = send(lax.optimization_barrier((keys, kv_near))[0], pair)
    v_pair = send(lax.optimization_barrier((values, kv_near))[0], pair)
    t_got = [send(part, pair) for part in t_send]
    total = sums
    if planes & (planes - 1) == 0:
        for d in [1 << n for n in range(planes.bit_length() - 1)]:
            total = total + lax.ppermute(total, "head", [(i, i ^ d) for i in range(planes)])
    else:
        total = lax.psum(sums, "head")
    pair_total = send(total, pair)
    cross_total = lax.ppermute(
        total,
        ("seq", "head"),
        [(i * planes + p, j * planes + (p ^ 1)) for i, j in cross for p in range(planes)],
    )
    k, *t_own = own_call(
        head_kind, queries, keys, values, query_gain, key_gain, total, t_got, spatial, dealt
    )
    last = k
    if dealt:
        pieces = deal_call(
            head_kind, t_own[0], t_got[0], query_gain, key_gain, pair_total, spatial, block
        )
        arrived = [pieces[0]] + [send(p, r) for p, r in zip(pieces[1:], turned)]
        last = pieces[0]
    kp = pair_call(head_kind, k_pair, key_gain, pair_total, last, spatial)
    near = near_call(
        head_kind, queries, k, values, kp, v_pair, query_gain, total, spatial, block
    )
    operands = (
        queries, k, values, kp, v_pair, kv_cross, query_gain, key_gain, total, cross_total
    )
    half = spatial // 2
    far = far_call(head_kind, operands, near, 0, half, spatial, block)
    last = far
    if dealt:
        results = frames_call(arrived, far)
        parts = [results[0]] + [send(p, r) for p, r in zip(results[1:], turned)]
        last = results[0]
    out, token = rest_call(
        head_kind, operands, near, far, last, half, spatial - half, spatial, block
    )
    if dealt:
        parts += [send(lax.optimization_barrier((p, token))[0], pair) for p in parts]
    else:
        index = lax.axis_index("seq").astype(jnp.int32)
        parts = temporal_folded(
            queries, keys, values, query_gain, key_gain, head_kind, total, spatial, index * rows
        )
    return place_call(head_kind, parts, out, spatial, block)


def solution(mesh):
    placed = (P("seq", "head"), P("seq", "head"), P("seq", "head"), P("head"), P("head"), P("head"))
    return jax.shard_map(
        per_device, mesh=mesh, in_specs=placed, out_specs=P("seq", "head"), check_vma=False
    )
```

```python
import functools
import math

import jax
import jax.numpy as jnp
from jax import lax
from jax.experimental import pallas as pl
from jax.experimental.pallas import tpu as pltpu
from jax.sharding import PartitionSpec as P

HEAD_DIM = 128
D = 5120
FRAME = 1024
OFFSET = 512
VMEM = 24 * 1024 * 1024
VMEM_PACK = 58 * 1024 * 1024
VMEM_SUMS = 32 * 1024 * 1024
LOW = -1e30
LATE = 1
FRAMES_COST = 10000000000
FACTOR = math.log2(math.e) / math.sqrt(HEAD_DIM)
F32 = jnp.float32
BF16 = jnp.bfloat16
ANY = pl.BlockSpec(memory_space=pltpu.HBM)
LOOSE = pl.BlockSpec(memory_space=pl.ANY)
IN_SMEM = pl.BlockSpec(memory_space=pltpu.SMEM)
IN_VMEM = pl.BlockSpec(memory_space=pltpu.VMEM)


def shape(dims, dtype=BF16):
    return jax.ShapeDtypeStruct(dims, dtype)


def call(kernel, name, out_shape, in_specs, out_specs, scratch, operands, aliases=None, cycles=1000, vmem=VMEM):
    return pl.pallas_call(
        kernel,
        out_shape=out_shape,
        in_specs=in_specs,
        out_specs=out_specs,
        scratch_shapes=scratch,
        input_output_aliases=aliases or {},
        compiler_params=pltpu.CompilerParams(vmem_limit_bytes=vmem),
        cost_estimate=pl.CostEstimate(flops=cycles, bytes_accessed=1000, transcendentals=0),
        name=name,
    )(*operands)


def column(ref, head, rows=None):
    lanes = pl.ds(pl.multiple_of(head * HEAD_DIM, HEAD_DIM), HEAD_DIM)
    return ref.at[:, lanes] if rows is None else ref.at[rows, lanes]


def put_order(kind_ref, order_ref, spatial):
    heads = kind_ref.shape[0]

    def step(h, count):
        s, t = count
        temporal = kind_ref[h] == 1
        order_ref[jnp.where(temporal, spatial + t, s)] = h
        return jnp.where(temporal, s, s + 1), jnp.where(temporal, t + 1, t)

    lax.fori_loop(0, heads, step, (jnp.int32(0), jnp.int32(0)))


def order_scratch(heads):
    return pltpu.SMEM((heads,), jnp.int32)


class Place:
    def __init__(self, block=1):
        index = lax.axis_index("seq").astype(jnp.int32)
        self.kind = index % 4
        self.core = index % 2
        self.chip = index // 2
        self.inner = (self.kind == 1) | (self.kind == 2)
        self.apart = jnp.where((self.kind == 0) | (self.kind == 1), 2 * block, 0)
        self.near = jnp.where(self.kind == 0, 2 * block, 0)
        self.far = jnp.where(self.kind == 0, 0, block)
        self.cross = jnp.where(self.kind == 0, 0, block)


def lanes(head):
    return pl.ds(pl.multiple_of(head * HEAD_DIM, HEAD_DIM), HEAD_DIM)


def start_all(copies):
    for copy in copies:
        copy.start()


def wait_all(copies):
    for copy in copies:
        copy.wait()


def pack_kernel(spatial, block, kind_ref, k_any, v_any, early_any, late_any, order, packed, sems):
    put_order(kind_ref, order, spatial)
    place = Place(block)
    across = pl.ds(pl.multiple_of(place.cross, block), 2 * block)
    early = early_any.shape[1]
    each = [(h, i) for h in range(spatial) for i in range(2)]
    ins = [
        pltpu.make_async_copy(
            column((k_any, v_any)[i], order[h], across), packed.at[i, h], sems.at[0, h, i]
        )
        for h, i in each
    ]
    start_all(ins)
    outs = []
    for (h, i), came in zip(each, ins):
        into = early_any.at[i, h] if h < early else late_any.at[i, h - early]
        came.wait()
        outs.append(pltpu.make_async_copy(packed.at[i, h], into, sems.at[1, h, i]))
        outs[-1].start()
    wait_all(outs)


def pack_call(head_kind, keys, values, spatial, late, block):
    return call(
        functools.partial(pack_kernel, spatial, block),
        "pack",
        [shape((2, n, 2 * block, HEAD_DIM)) for n in (spatial - late, late)],
        [IN_SMEM] + [ANY] * 2,
        [ANY] * 2,
        [
            order_scratch(head_kind.shape[0]),
            pltpu.VMEM((2, spatial, 2 * block, HEAD_DIM), BF16),
            pltpu.SemaphoreType.DMA((2, spatial, 2)),
        ],
        (head_kind, keys, values),
        vmem=VMEM_PACK,
    )


def sums_kernel(spatial, dealt, kind_ref, q_ref, k_ref, v_ref, after_ref, sums_ref, *refs):
    order, squares = refs[-2:]
    rows, width = q_ref.shape
    size = HEAD_DIM
    put_order(kind_ref, order, spatial)
    for i, ref in enumerate((q_ref, k_ref)):
        for s in range(rows // size):
            total = None
            for c in range(width // HEAD_DIM):
                x = ref[s * size : (s + 1) * size, c * HEAD_DIM : (c + 1) * HEAD_DIM].astype(F32)
                total = x * x if total is None else total + x * x
            squares[s * size : (s + 1) * size, :] = total
        sums_ref[i : i + 1, :] = jnp.sum(jnp.transpose(squares[...]), axis=0, keepdims=True)
    if dealt:
        one = lanes(order[spatial + 1 - Place().core])
        for i, ref in enumerate((q_ref, k_ref, v_ref)):
            refs[0][i] = ref[:, one]


def sums_call(head_kind, queries, keys, values, after, spatial, dealt):
    rows, width = queries.shape
    outs = [shape((2, rows), F32)]
    if dealt:
        outs.append(shape((3, rows, HEAD_DIM)))
    return call(
        functools.partial(sums_kernel, spatial, dealt),
        "sums",
        outs,
        [IN_SMEM] + [IN_VMEM] * 3 + [LOOSE],
        [IN_VMEM] * len(outs),
        [order_scratch(head_kind.shape[0]), pltpu.VMEM((rows, HEAD_DIM), F32)],
        (head_kind, queries, keys, values, after),
        vmem=VMEM_SUMS,
    )


def row_factors(sums, which, start, size):
    total = None
    for part in sums:
        row = part[which : which + 1, pl.ds(start, size)]
        total = row if total is None else total + row
    inverse = lax.rsqrt(total / D + 1e-06)
    return jnp.transpose(jnp.broadcast_to(inverse, (HEAD_DIM, size)))


def gain_of(gain_ref, head):
    gain = gain_ref[lanes(head)]
    return jnp.broadcast_to(gain[None, :], (8, HEAD_DIM))[0:1, :]


def own_kernel(spatial, dealt, afters, kind_ref, q_ref, k_ref, v_ref, gq_ref, gk_ref, total_ref, *refs):
    ks_ref, (order, factors) = refs[afters], refs[-2:]
    rows = k_ref.shape[0]
    put_order(kind_ref, order, spatial)
    place = Place()
    factors[...] = row_factors([total_ref], 1, 0, rows)
    for h in range(spatial):
        gain = gain_of(gk_ref, order[h])
        ks_ref[h] = (k_ref[:, lanes(order[h])].astype(F32) * factors[...] * gain).astype(BF16)
    if dealt:
        t_ref = refs[afters + 1]
        head = order[spatial + place.core]
        one = lanes(head)
        scale = row_factors([total_ref], 0, 0, rows)
        t_ref[0] = (q_ref[:, one].astype(F32) * scale * (gain_of(gq_ref, head) * FACTOR)).astype(BF16)
        t_ref[1] = (k_ref[:, one].astype(F32) * factors[...] * gain_of(gk_ref, head)).astype(BF16)
        t_ref[2] = v_ref[:, one]


def own_call(head_kind, queries, keys, values, query_gain, key_gain, total, afters, spatial, dealt):
    rows = keys.shape[0]
    outs = [shape((spatial, rows, HEAD_DIM))]
    if dealt:
        outs.append(shape((3, rows, HEAD_DIM)))
    return call(
        functools.partial(own_kernel, spatial, dealt, len(afters)),
        "own",
        outs,
        [IN_SMEM] + [IN_VMEM] * 6 + [LOOSE] * len(afters),
        [IN_VMEM] * len(outs),
        [order_scratch(head_kind.shape[0]), pltpu.VMEM((rows, HEAD_DIM), F32)],
        (head_kind, queries, keys, values, query_gain, key_gain, total, *afters),
    )


def pair_kernel(spatial, kind_ref, k_ref, gain_ref, sums_ref, after_ref, kp_ref, order, factors):
    put_order(kind_ref, order, spatial)
    factors[...] = row_factors([sums_ref], 1, 0, k_ref.shape[0])
    for h in range(spatial):
        gain = gain_of(gain_ref, order[h])
        kp_ref[h] = (k_ref[:, lanes(order[h])].astype(F32) * factors[...] * gain).astype(BF16)


def pair_call(head_kind, keys, gain, sums, after, spatial):
    rows = keys.shape[0]
    return call(
        functools.partial(pair_kernel, spatial),
        "pair",
        shape((spatial, rows, HEAD_DIM)),
        [IN_SMEM] + [IN_VMEM] * 3 + [LOOSE],
        IN_VMEM,
        [order_scratch(head_kind.shape[0]), pltpu.VMEM((rows, HEAD_DIM), F32)],
        (head_kind, keys, gain, sums, after),
    )


def attend_all(work, query_of, keys_of, values_of, put):
    def scores_of(item):
        parts = [
            lax.dot_general(query_of(*item), k, (((1,), (1,)), ((), ())), preferred_element_type=F32)
            for k in keys_of(*item)
        ]
        return jnp.concatenate(parts, axis=1)

    scores = scores_of(work[0])
    for n, item in enumerate(work):
        ahead = scores_of(work[n + 1]) if n + 1 < len(work) else None
        top = jnp.max(scores, axis=1, keepdims=True)
        weights = jnp.exp2(scores - top).astype(BF16)
        value = jnp.concatenate(values_of(*item), axis=0)
        wide = jnp.concatenate([value, jnp.ones_like(value)], axis=1)
        total = jnp.dot(weights, wide, preferred_element_type=F32)
        put(item, (total[:, :HEAD_DIM] / total[:, HEAD_DIM:]).astype(BF16))
        scores = ahead


def query_part(q_ref, gain_ref, factors, head, start, size, part):
    rows = pl.ds(pl.multiple_of(start + part * size, size), size)
    gain = gain_of(gain_ref, head) * FACTOR
    scale = factors[part * size : (part + 1) * size, :]
    return (q_ref[rows, lanes(head)].astype(F32) * scale * gain).astype(BF16)


def near_kernel(spatial, block, kind_ref, q_ref, k_ref, v_ref, kp_ref, v_pair_ref, gain_ref, total_ref, out_ref, order, factors):
    put_order(kind_ref, order, spatial)
    place = Place(block)
    one = pl.ds(pl.multiple_of(place.apart, block), block)
    factors[...] = row_factors([total_ref], 0, pl.multiple_of(place.near, block), block)

    def both(own_ref, pair_ref):
        return (
            jnp.where(place.inner, own_ref[...], pair_ref[...]),
            jnp.where(place.inner, pair_ref[one, :], own_ref[one, :]),
        )

    def values_of(h):
        head = lanes(order[h])
        return both(v_ref.at[:, head], v_pair_ref.at[:, head])

    def put(item, result):
        out_ref[item[0]] = result

    attend_all(
        [(h,) for h in range(spatial)],
        lambda h: query_part(q_ref, gain_ref, factors, order[h], place.near, block, 0),
        lambda h: both(k_ref.at[h], kp_ref.at[h]),
        values_of,
        put,
    )


def near_call(head_kind, q, k, v, k_pair, v_pair, gain, total, spatial, block):
    return call(
        functools.partial(near_kernel, spatial, block),
        "near",
        shape((spatial, block, HEAD_DIM)),
        [IN_SMEM] + [IN_VMEM] * 7,
        IN_VMEM,
        [order_scratch(head_kind.shape[0]), pltpu.VMEM((block, HEAD_DIM), F32)],
        (head_kind, q, k, v, k_pair, v_pair, gain, total),
    )


def far_attention(first, count, block, place, order, refs, put):
    q_ref, k_ref, v_ref, kp_ref, v_pair_ref, gq_ref, gk_ref, total_ref, cross_ref, *refs = refs
    kvx_refs, (factors, x_factors, x_keys) = refs[:-3], refs[-3:]
    early = kvx_refs[0].shape[1]

    def crossed(i, n):
        return kvx_refs[0][i, n] if n < early else kvx_refs[1][i, n - early]

    one = pl.ds(pl.multiple_of(place.apart, block), block)
    start = jnp.where(place.inner, 0, place.far)
    two = pl.ds(pl.multiple_of(start, block), 2 * block)
    factors[...] = row_factors([total_ref], 0, pl.multiple_of(place.far, block), 2 * block)
    sent = pl.multiple_of(jnp.where(place.kind == 0, block, 0), block)
    x_factors[...] = row_factors([cross_ref], 1, sent, 2 * block)

    def three(own_ref, pair_ref, cross):
        return (
            own_ref[two, :],
            jnp.where(place.inner, own_ref[2 * block :, :], cross[:block]),
            jnp.where(place.inner, pair_ref[one, :], cross[block:]),
        )

    def keys_of(h, part):
        n = first + h
        if part == 0:
            gain = gain_of(gk_ref, order[n])
            x_keys[h % 2] = (crossed(0, n).astype(F32) * x_factors[...] * gain).astype(BF16)
        return three(k_ref.at[n], kp_ref.at[n], x_keys[h % 2])

    def values_of(h, part):
        head = lanes(order[first + h])
        return three(v_ref.at[:, head], v_pair_ref.at[:, head], crossed(1, first + h))

    attend_all(
        [(h, part) for h in range(count) for part in range(2)],
        lambda h, part: query_part(q_ref, gq_ref, factors, order[first + h], place.far, block, part),
        keys_of,
        values_of,
        put,
    )


def far_kernel(spatial, first, count, block, kind_ref, *refs):
    operands, (out_ref, order, factors, x_factors, x_keys) = refs[:-6], refs[-5:]
    put_order(kind_ref, order, spatial)
    place = Place(block)

    def put(item, result):
        h, part = item
        out_ref[h, part * block : (part + 1) * block, :] = result

    far_attention(first, count, block, place, order, operands + (factors, x_factors, x_keys), put)


def far_call(head_kind, operands, after, first, count, spatial, block):
    return call(
        functools.partial(far_kernel, spatial, first, count, block),
        "far",
        shape((count, 2 * block, HEAD_DIM)),
        [IN_SMEM] + [IN_VMEM] * len(operands) + [LOOSE],
        IN_VMEM,
        [order_scratch(head_kind.shape[0])]
        + [pltpu.VMEM((2 * block, HEAD_DIM), F32)] * 2
        + [pltpu.VMEM((2, 2 * block, HEAD_DIM), BF16)],
        (head_kind, *operands, after),
    )


def rest_kernel(spatial, first, count, block, given, kind_ref, *refs):
    operands, refs = refs[:given], refs[given:]
    near_ref, far_ref, _, out_ref, token_ref, order, factors, x_factors, x_keys, done, sems = refs
    token_ref[...] = jnp.zeros_like(token_ref)
    put_order(kind_ref, order, spatial)
    place = Place(block)
    near_rows = pl.ds(pl.multiple_of(place.near, block), block)
    far_rows = pl.ds(pl.multiple_of(place.far, block), 2 * block)
    copies = []

    def send(source, head, rows):
        copies.append(
            pltpu.make_async_copy(source, column(out_ref, head, rows), sems.at[len(copies)])
        )
        copies[-1].start()

    for h in range(spatial):
        send(near_ref.at[h], order[h], near_rows)
    for h in range(first):
        send(far_ref.at[h], order[h], far_rows)

    def put(item, result):
        h, part = item
        done[h, part * block : (part + 1) * block, :] = result
        if part == 1:
            send(done.at[h], order[first + h], far_rows)

    far_attention(first, count, block, place, order, operands + (factors, x_factors, x_keys), put)
    wait_all(copies)


def rest_call(head_kind, operands, near, far, after, first, count, spatial, block):
    rows, width = operands[0].shape
    heads = head_kind.shape[0]
    return call(
        functools.partial(rest_kernel, spatial, first, count, block, len(operands)),
        "rest",
        [shape((rows, width)), shape((8, HEAD_DIM), F32)],
        [IN_SMEM] + [IN_VMEM] * (len(operands) + 2) + [LOOSE],
        [ANY, IN_VMEM],
        [
            order_scratch(heads),
            pltpu.VMEM((2 * block, HEAD_DIM), F32),
            pltpu.VMEM((2 * block, HEAD_DIM), F32),
            pltpu.VMEM((2, 2 * block, HEAD_DIM), BF16),
            pltpu.VMEM((count, 2 * block, HEAD_DIM), BF16),
            pltpu.SemaphoreType.DMA((2 * spatial,)),
        ],
        (head_kind, *operands, near, far, after),
    )


def place_kernel(spatial, block, parts, kind_ref, *refs):
    t_refs, (_, out_ref, order, held, sems) = refs[:parts], refs[parts:]
    put_order(kind_ref, order, spatial)
    place = Place(block)
    rows = 3 * block
    copies = []

    def send(source, head):
        copies.append(
            pltpu.make_async_copy(source, column(out_ref, head), sems.at[len(copies)])
        )
        copies[-1].start()

    if parts == 2 * CHIPS:
        for j in range(2):
            for turn in range(CHIPS):
                for g in range(TURNS):
                    piece = (place.chip ^ turn) + CHIPS * g
                    into = pl.ds(pl.multiple_of(piece * PIECE, PIECE), PIECE)
                    held[j, into, :] = t_refs[j * CHIPS + turn][g]
            own = pl.ds(pl.multiple_of(place.core * rows, block), rows)
            send(held.at[j, own], order[spatial + (place.core ^ j)])
    else:
        for j in range(parts):
            send(t_refs[j], order[spatial + j])
    wait_all(copies)


def place_call(head_kind, parts, have, spatial, block):
    heads = head_kind.shape[0]
    return call(
        functools.partial(place_kernel, spatial, block, len(parts)),
        "place",
        shape(have.shape),
        [IN_SMEM] + [IN_VMEM] * len(parts) + [ANY],
        ANY,
        [
            order_scratch(heads),
            pltpu.VMEM((2, 2 * have.shape[0], HEAD_DIM), BF16),
            pltpu.SemaphoreType.DMA((heads - spatial,)),
        ],
        (head_kind, *parts, have),
        aliases={1 + len(parts): 0},
    )


PIECE = 128
CHIPS = 4
TURNS = 3


def deal_kernel(spatial, block, kind_ref, own_ref, got_ref, gq_ref, gk_ref, sums_ref, *refs):
    outs, (order, held) = refs[:CHIPS], refs[CHIPS:]
    put_order(kind_ref, order, spatial)
    place = Place(block)
    rows = own_ref.shape[1]
    head = order[spatial + place.core]
    own = pl.ds(pl.multiple_of(place.core * rows, rows), rows)
    other = pl.ds(pl.multiple_of((1 - place.core) * rows, rows), rows)
    gains = (gain_of(gq_ref, head) * FACTOR, gain_of(gk_ref, head))
    for i in range(2):
        factors = row_factors([sums_ref], i, 0, rows)
        held[i, other, :] = (got_ref[i].astype(F32) * factors * gains[i]).astype(BF16)
    held[2, other, :] = got_ref[2]
    for i in range(3):
        held[i, own, :] = own_ref[i]
    for turn in range(CHIPS):
        owner = place.chip ^ turn
        for g in range(TURNS):
            at = pl.multiple_of((owner + CHIPS * g) * PIECE, PIECE)
            for i in range(3):
                outs[turn][i, g] = held[i, pl.ds(at, PIECE), :]


def deal_call(head_kind, own, got, query_gain, key_gain, sums, spatial, block):
    return call(
        functools.partial(deal_kernel, spatial, block),
        "deal",
        [shape((3, TURNS, PIECE, HEAD_DIM))] * CHIPS,
        [IN_SMEM] + [IN_VMEM] * 5,
        [IN_VMEM] * CHIPS,
        [
            order_scratch(head_kind.shape[0]),
            pltpu.VMEM((3, 2 * own.shape[1], HEAD_DIM), BF16),
        ],
        (head_kind, own, got, query_gain, key_gain, sums),
    )


GROUPS = (
    ((0, 1), (2, 1), (1, 0), (1, 2), (3, 0), (3, 2)),
    ((0, 0), (0, 2), (2, 0), (2, 2), (1, 1), (3, 1)),
)


def frames_kernel(*refs):
    ins, outs = refs[:CHIPS], refs[-CHIPS:]
    side = len(GROUPS[0]) * PIECE
    row = lax.broadcasted_iota(jnp.int32, (PIECE, PIECE), 0)
    col = lax.broadcasted_iota(jnp.int32, (PIECE, PIECE), 1)
    same = jnp.tile(row == col, (1, len(GROUPS[0])))
    half = side // 2
    work = [(n, part) for n in range(len(GROUPS)) for part in range(2)]
    query, key, value = (
        [jnp.concatenate([ins[s][i, g] for s, g in group], axis=0) for group in GROUPS]
        for i in range(3)
    )
    same = jnp.concatenate([same] * (half // PIECE), axis=0)

    def scores_of(n, part):
        return lax.dot_general(
            query[n][part * half : (part + 1) * half],
            key[n],
            (((1,), (1,)), ((), ())),
            preferred_element_type=F32,
        )

    scores = scores_of(*work[0])
    for at, (n, part) in enumerate(work):
        ahead = scores_of(*work[at + 1]) if at + 1 < len(work) else None
        scores = jnp.where(same, scores, LOW)
        top = jnp.max(scores, axis=1, keepdims=True)
        weights = jnp.exp2(scores - top).astype(BF16)
        wide = jnp.concatenate([value[n], jnp.ones_like(value[n])], axis=1)
        total = jnp.dot(weights, wide, preferred_element_type=F32)
        done = (total[:, :HEAD_DIM] / total[:, HEAD_DIM:]).astype(BF16)
        for i in range(half // PIECE):
            s, g = GROUPS[n][part * (half // PIECE) + i]
            outs[s][g] = done[i * PIECE : (i + 1) * PIECE]
        scores = ahead


def frames_call(parts, after):
    return call(
        frames_kernel,
        "frames",
        [shape((TURNS, PIECE, HEAD_DIM))] * CHIPS,
        [IN_VMEM] * CHIPS + [LOOSE],
        [IN_VMEM] * CHIPS,
        [],
        (*parts, after),
        cycles=FRAMES_COST,
    )


def temporal_folded(queries, keys, values, query_gain, key_gain, head_kind, total, spatial, first):
    rows = queries.shape[0]
    heads = head_kind.shape[0]
    count = heads - spatial
    ids = jnp.argsort(head_kind, stable=True)[spatial:]
    take = lambda x: jnp.take(x.reshape(-1, heads, HEAD_DIM), ids, axis=1)
    inverse = lax.rsqrt(total / D + 1e-06)[:, :, None, None]
    norm = lambda x, i, gain: (take(x).astype(F32) * inverse[i] * take(gain)).astype(BF16)
    query = norm(queries, 0, query_gain * FACTOR).astype(F32)
    flat = lambda x: lax.all_gather(x.reshape(rows, -1), "seq", axis=0, tiled=True)
    key_all = flat(norm(keys, 1, key_gain))
    value_all = flat(take(values))
    place = (first + jnp.arange(rows, dtype=jnp.int32)) % FRAME
    running = jnp.full((rows, count), LOW, F32)
    summed = jnp.zeros((rows, count), F32)
    result = jnp.zeros((rows, count, HEAD_DIM), F32)
    for step in range(key_all.shape[0] // FRAME):
        at = place + step * FRAME
        key = jnp.take(key_all, at, axis=0).reshape(rows, count, HEAD_DIM).astype(F32)
        value = jnp.take(value_all, at, axis=0).reshape(rows, count, HEAD_DIM).astype(F32)
        scores = jnp.sum(query * key, axis=2)
        newest = jnp.maximum(running, scores)
        shrink = jnp.exp2(running - newest)
        weight = jnp.exp2(scores - newest)
        summed = summed * shrink + weight
        result = result * shrink[:, :, None] + weight[:, :, None] * value
        running = newest
    done = (result / summed[:, :, None]).astype(BF16)
    return [done[:, j] for j in range(count)]


def per_device(queries, keys, values, query_gain, key_gain, head_kind):
    rows = queries.shape[0]
    heads = head_kind.shape[0]
    temporal = heads // 5
    spatial = heads - temporal
    block = rows // 3
    devices = lax.axis_size("seq")
    planes = lax.axis_size("head")
    dealt = temporal == 2 and devices == 2 * CHIPS and rows == 6 * PIECE
    pair = [(i, i ^ 1) for i in range(devices)]
    cross = []
    for i in range(3, devices, 4):
        after = (i + 1) % devices
        cross += [(i, after), (after, i)]
    turned = [[(i, i ^ (2 * turn)) for i in range(devices)] for turn in range(1, CHIPS)]
    send = lambda x, route: lax.ppermute(x, "seq", route)

    late = LATE
    kv_near, kv_late = pack_call(head_kind, keys, values, spatial, late, block)
    kv_cross = send(kv_near, cross)
    sums, *t_send = sums_call(head_kind, queries, keys, values, kv_late, spatial, dealt)
    k_pair = send(lax.optimization_barrier((keys, kv_near))[0], pair)
    v_pair = send(lax.optimization_barrier((values, kv_near))[0], pair)
    t_got = [send(part, pair) for part in t_send]
    total = sums
    if planes & (planes - 1) == 0:
        for d in [1 << n for n in range(planes.bit_length() - 1)]:
            total = total + lax.ppermute(total, "head", [(i, i ^ d) for i in range(planes)])
    else:
        total = lax.psum(sums, "head")
    pair_total = send(total, pair)
    cross_total = lax.ppermute(
        total,
        ("seq", "head"),
        [(i * planes + p, j * planes + (p ^ 1)) for i, j in cross for p in range(planes)],
    )
    k, *t_own = own_call(
        head_kind, queries, keys, values, query_gain, key_gain, total, t_got, spatial, dealt
    )
    last = k
    if dealt:
        pieces = deal_call(
            head_kind, t_own[0], t_got[0], query_gain, key_gain, pair_total, spatial, block
        )
        arrived = [pieces[0]] + [send(p, r) for p, r in zip(pieces[1:], turned)]
        last = pieces[0]
    kp = pair_call(head_kind, k_pair, key_gain, pair_total, last, spatial)
    near = near_call(
        head_kind, queries, k, values, kp, v_pair, query_gain, total, spatial, block
    )
    operands = (queries, k, values, kp, v_pair, query_gain, key_gain, total, cross_total, kv_cross)
    half = spatial // 2
    far = far_call(head_kind, operands, near, 0, half, spatial, block)
    late_cross = send(lax.optimization_barrier((kv_late, far))[0], cross)
    last = far
    if dealt:
        results = frames_call(arrived, far)
        parts = [send(p, r) for p, r in zip(results[:0:-1], turned[::-1])]
        parts = [results[0]] + parts[::-1]
        last = results[0]
    out, token = rest_call(
        head_kind, operands + (late_cross,), near, far, last, half, spatial - half, spatial, block
    )
    if dealt:
        parts += [send(lax.optimization_barrier((p, token))[0], pair) for p in parts]
    else:
        index = lax.axis_index("seq").astype(jnp.int32)
        parts = temporal_folded(
            queries, keys, values, query_gain, key_gain, head_kind, total, spatial, index * rows
        )
    return place_call(head_kind, parts, out, spatial, block)


def solution(mesh):
    placed = (P("seq", "head"), P("seq", "head"), P("seq", "head"), P("head"), P("head"), P("head"))
    return jax.shard_map(
        per_device, mesh=mesh, in_specs=placed, out_specs=P("seq", "head"), check_vma=False
    )
```

```python
import functools
import math

import jax
import jax.numpy as jnp
from jax import lax
from jax.experimental import pallas as pl
from jax.experimental.pallas import tpu as pltpu
from jax.sharding import PartitionSpec as P

HEAD_DIM = 128
D = 5120
FRAME = 1024
OFFSET = 512
VMEM = 24 * 1024 * 1024
VMEM_PACK = 58 * 1024 * 1024
VMEM_SUMS = 32 * 1024 * 1024
LOW = -1e30
LATE = 1
FRAMES_COST = 10000000000
FACTOR = math.log2(math.e) / math.sqrt(HEAD_DIM)
F32 = jnp.float32
BF16 = jnp.bfloat16
ANY = pl.BlockSpec(memory_space=pltpu.HBM)
LOOSE = pl.BlockSpec(memory_space=pl.ANY)
IN_SMEM = pl.BlockSpec(memory_space=pltpu.SMEM)
IN_VMEM = pl.BlockSpec(memory_space=pltpu.VMEM)


def shape(dims, dtype=BF16):
    return jax.ShapeDtypeStruct(dims, dtype)


def call(kernel, name, out_shape, in_specs, out_specs, scratch, operands, aliases=None, cycles=1000, vmem=VMEM):
    return pl.pallas_call(
        kernel,
        out_shape=out_shape,
        in_specs=in_specs,
        out_specs=out_specs,
        scratch_shapes=scratch,
        input_output_aliases=aliases or {},
        compiler_params=pltpu.CompilerParams(vmem_limit_bytes=vmem),
        cost_estimate=pl.CostEstimate(flops=cycles, bytes_accessed=1000, transcendentals=0),
        name=name,
    )(*operands)


def column(ref, head, rows=None):
    lanes = pl.ds(pl.multiple_of(head * HEAD_DIM, HEAD_DIM), HEAD_DIM)
    return ref.at[:, lanes] if rows is None else ref.at[rows, lanes]


def put_order(kind_ref, order_ref, spatial):
    heads = kind_ref.shape[0]

    def step(h, count):
        s, t = count
        temporal = kind_ref[h] == 1
        order_ref[jnp.where(temporal, spatial + t, s)] = h
        return jnp.where(temporal, s, s + 1), jnp.where(temporal, t + 1, t)

    lax.fori_loop(0, heads, step, (jnp.int32(0), jnp.int32(0)))


def order_scratch(heads):
    return pltpu.SMEM((heads,), jnp.int32)


class Place:
    def __init__(self, block=1):
        index = lax.axis_index("seq").astype(jnp.int32)
        self.kind = index % 4
        self.core = index % 2
        self.chip = index // 2
        self.inner = (self.kind == 1) | (self.kind == 2)
        self.apart = jnp.where((self.kind == 0) | (self.kind == 1), 2 * block, 0)
        self.near = jnp.where(self.kind == 0, 2 * block, 0)
        self.far = jnp.where(self.kind == 0, 0, block)
        self.cross = jnp.where(self.kind == 0, 0, block)


def lanes(head):
    return pl.ds(pl.multiple_of(head * HEAD_DIM, HEAD_DIM), HEAD_DIM)


def start_all(copies):
    for copy in copies:
        copy.start()


def wait_all(copies):
    for copy in copies:
        copy.wait()


def pack_kernel(spatial, block, kind_any, k_any, v_any, early_any, late_any, kind_ref, order, held, sems, in_sems):
    place = Place(block)
    across = pl.ds(pl.multiple_of(place.cross, block), 2 * block)
    ins = [
        pltpu.make_async_copy(ref.at[across, :], held.at[i], in_sems.at[i])
        for i, ref in enumerate((k_any, v_any))
    ]
    kinds = pltpu.make_async_copy(kind_any, kind_ref, in_sems.at[2])
    kinds.start()
    start_all(ins)
    kinds.wait()
    put_order(kind_ref, order, spatial)
    early = early_any.shape[1]
    outs = []
    for i in range(2):
        ins[i].wait()
        for h in range(spatial):
            into = early_any.at[i, h] if h < early else late_any.at[i, h - early]
            outs.append(
                pltpu.make_async_copy(held.at[i, :, lanes(order[h])], into, sems.at[i, h])
            )
            outs[-1].start()
    wait_all(outs)


def pack_call(head_kind, keys, values, spatial, late, block):
    return call(
        functools.partial(pack_kernel, spatial, block),
        "pack",
        [shape((2, n, 2 * block, HEAD_DIM)) for n in (spatial - late, late)],
        [ANY] * 3,
        [ANY] * 2,
        [
            pltpu.SMEM(head_kind.shape, jnp.int32),
            order_scratch(head_kind.shape[0]),
            pltpu.VMEM((2, 2 * block, keys.shape[1]), BF16),
            pltpu.SemaphoreType.DMA((2, spatial)),
            pltpu.SemaphoreType.DMA((3,)),
        ],
        (head_kind, keys, values),
        vmem=VMEM_PACK,
    )


def sums_kernel(spatial, dealt, kind_ref, q_ref, k_ref, v_ref, sums_ref, *refs):
    order, squares = refs[-2:]
    rows, width = q_ref.shape
    size = HEAD_DIM
    put_order(kind_ref, order, spatial)
    for i, ref in enumerate((q_ref, k_ref)):
        for s in range(rows // size):
            total = None
            for c in range(width // HEAD_DIM):
                x = ref[s * size : (s + 1) * size, c * HEAD_DIM : (c + 1) * HEAD_DIM].astype(F32)
                total = x * x if total is None else total + x * x
            squares[s * size : (s + 1) * size, :] = total
        sums_ref[i : i + 1, :] = jnp.sum(jnp.transpose(squares[...]), axis=0, keepdims=True)
    if dealt:
        one = lanes(order[spatial + 1 - Place().core])
        for i, ref in enumerate((q_ref, k_ref, v_ref)):
            refs[0][i] = ref[:, one]


def sums_call(head_kind, queries, keys, values, spatial, dealt):
    rows, width = queries.shape
    outs = [shape((2, rows), F32)]
    if dealt:
        outs.append(shape((3, rows, HEAD_DIM)))
    return call(
        functools.partial(sums_kernel, spatial, dealt),
        "sums",
        outs,
        [IN_SMEM] + [IN_VMEM] * 3,
        [IN_VMEM] * len(outs),
        [order_scratch(head_kind.shape[0]), pltpu.VMEM((rows, HEAD_DIM), F32)],
        (head_kind, queries, keys, values),
        vmem=VMEM_SUMS,
    )


def row_factors(sums, which, start, size):
    total = None
    for part in sums:
        row = part[which : which + 1, pl.ds(start, size)]
        total = row if total is None else total + row
    inverse = lax.rsqrt(total / D + 1e-06)
    return jnp.transpose(jnp.broadcast_to(inverse, (HEAD_DIM, size)))


def gain_of(gain_ref, head):
    gain = gain_ref[lanes(head)]
    return jnp.broadcast_to(gain[None, :], (8, HEAD_DIM))[0:1, :]


def own_kernel(spatial, dealt, afters, kind_ref, q_ref, k_ref, v_ref, gq_ref, gk_ref, total_ref, *refs):
    ks_ref, (order, factors) = refs[afters], refs[-2:]
    rows = k_ref.shape[0]
    put_order(kind_ref, order, spatial)
    place = Place()
    factors[...] = row_factors([total_ref], 1, 0, rows)
    for h in range(spatial):
        gain = gain_of(gk_ref, order[h])
        ks_ref[h] = (k_ref[:, lanes(order[h])].astype(F32) * factors[...] * gain).astype(BF16)
    if dealt:
        t_ref = refs[afters + 1]
        head = order[spatial + place.core]
        one = lanes(head)
        scale = row_factors([total_ref], 0, 0, rows)
        t_ref[0] = (q_ref[:, one].astype(F32) * scale * (gain_of(gq_ref, head) * FACTOR)).astype(BF16)
        t_ref[1] = (k_ref[:, one].astype(F32) * factors[...] * gain_of(gk_ref, head)).astype(BF16)
        t_ref[2] = v_ref[:, one]


def own_call(head_kind, queries, keys, values, query_gain, key_gain, total, afters, spatial, dealt):
    rows = keys.shape[0]
    outs = [shape((spatial, rows, HEAD_DIM))]
    if dealt:
        outs.append(shape((3, rows, HEAD_DIM)))
    return call(
        functools.partial(own_kernel, spatial, dealt, len(afters)),
        "own",
        outs,
        [IN_SMEM] + [IN_VMEM] * 6 + [LOOSE] * len(afters),
        [IN_VMEM] * len(outs),
        [order_scratch(head_kind.shape[0]), pltpu.VMEM((rows, HEAD_DIM), F32)],
        (head_kind, queries, keys, values, query_gain, key_gain, total, *afters),
    )


def pair_kernel(spatial, kind_ref, k_ref, gain_ref, sums_ref, after_ref, kp_ref, order, factors):
    put_order(kind_ref, order, spatial)
    factors[...] = row_factors([sums_ref], 1, 0, k_ref.shape[0])
    for h in range(spatial):
        gain = gain_of(gain_ref, order[h])
        kp_ref[h] = (k_ref[:, lanes(order[h])].astype(F32) * factors[...] * gain).astype(BF16)


def pair_call(head_kind, keys, gain, sums, after, spatial):
    rows = keys.shape[0]
    return call(
        functools.partial(pair_kernel, spatial),
        "pair",
        shape((spatial, rows, HEAD_DIM)),
        [IN_SMEM] + [IN_VMEM] * 3 + [LOOSE],
        IN_VMEM,
        [order_scratch(head_kind.shape[0]), pltpu.VMEM((rows, HEAD_DIM), F32)],
        (head_kind, keys, gain, sums, after),
    )


def attend_all(work, query_of, keys_of, values_of, put):
    def scores_of(item):
        parts = [
            lax.dot_general(query_of(*item), k, (((1,), (1,)), ((), ())), preferred_element_type=F32)
            for k in keys_of(*item)
        ]
        return jnp.concatenate(parts, axis=1)

    scores = scores_of(work[0])
    for n, item in enumerate(work):
        ahead = scores_of(work[n + 1]) if n + 1 < len(work) else None
        top = jnp.max(scores, axis=1, keepdims=True)
        weights = jnp.exp2(scores - top).astype(BF16)
        value = jnp.concatenate(values_of(*item), axis=0)
        wide = jnp.concatenate([value, jnp.ones_like(value)], axis=1)
        total = jnp.dot(weights, wide, preferred_element_type=F32)
        put(item, (total[:, :HEAD_DIM] / total[:, HEAD_DIM:]).astype(BF16))
        scores = ahead


def query_part(q_ref, gain_ref, factors, head, start, size, part):
    rows = pl.ds(pl.multiple_of(start + part * size, size), size)
    gain = gain_of(gain_ref, head) * FACTOR
    scale = factors[part * size : (part + 1) * size, :]
    return (q_ref[rows, lanes(head)].astype(F32) * scale * gain).astype(BF16)


def near_kernel(spatial, block, kind_ref, q_ref, k_ref, v_ref, kp_ref, v_pair_ref, gain_ref, total_ref, out_ref, order, factors):
    put_order(kind_ref, order, spatial)
    place = Place(block)
    one = pl.ds(pl.multiple_of(place.apart, block), block)
    factors[...] = row_factors([total_ref], 0, pl.multiple_of(place.near, block), block)

    def both(own_ref, pair_ref):
        return (
            jnp.where(place.inner, own_ref[...], pair_ref[...]),
            jnp.where(place.inner, pair_ref[one, :], own_ref[one, :]),
        )

    def values_of(h):
        head = lanes(order[h])
        return both(v_ref.at[:, head], v_pair_ref.at[:, head])

    def put(item, result):
        out_ref[item[0]] = result

    attend_all(
        [(h,) for h in range(spatial)],
        lambda h: query_part(q_ref, gain_ref, factors, order[h], place.near, block, 0),
        lambda h: both(k_ref.at[h], kp_ref.at[h]),
        values_of,
        put,
    )


def near_call(head_kind, q, k, v, k_pair, v_pair, gain, total, spatial, block):
    return call(
        functools.partial(near_kernel, spatial, block),
        "near",
        shape((spatial, block, HEAD_DIM)),
        [IN_SMEM] + [IN_VMEM] * 7,
        IN_VMEM,
        [order_scratch(head_kind.shape[0]), pltpu.VMEM((block, HEAD_DIM), F32)],
        (head_kind, q, k, v, k_pair, v_pair, gain, total),
    )


def far_attention(first, count, block, place, order, refs, put):
    q_ref, k_ref, v_ref, kp_ref, v_pair_ref, gq_ref, gk_ref, total_ref, cross_ref, *refs = refs
    kvx_refs, (factors, x_factors, x_keys) = refs[:-3], refs[-3:]
    early = kvx_refs[0].shape[1]

    def crossed(i, n):
        return kvx_refs[0][i, n] if n < early else kvx_refs[1][i, n - early]

    one = pl.ds(pl.multiple_of(place.apart, block), block)
    start = jnp.where(place.inner, 0, place.far)
    two = pl.ds(pl.multiple_of(start, block), 2 * block)
    factors[...] = row_factors([total_ref], 0, pl.multiple_of(place.far, block), 2 * block)
    sent = pl.multiple_of(jnp.where(place.kind == 0, block, 0), block)
    x_factors[...] = row_factors([cross_ref], 1, sent, 2 * block)

    def three(own_ref, pair_ref, cross):
        return (
            own_ref[two, :],
            jnp.where(place.inner, own_ref[2 * block :, :], cross[:block]),
            jnp.where(place.inner, pair_ref[one, :], cross[block:]),
        )

    def keys_of(h, part):
        n = first + h
        if part == 0:
            gain = gain_of(gk_ref, order[n])
            x_keys[h % 2] = (crossed(0, n).astype(F32) * x_factors[...] * gain).astype(BF16)
        return three(k_ref.at[n], kp_ref.at[n], x_keys[h % 2])

    def values_of(h, part):
        head = lanes(order[first + h])
        return three(v_ref.at[:, head], v_pair_ref.at[:, head], crossed(1, first + h))

    attend_all(
        [(h, part) for h in range(count) for part in range(2)],
        lambda h, part: query_part(q_ref, gq_ref, factors, order[first + h], place.far, block, part),
        keys_of,
        values_of,
        put,
    )


def far_kernel(spatial, first, count, block, kind_ref, *refs):
    operands, (out_ref, order, factors, x_factors, x_keys) = refs[:-6], refs[-5:]
    put_order(kind_ref, order, spatial)
    place = Place(block)

    def put(item, result):
        h, part = item
        out_ref[h, part * block : (part + 1) * block, :] = result

    far_attention(first, count, block, place, order, operands + (factors, x_factors, x_keys), put)


def far_call(head_kind, operands, after, first, count, spatial, block):
    return call(
        functools.partial(far_kernel, spatial, first, count, block),
        "far",
        shape((count, 2 * block, HEAD_DIM)),
        [IN_SMEM] + [IN_VMEM] * len(operands) + [LOOSE],
        IN_VMEM,
        [order_scratch(head_kind.shape[0])]
        + [pltpu.VMEM((2 * block, HEAD_DIM), F32)] * 2
        + [pltpu.VMEM((2, 2 * block, HEAD_DIM), BF16)],
        (head_kind, *operands, after),
    )


def rest_kernel(spatial, first, count, block, given, kind_ref, *refs):
    operands, refs = refs[:given], refs[given:]
    near_ref, far_ref, _, out_ref, order, factors, x_factors, x_keys, done, sems = refs
    put_order(kind_ref, order, spatial)
    place = Place(block)
    near_rows = pl.ds(pl.multiple_of(place.near, block), block)
    far_rows = pl.ds(pl.multiple_of(place.far, block), 2 * block)
    copies = []

    def send(source, head, rows):
        copies.append(
            pltpu.make_async_copy(source, column(out_ref, head, rows), sems.at[len(copies)])
        )
        copies[-1].start()

    waiting = [(near_ref.at[h], order[h], near_rows) for h in range(spatial)]
    waiting += [(far_ref.at[h], order[h], far_rows) for h in range(first)]
    some = -(-len(waiting) // (2 * count - 1))

    def put(item, result):
        h, part = item
        done[h, part * block : (part + 1) * block, :] = result
        if part == 1:
            send(done.at[h], order[first + h], far_rows)
        for _ in range(min(some, len(waiting))):
            send(*waiting.pop(0))

    far_attention(first, count, block, place, order, operands + (factors, x_factors, x_keys), put)
    wait_all(copies)


def rest_call(head_kind, operands, near, far, after, first, count, spatial, block):
    rows, width = operands[0].shape
    heads = head_kind.shape[0]
    return call(
        functools.partial(rest_kernel, spatial, first, count, block, len(operands)),
        "rest",
        shape((rows, width)),
        [IN_SMEM] + [IN_VMEM] * (len(operands) + 2) + [LOOSE],
        ANY,
        [
            order_scratch(heads),
            pltpu.VMEM((2 * block, HEAD_DIM), F32),
            pltpu.VMEM((2 * block, HEAD_DIM), F32),
            pltpu.VMEM((2, 2 * block, HEAD_DIM), BF16),
            pltpu.VMEM((count, 2 * block, HEAD_DIM), BF16),
            pltpu.SemaphoreType.DMA((2 * spatial,)),
        ],
        (head_kind, *operands, near, far, after),
    )


def place_kernel(spatial, block, parts, kind_ref, *refs):
    t_refs, (_, out_ref, order, held, sems) = refs[:parts], refs[parts:]
    put_order(kind_ref, order, spatial)
    place = Place(block)
    rows = 3 * block
    copies = []

    def send(source, head):
        copies.append(
            pltpu.make_async_copy(source, column(out_ref, head), sems.at[len(copies)])
        )
        copies[-1].start()

    if parts == 2 * CHIPS:
        for j in range(2):
            for turn in range(CHIPS):
                for g in range(TURNS):
                    piece = (place.chip ^ turn) + CHIPS * g
                    into = pl.ds(pl.multiple_of(piece * PIECE, PIECE), PIECE)
                    held[j, into, :] = t_refs[j * CHIPS + turn][g]
            own = pl.ds(pl.multiple_of(place.core * rows, block), rows)
            send(held.at[j, own], order[spatial + (place.core ^ j)])
    else:
        for j in range(parts):
            send(t_refs[j], order[spatial + j])
    wait_all(copies)


def place_call(head_kind, parts, have, spatial, block):
    heads = head_kind.shape[0]
    return call(
        functools.partial(place_kernel, spatial, block, len(parts)),
        "place",
        shape(have.shape),
        [IN_SMEM] + [IN_VMEM] * len(parts) + [ANY],
        ANY,
        [
            order_scratch(heads),
            pltpu.VMEM((2, 2 * have.shape[0], HEAD_DIM), BF16),
            pltpu.SemaphoreType.DMA((heads - spatial,)),
        ],
        (head_kind, *parts, have),
        aliases={1 + len(parts): 0},
    )


PIECE = 128
CHIPS = 4
TURNS = 3


def deal_kernel(spatial, block, kind_ref, own_ref, got_ref, gq_ref, gk_ref, sums_ref, *refs):
    outs, (order, held) = refs[:CHIPS], refs[CHIPS:]
    put_order(kind_ref, order, spatial)
    place = Place(block)
    rows = own_ref.shape[1]
    head = order[spatial + place.core]
    own = pl.ds(pl.multiple_of(place.core * rows, rows), rows)
    other = pl.ds(pl.multiple_of((1 - place.core) * rows, rows), rows)
    gains = (gain_of(gq_ref, head) * FACTOR, gain_of(gk_ref, head))
    for i in range(2):
        factors = row_factors([sums_ref], i, 0, rows)
        held[i, other, :] = (got_ref[i].astype(F32) * factors * gains[i]).astype(BF16)
    held[2, other, :] = got_ref[2]
    for i in range(3):
        held[i, own, :] = own_ref[i]
    for turn in range(CHIPS):
        owner = place.chip ^ turn
        for g in range(TURNS):
            at = pl.multiple_of((owner + CHIPS * g) * PIECE, PIECE)
            for i in range(3):
                outs[turn][i, g] = held[i, pl.ds(at, PIECE), :]


def deal_call(head_kind, own, got, query_gain, key_gain, sums, spatial, block):
    return call(
        functools.partial(deal_kernel, spatial, block),
        "deal",
        [shape((3, TURNS, PIECE, HEAD_DIM))] * CHIPS,
        [IN_SMEM] + [IN_VMEM] * 5,
        [IN_VMEM] * CHIPS,
        [
            order_scratch(head_kind.shape[0]),
            pltpu.VMEM((3, 2 * own.shape[1], HEAD_DIM), BF16),
        ],
        (head_kind, own, got, query_gain, key_gain, sums),
    )


GROUPS = (
    ((0, 1), (2, 1), (1, 0), (1, 2), (3, 0), (3, 2)),
    ((0, 0), (0, 2), (2, 0), (2, 2), (1, 1), (3, 1)),
)


def frames_kernel(*refs):
    ins, outs = refs[:CHIPS], refs[-CHIPS:]
    side = len(GROUPS[0]) * PIECE
    row = lax.broadcasted_iota(jnp.int32, (PIECE, PIECE), 0)
    col = lax.broadcasted_iota(jnp.int32, (PIECE, PIECE), 1)
    same = jnp.tile(row == col, (1, len(GROUPS[0])))
    half = side // 2
    work = [(n, part) for n in range(len(GROUPS)) for part in range(2)]
    query, key, value = (
        [jnp.concatenate([ins[s][i, g] for s, g in group], axis=0) for group in GROUPS]
        for i in range(3)
    )
    same = jnp.concatenate([same] * (half // PIECE), axis=0)

    def scores_of(n, part):
        return lax.dot_general(
            query[n][part * half : (part + 1) * half],
            key[n],
            (((1,), (1,)), ((), ())),
            preferred_element_type=F32,
        )

    scores = scores_of(*work[0])
    for at, (n, part) in enumerate(work):
        ahead = scores_of(*work[at + 1]) if at + 1 < len(work) else None
        scores = jnp.where(same, scores, LOW)
        top = jnp.max(scores, axis=1, keepdims=True)
        weights = jnp.exp2(scores - top).astype(BF16)
        wide = jnp.concatenate([value[n], jnp.ones_like(value[n])], axis=1)
        total = jnp.dot(weights, wide, preferred_element_type=F32)
        done = (total[:, :HEAD_DIM] / total[:, HEAD_DIM:]).astype(BF16)
        for i in range(half // PIECE):
            s, g = GROUPS[n][part * (half // PIECE) + i]
            outs[s][g] = done[i * PIECE : (i + 1) * PIECE]
        scores = ahead


def frames_call(parts, after):
    return call(
        frames_kernel,
        "frames",
        [shape((TURNS, PIECE, HEAD_DIM))] * CHIPS,
        [IN_VMEM] * CHIPS + [LOOSE],
        [IN_VMEM] * CHIPS,
        [],
        (*parts, after),
        cycles=FRAMES_COST,
    )


def temporal_folded(queries, keys, values, query_gain, key_gain, head_kind, total, spatial, first):
    rows = queries.shape[0]
    heads = head_kind.shape[0]
    count = heads - spatial
    ids = jnp.argsort(head_kind, stable=True)[spatial:]
    take = lambda x: jnp.take(x.reshape(-1, heads, HEAD_DIM), ids, axis=1)
    inverse = lax.rsqrt(total / D + 1e-06)[:, :, None, None]
    norm = lambda x, i, gain: (take(x).astype(F32) * inverse[i] * take(gain)).astype(BF16)
    query = norm(queries, 0, query_gain * FACTOR).astype(F32)
    flat = lambda x: lax.all_gather(x.reshape(rows, -1), "seq", axis=0, tiled=True)
    key_all = flat(norm(keys, 1, key_gain))
    value_all = flat(take(values))
    place = (first + jnp.arange(rows, dtype=jnp.int32)) % FRAME
    running = jnp.full((rows, count), LOW, F32)
    summed = jnp.zeros((rows, count), F32)
    result = jnp.zeros((rows, count, HEAD_DIM), F32)
    for step in range(key_all.shape[0] // FRAME):
        at = place + step * FRAME
        key = jnp.take(key_all, at, axis=0).reshape(rows, count, HEAD_DIM).astype(F32)
        value = jnp.take(value_all, at, axis=0).reshape(rows, count, HEAD_DIM).astype(F32)
        scores = jnp.sum(query * key, axis=2)
        newest = jnp.maximum(running, scores)
        shrink = jnp.exp2(running - newest)
        weight = jnp.exp2(scores - newest)
        summed = summed * shrink + weight
        result = result * shrink[:, :, None] + weight[:, :, None] * value
        running = newest
    done = (result / summed[:, :, None]).astype(BF16)
    return [done[:, j] for j in range(count)]


def per_device(queries, keys, values, query_gain, key_gain, head_kind):
    rows = queries.shape[0]
    heads = head_kind.shape[0]
    temporal = heads // 5
    spatial = heads - temporal
    block = rows // 3
    devices = lax.axis_size("seq")
    planes = lax.axis_size("head")
    dealt = temporal == 2 and devices == 2 * CHIPS and rows == 6 * PIECE
    pair = [(i, i ^ 1) for i in range(devices)]
    cross = []
    for i in range(3, devices, 4):
        after = (i + 1) % devices
        cross += [(i, after), (after, i)]
    turned = [[(i, i ^ (2 * turn)) for i in range(devices)] for turn in range(1, CHIPS)]
    send = lambda x, route: lax.ppermute(x, "seq", route)

    late = LATE
    kv_near, kv_late = pack_call(head_kind, keys, values, spatial, late, block)
    kv_cross = send(kv_near, cross)
    sums, *t_send = sums_call(head_kind, queries, keys, values, spatial, dealt)
    k_pair = send(lax.optimization_barrier((keys, kv_near))[0], pair)
    v_pair = send(lax.optimization_barrier((values, kv_near))[0], pair)
    t_got = [send(part, pair) for part in t_send]
    total = sums
    if planes & (planes - 1) == 0:
        for d in [1 << n for n in range(planes.bit_length() - 1)]:
            total = total + lax.ppermute(total, "head", [(i, i ^ d) for i in range(planes)])
    else:
        total = lax.psum(sums, "head")
    pair_total = send(total, pair)
    cross_total = lax.ppermute(
        total,
        ("seq", "head"),
        [(i * planes + p, j * planes + (p ^ 1)) for i, j in cross for p in range(planes)],
    )
    k, *t_own = own_call(
        head_kind, queries, keys, values, query_gain, key_gain, total, t_got, spatial, dealt
    )
    last = k
    if dealt:
        pieces = deal_call(
            head_kind, t_own[0], t_got[0], query_gain, key_gain, pair_total, spatial, block
        )
        arrived = [pieces[0]] + [send(p, r) for p, r in zip(pieces[1:], turned)]
        last = pieces[0]
    kp = pair_call(head_kind, k_pair, key_gain, pair_total, last, spatial)
    near = near_call(
        head_kind, queries, k, values, kp, v_pair, query_gain, total, spatial, block
    )
    operands = (queries, k, values, kp, v_pair, query_gain, key_gain, total, cross_total, kv_cross)
    half = spatial // 2
    far = far_call(head_kind, operands, near, 0, half, spatial, block)
    late_cross = send(lax.optimization_barrier((kv_late, far))[0], cross)
    last = far
    if dealt:
        results = frames_call(arrived, far)
        parts = [send(p, r) for p, r in zip(results[:0:-1], turned[::-1])]
        parts = [results[0]] + parts[::-1]
        last = results[0]
    out = rest_call(
        head_kind, operands + (late_cross,), near, far, last, half, spatial - half, spatial, block
    )
    if dealt:
        parts += [send(lax.optimization_barrier((p, out))[0], pair) for p in parts]
    else:
        index = lax.axis_index("seq").astype(jnp.int32)
        parts = temporal_folded(
            queries, keys, values, query_gain, key_gain, head_kind, total, spatial, index * rows
        )
    return place_call(head_kind, parts, out, spatial, block)


def solution(mesh):
    placed = (P("seq", "head"), P("seq", "head"), P("seq", "head"), P("head"), P("head"), P("head"))
    return jax.shard_map(
        per_device, mesh=mesh, in_specs=placed, out_specs=P("seq", "head"), check_vma=False
    )
```

```python
import functools
import math

import jax
import jax.numpy as jnp
from jax import lax
from jax.experimental import pallas as pl
from jax.experimental.pallas import tpu as pltpu
from jax.sharding import PartitionSpec as P

HEAD_DIM = 128
D = 5120
FRAME = 1024
OFFSET = 512
VMEM = 24 * 1024 * 1024
VMEM_PACK = 58 * 1024 * 1024
VMEM_SUMS = 32 * 1024 * 1024
LOW = -1e30
LATE = 4
FRAMES_COST = 10000000000
FACTOR = math.log2(math.e) / math.sqrt(HEAD_DIM)
F32 = jnp.float32
BF16 = jnp.bfloat16
ANY = pl.BlockSpec(memory_space=pltpu.HBM)
LOOSE = pl.BlockSpec(memory_space=pl.ANY)
IN_SMEM = pl.BlockSpec(memory_space=pltpu.SMEM)
IN_VMEM = pl.BlockSpec(memory_space=pltpu.VMEM)


def shape(dims, dtype=BF16):
    return jax.ShapeDtypeStruct(dims, dtype)


def call(kernel, name, out_shape, in_specs, out_specs, scratch, operands, aliases=None, cycles=1000, vmem=VMEM):
    return pl.pallas_call(
        kernel,
        out_shape=out_shape,
        in_specs=in_specs,
        out_specs=out_specs,
        scratch_shapes=scratch,
        input_output_aliases=aliases or {},
        compiler_params=pltpu.CompilerParams(vmem_limit_bytes=vmem),
        cost_estimate=pl.CostEstimate(flops=cycles, bytes_accessed=1000, transcendentals=0),
        name=name,
    )(*operands)


def column(ref, head, rows=None):
    lanes = pl.ds(pl.multiple_of(head * HEAD_DIM, HEAD_DIM), HEAD_DIM)
    return ref.at[:, lanes] if rows is None else ref.at[rows, lanes]


def put_order(kind_ref, order_ref, spatial):
    heads = kind_ref.shape[0]

    def step(h, count):
        s, t = count
        temporal = kind_ref[h] == 1
        order_ref[jnp.where(temporal, spatial + t, s)] = h
        return jnp.where(temporal, s, s + 1), jnp.where(temporal, t + 1, t)

    lax.fori_loop(0, heads, step, (jnp.int32(0), jnp.int32(0)))


def order_scratch(heads):
    return pltpu.SMEM((heads,), jnp.int32)


class Place:
    def __init__(self, block=1):
        index = lax.axis_index("seq").astype(jnp.int32)
        self.kind = index % 4
        self.core = index % 2
        self.chip = index // 2
        self.inner = (self.kind == 1) | (self.kind == 2)
        self.apart = jnp.where((self.kind == 0) | (self.kind == 1), 2 * block, 0)
        self.near = jnp.where(self.kind == 0, 2 * block, 0)
        self.far = jnp.where(self.kind == 0, 0, block)
        self.cross = jnp.where(self.kind == 0, 0, block)


def lanes(head):
    return pl.ds(pl.multiple_of(head * HEAD_DIM, HEAD_DIM), HEAD_DIM)


def start_all(copies):
    for copy in copies:
        copy.start()


def wait_all(copies):
    for copy in copies:
        copy.wait()


def pack_kernel(spatial, block, kind_any, k_any, v_any, early_any, late_any, kind_ref, order, held, sems, in_sems):
    place = Place(block)
    across = pl.ds(pl.multiple_of(place.cross, block), 2 * block)
    ins = [
        pltpu.make_async_copy(ref.at[across, :], held.at[i], in_sems.at[i])
        for i, ref in enumerate((k_any, v_any))
    ]
    kinds = pltpu.make_async_copy(kind_any, kind_ref, in_sems.at[2])
    kinds.start()
    start_all(ins)
    kinds.wait()
    put_order(kind_ref, order, spatial)
    early = early_any.shape[1]
    outs = []
    for i in range(2):
        ins[i].wait()
        for h in range(spatial):
            into = early_any.at[i, h] if h < early else late_any.at[i, h - early]
            outs.append(
                pltpu.make_async_copy(held.at[i, :, lanes(order[h])], into, sems.at[i, h])
            )
            outs[-1].start()
    wait_all(outs)


def pack_call(head_kind, keys, values, spatial, late, block):
    return call(
        functools.partial(pack_kernel, spatial, block),
        "pack",
        [shape((2, n, 2 * block, HEAD_DIM)) for n in (spatial - late, late)],
        [ANY] * 3,
        [ANY] * 2,
        [
            pltpu.SMEM(head_kind.shape, jnp.int32),
            order_scratch(head_kind.shape[0]),
            pltpu.VMEM((2, 2 * block, keys.shape[1]), BF16),
            pltpu.SemaphoreType.DMA((2, spatial)),
            pltpu.SemaphoreType.DMA((3,)),
        ],
        (head_kind, keys, values),
        vmem=VMEM_PACK,
    )


def row_sums(ref, squares):
    rows, width = ref.shape
    size = HEAD_DIM
    for s in range(rows // size):
        total = None
        for c in range(width // HEAD_DIM):
            x = ref[s * size : (s + 1) * size, c * HEAD_DIM : (c + 1) * HEAD_DIM].astype(F32)
            total = x * x if total is None else total + x * x
        squares[s * size : (s + 1) * size, :] = total
    return jnp.sum(jnp.transpose(squares[...]), axis=0, keepdims=True)


def key_sums_kernel(k_ref, sums_ref, squares):
    sums_ref[...] = row_sums(k_ref, squares)


def sums_kernel(spatial, dealt, kind_ref, q_ref, k_ref, v_ref, key_sums_ref, sums_ref, *refs):
    order, squares = refs[-2:]
    put_order(kind_ref, order, spatial)
    sums_ref[0:1, :] = row_sums(q_ref, squares)
    sums_ref[1:2, :] = key_sums_ref[...]
    if dealt:
        one = lanes(order[spatial + 1 - Place().core])
        for i, ref in enumerate((q_ref, k_ref, v_ref)):
            refs[0][i] = ref[:, one]


def sums_call(head_kind, queries, keys, values, spatial, dealt):
    rows, width = queries.shape
    key_sums = call(
        key_sums_kernel,
        "key_sums",
        shape((1, rows), F32),
        [IN_VMEM],
        IN_VMEM,
        [pltpu.VMEM((rows, HEAD_DIM), F32)],
        (keys,),
        vmem=VMEM_SUMS,
    )
    outs = [shape((2, rows), F32)]
    if dealt:
        outs.append(shape((3, rows, HEAD_DIM)))
    return call(
        functools.partial(sums_kernel, spatial, dealt),
        "sums",
        outs,
        [IN_SMEM] + [IN_VMEM] * 4,
        [IN_VMEM] * len(outs),
        [order_scratch(head_kind.shape[0]), pltpu.VMEM((rows, HEAD_DIM), F32)],
        (head_kind, queries, keys, values, key_sums),
        vmem=VMEM_SUMS,
    )


def row_factors(sums, which, start, size):
    total = None
    for part in sums:
        row = part[which : which + 1, pl.ds(start, size)]
        total = row if total is None else total + row
    inverse = lax.rsqrt(total / D + 1e-06)
    return jnp.transpose(jnp.broadcast_to(inverse, (HEAD_DIM, size)))


def gain_of(gain_ref, head):
    gain = gain_ref[lanes(head)]
    return jnp.broadcast_to(gain[None, :], (8, HEAD_DIM))[0:1, :]


def own_kernel(spatial, dealt, afters, kind_ref, q_ref, k_ref, v_ref, gq_ref, gk_ref, total_ref, *refs):
    ks_ref, (order, factors) = refs[afters], refs[-2:]
    rows = k_ref.shape[0]
    put_order(kind_ref, order, spatial)
    place = Place()
    factors[...] = row_factors([total_ref], 1, 0, rows)
    for h in range(spatial):
        gain = gain_of(gk_ref, order[h])
        ks_ref[h] = (k_ref[:, lanes(order[h])].astype(F32) * factors[...] * gain).astype(BF16)
    if dealt:
        t_ref = refs[afters + 1]
        head = order[spatial + place.core]
        one = lanes(head)
        scale = row_factors([total_ref], 0, 0, rows)
        t_ref[0] = (q_ref[:, one].astype(F32) * scale * (gain_of(gq_ref, head) * FACTOR)).astype(BF16)
        t_ref[1] = (k_ref[:, one].astype(F32) * factors[...] * gain_of(gk_ref, head)).astype(BF16)
        t_ref[2] = v_ref[:, one]


def own_call(head_kind, queries, keys, values, query_gain, key_gain, total, afters, spatial, dealt):
    rows = keys.shape[0]
    outs = [shape((spatial, rows, HEAD_DIM))]
    if dealt:
        outs.append(shape((3, rows, HEAD_DIM)))
    return call(
        functools.partial(own_kernel, spatial, dealt, len(afters)),
        "own",
        outs,
        [IN_SMEM] + [IN_VMEM] * 6 + [LOOSE] * len(afters),
        [IN_VMEM] * len(outs),
        [order_scratch(head_kind.shape[0]), pltpu.VMEM((rows, HEAD_DIM), F32)],
        (head_kind, queries, keys, values, query_gain, key_gain, total, *afters),
    )


def pair_kernel(spatial, kind_ref, k_ref, gain_ref, sums_ref, after_ref, kp_ref, order, factors):
    put_order(kind_ref, order, spatial)
    factors[...] = row_factors([sums_ref], 1, 0, k_ref.shape[0])
    for h in range(spatial):
        gain = gain_of(gain_ref, order[h])
        kp_ref[h] = (k_ref[:, lanes(order[h])].astype(F32) * factors[...] * gain).astype(BF16)


def pair_call(head_kind, keys, gain, sums, after, spatial):
    rows = keys.shape[0]
    return call(
        functools.partial(pair_kernel, spatial),
        "pair",
        shape((spatial, rows, HEAD_DIM)),
        [IN_SMEM] + [IN_VMEM] * 3 + [LOOSE],
        IN_VMEM,
        [order_scratch(head_kind.shape[0]), pltpu.VMEM((rows, HEAD_DIM), F32)],
        (head_kind, keys, gain, sums, after),
    )


def attend_all(work, query_of, keys_of, values_of, put):
    def scores_of(item):
        parts = [
            lax.dot_general(query_of(*item), k, (((1,), (1,)), ((), ())), preferred_element_type=F32)
            for k in keys_of(*item)
        ]
        return jnp.concatenate(parts, axis=1)

    scores = scores_of(work[0])
    for n, item in enumerate(work):
        ahead = scores_of(work[n + 1]) if n + 1 < len(work) else None
        top = jnp.max(scores, axis=1, keepdims=True)
        weights = jnp.exp2(scores - top).astype(BF16)
        value = jnp.concatenate(values_of(*item), axis=0)
        wide = jnp.concatenate([value, jnp.ones_like(value)], axis=1)
        total = jnp.dot(weights, wide, preferred_element_type=F32)
        put(item, (total[:, :HEAD_DIM] / total[:, HEAD_DIM:]).astype(BF16))
        scores = ahead


def query_part(q_ref, gain_ref, factors, head, start, size, part):
    rows = pl.ds(pl.multiple_of(start + part * size, size), size)
    gain = gain_of(gain_ref, head) * FACTOR
    scale = factors[part * size : (part + 1) * size, :]
    return (q_ref[rows, lanes(head)].astype(F32) * scale * gain).astype(BF16)


def near_kernel(spatial, block, kind_ref, q_ref, k_ref, v_ref, kp_ref, v_pair_ref, gain_ref, total_ref, out_ref, order, factors):
    put_order(kind_ref, order, spatial)
    place = Place(block)
    one = pl.ds(pl.multiple_of(place.apart, block), block)
    factors[...] = row_factors([total_ref], 0, pl.multiple_of(place.near, block), block)

    def both(own_ref, pair_ref):
        return (
            jnp.where(place.inner, own_ref[...], pair_ref[...]),
            jnp.where(place.inner, pair_ref[one, :], own_ref[one, :]),
        )

    def values_of(h):
        head = lanes(order[h])
        return both(v_ref.at[:, head], v_pair_ref.at[:, head])

    def put(item, result):
        out_ref[item[0]] = result

    attend_all(
        [(h,) for h in range(spatial)],
        lambda h: query_part(q_ref, gain_ref, factors, order[h], place.near, block, 0),
        lambda h: both(k_ref.at[h], kp_ref.at[h]),
        values_of,
        put,
    )


def near_call(head_kind, q, k, v, k_pair, v_pair, gain, total, spatial, block):
    return call(
        functools.partial(near_kernel, spatial, block),
        "near",
        shape((spatial, block, HEAD_DIM)),
        [IN_SMEM] + [IN_VMEM] * 7,
        IN_VMEM,
        [order_scratch(head_kind.shape[0]), pltpu.VMEM((block, HEAD_DIM), F32)],
        (head_kind, q, k, v, k_pair, v_pair, gain, total),
    )


def far_attention(first, count, block, place, order, refs, put):
    q_ref, k_ref, v_ref, kp_ref, v_pair_ref, gq_ref, gk_ref, total_ref, cross_ref, *refs = refs
    kvx_refs, (factors, x_factors, x_keys) = refs[:-3], refs[-3:]
    early = kvx_refs[0].shape[1]

    def crossed(i, n):
        return kvx_refs[0][i, n] if n < early else kvx_refs[1][i, n - early]

    one = pl.ds(pl.multiple_of(place.apart, block), block)
    start = jnp.where(place.inner, 0, place.far)
    two = pl.ds(pl.multiple_of(start, block), 2 * block)
    factors[...] = row_factors([total_ref], 0, pl.multiple_of(place.far, block), 2 * block)
    sent = pl.multiple_of(jnp.where(place.kind == 0, block, 0), block)
    x_factors[...] = row_factors([cross_ref], 1, sent, 2 * block)

    def three(own_ref, pair_ref, cross):
        return (
            own_ref[two, :],
            jnp.where(place.inner, own_ref[2 * block :, :], cross[:block]),
            jnp.where(place.inner, pair_ref[one, :], cross[block:]),
        )

    def keys_of(h, part):
        n = first + h
        if part == 0:
            gain = gain_of(gk_ref, order[n])
            x_keys[h % 2] = (crossed(0, n).astype(F32) * x_factors[...] * gain).astype(BF16)
        return three(k_ref.at[n], kp_ref.at[n], x_keys[h % 2])

    def values_of(h, part):
        head = lanes(order[first + h])
        return three(v_ref.at[:, head], v_pair_ref.at[:, head], crossed(1, first + h))

    attend_all(
        [(h, part) for h in range(count) for part in range(2)],
        lambda h, part: query_part(q_ref, gq_ref, factors, order[first + h], place.far, block, part),
        keys_of,
        values_of,
        put,
    )


def far_kernel(spatial, first, count, block, kind_ref, *refs):
    operands, (out_ref, order, factors, x_factors, x_keys) = refs[:-6], refs[-5:]
    put_order(kind_ref, order, spatial)
    place = Place(block)

    def put(item, result):
        h, part = item
        out_ref[h, part * block : (part + 1) * block, :] = result

    far_attention(first, count, block, place, order, operands + (factors, x_factors, x_keys), put)


def far_call(head_kind, operands, after, first, count, spatial, block):
    return call(
        functools.partial(far_kernel, spatial, first, count, block),
        "far",
        shape((count, 2 * block, HEAD_DIM)),
        [IN_SMEM] + [IN_VMEM] * len(operands) + [LOOSE],
        IN_VMEM,
        [order_scratch(head_kind.shape[0])]
        + [pltpu.VMEM((2 * block, HEAD_DIM), F32)] * 2
        + [pltpu.VMEM((2, 2 * block, HEAD_DIM), BF16)],
        (head_kind, *operands, after),
    )


def rest_kernel(spatial, first, count, block, given, kind_ref, *refs):
    operands, refs = refs[:given], refs[given:]
    near_ref, far_ref, mid_ref, out_ref, order, factors, x_factors, x_keys, done, sems = refs
    put_order(kind_ref, order, spatial)
    place = Place(block)
    near_rows = pl.ds(pl.multiple_of(place.near, block), block)
    far_rows = pl.ds(pl.multiple_of(place.far, block), 2 * block)
    copies = []

    def send(source, head, rows):
        copies.append(
            pltpu.make_async_copy(source, column(out_ref, head, rows), sems.at[len(copies)])
        )
        copies[-1].start()

    waiting = [(near_ref.at[h], order[h], near_rows) for h in range(spatial)]
    for at, ref in ((0, far_ref), (far_ref.shape[0], mid_ref)):
        waiting += [(ref.at[h], order[at + h], far_rows) for h in range(ref.shape[0])]
    some = -(-len(waiting) // (2 * count - 1))

    def put(item, result):
        h, part = item
        done[h, part * block : (part + 1) * block, :] = result
        if part == 1:
            send(done.at[h], order[first + h], far_rows)
        for _ in range(min(some, len(waiting))):
            send(*waiting.pop(0))

    far_attention(first, count, block, place, order, operands + (factors, x_factors, x_keys), put)
    wait_all(copies)


def rest_call(head_kind, operands, near, far, mid, first, count, spatial, block):
    rows, width = operands[0].shape
    heads = head_kind.shape[0]
    return call(
        functools.partial(rest_kernel, spatial, first, count, block, len(operands)),
        "rest",
        shape((rows, width)),
        [IN_SMEM] + [IN_VMEM] * (len(operands) + 3),
        ANY,
        [
            order_scratch(heads),
            pltpu.VMEM((2 * block, HEAD_DIM), F32),
            pltpu.VMEM((2 * block, HEAD_DIM), F32),
            pltpu.VMEM((2, 2 * block, HEAD_DIM), BF16),
            pltpu.VMEM((count, 2 * block, HEAD_DIM), BF16),
            pltpu.SemaphoreType.DMA((2 * spatial,)),
        ],
        (head_kind, *operands, near, far, mid),
    )


def place_kernel(spatial, block, parts, kind_ref, *refs):
    t_refs, (_, out_ref, order, held, sems) = refs[:parts], refs[parts:]
    put_order(kind_ref, order, spatial)
    place = Place(block)
    rows = 3 * block
    copies = []

    def send(source, head):
        copies.append(
            pltpu.make_async_copy(source, column(out_ref, head), sems.at[len(copies)])
        )
        copies[-1].start()

    if parts == 2 * CHIPS:
        for j in range(2):
            for turn in range(CHIPS):
                for g in range(TURNS):
                    piece = (place.chip ^ turn) + CHIPS * g
                    into = pl.ds(pl.multiple_of(piece * PIECE, PIECE), PIECE)
                    held[j, into, :] = t_refs[j * CHIPS + turn][g]
            own = pl.ds(pl.multiple_of(place.core * rows, block), rows)
            send(held.at[j, own], order[spatial + (place.core ^ j)])
    else:
        for j in range(parts):
            send(t_refs[j], order[spatial + j])
    wait_all(copies)


def place_call(head_kind, parts, have, spatial, block):
    heads = head_kind.shape[0]
    return call(
        functools.partial(place_kernel, spatial, block, len(parts)),
        "place",
        shape(have.shape),
        [IN_SMEM] + [IN_VMEM] * len(parts) + [ANY],
        ANY,
        [
            order_scratch(heads),
            pltpu.VMEM((2, 2 * have.shape[0], HEAD_DIM), BF16),
            pltpu.SemaphoreType.DMA((heads - spatial,)),
        ],
        (head_kind, *parts, have),
        aliases={1 + len(parts): 0},
    )


PIECE = 128
CHIPS = 4
TURNS = 3


def deal_kernel(spatial, block, kind_ref, own_ref, got_ref, gq_ref, gk_ref, sums_ref, *refs):
    outs, (order, held) = refs[:CHIPS], refs[CHIPS:]
    put_order(kind_ref, order, spatial)
    place = Place(block)
    rows = own_ref.shape[1]
    head = order[spatial + place.core]
    own = pl.ds(pl.multiple_of(place.core * rows, rows), rows)
    other = pl.ds(pl.multiple_of((1 - place.core) * rows, rows), rows)
    gains = (gain_of(gq_ref, head) * FACTOR, gain_of(gk_ref, head))
    for i in range(2):
        factors = row_factors([sums_ref], i, 0, rows)
        held[i, other, :] = (got_ref[i].astype(F32) * factors * gains[i]).astype(BF16)
    held[2, other, :] = got_ref[2]
    for i in range(3):
        held[i, own, :] = own_ref[i]
    for turn in range(CHIPS):
        owner = place.chip ^ turn
        for g in range(TURNS):
            at = pl.multiple_of((owner + CHIPS * g) * PIECE, PIECE)
            for i in range(3):
                outs[turn][i, g] = held[i, pl.ds(at, PIECE), :]


def deal_call(head_kind, own, got, query_gain, key_gain, sums, spatial, block):
    return call(
        functools.partial(deal_kernel, spatial, block),
        "deal",
        [shape((3, TURNS, PIECE, HEAD_DIM))] * CHIPS,
        [IN_SMEM] + [IN_VMEM] * 5,
        [IN_VMEM] * CHIPS,
        [
            order_scratch(head_kind.shape[0]),
            pltpu.VMEM((3, 2 * own.shape[1], HEAD_DIM), BF16),
        ],
        (head_kind, own, got, query_gain, key_gain, sums),
    )


GROUPS = (
    ((0, 1), (2, 1), (1, 0), (1, 2), (3, 0), (3, 2)),
    ((0, 0), (0, 2), (2, 0), (2, 2), (1, 1), (3, 1)),
)


def frames_kernel(*refs):
    ins, outs = refs[:CHIPS], refs[-CHIPS:]
    side = len(GROUPS[0]) * PIECE
    row = lax.broadcasted_iota(jnp.int32, (PIECE, PIECE), 0)
    col = lax.broadcasted_iota(jnp.int32, (PIECE, PIECE), 1)
    same = jnp.tile(row == col, (1, len(GROUPS[0])))
    half = side // 2
    work = [(n, part) for n in range(len(GROUPS)) for part in range(2)]
    query, key, value = (
        [jnp.concatenate([ins[s][i, g] for s, g in group], axis=0) for group in GROUPS]
        for i in range(3)
    )
    same = jnp.concatenate([same] * (half // PIECE), axis=0)

    def scores_of(n, part):
        return lax.dot_general(
            query[n][part * half : (part + 1) * half],
            key[n],
            (((1,), (1,)), ((), ())),
            preferred_element_type=F32,
        )

    scores = scores_of(*work[0])
    for at, (n, part) in enumerate(work):
        ahead = scores_of(*work[at + 1]) if at + 1 < len(work) else None
        scores = jnp.where(same, scores, LOW)
        top = jnp.max(scores, axis=1, keepdims=True)
        weights = jnp.exp2(scores - top).astype(BF16)
        wide = jnp.concatenate([value[n], jnp.ones_like(value[n])], axis=1)
        total = jnp.dot(weights, wide, preferred_element_type=F32)
        done = (total[:, :HEAD_DIM] / total[:, HEAD_DIM:]).astype(BF16)
        for i in range(half // PIECE):
            s, g = GROUPS[n][part * (half // PIECE) + i]
            outs[s][g] = done[i * PIECE : (i + 1) * PIECE]
        scores = ahead


def frames_call(parts, after):
    return call(
        frames_kernel,
        "frames",
        [shape((TURNS, PIECE, HEAD_DIM))] * CHIPS,
        [IN_VMEM] * CHIPS + [LOOSE],
        [IN_VMEM] * CHIPS,
        [],
        (*parts, after),
        cycles=FRAMES_COST,
    )


def temporal_folded(queries, keys, values, query_gain, key_gain, head_kind, total, spatial, first):
    rows = queries.shape[0]
    heads = head_kind.shape[0]
    count = heads - spatial
    ids = jnp.argsort(head_kind, stable=True)[spatial:]
    take = lambda x: jnp.take(x.reshape(-1, heads, HEAD_DIM), ids, axis=1)
    inverse = lax.rsqrt(total / D + 1e-06)[:, :, None, None]
    norm = lambda x, i, gain: (take(x).astype(F32) * inverse[i] * take(gain)).astype(BF16)
    query = norm(queries, 0, query_gain * FACTOR).astype(F32)
    flat = lambda x: lax.all_gather(x.reshape(rows, -1), "seq", axis=0, tiled=True)
    key_all = flat(norm(keys, 1, key_gain))
    value_all = flat(take(values))
    place = (first + jnp.arange(rows, dtype=jnp.int32)) % FRAME
    running = jnp.full((rows, count), LOW, F32)
    summed = jnp.zeros((rows, count), F32)
    result = jnp.zeros((rows, count, HEAD_DIM), F32)
    for step in range(key_all.shape[0] // FRAME):
        at = place + step * FRAME
        key = jnp.take(key_all, at, axis=0).reshape(rows, count, HEAD_DIM).astype(F32)
        value = jnp.take(value_all, at, axis=0).reshape(rows, count, HEAD_DIM).astype(F32)
        scores = jnp.sum(query * key, axis=2)
        newest = jnp.maximum(running, scores)
        shrink = jnp.exp2(running - newest)
        weight = jnp.exp2(scores - newest)
        summed = summed * shrink + weight
        result = result * shrink[:, :, None] + weight[:, :, None] * value
        running = newest
    done = (result / summed[:, :, None]).astype(BF16)
    return [done[:, j] for j in range(count)]


def per_device(queries, keys, values, query_gain, key_gain, head_kind):
    rows = queries.shape[0]
    heads = head_kind.shape[0]
    temporal = heads // 5
    spatial = heads - temporal
    block = rows // 3
    devices = lax.axis_size("seq")
    planes = lax.axis_size("head")
    dealt = temporal == 2 and devices == 2 * CHIPS and rows == 6 * PIECE
    pair = [(i, i ^ 1) for i in range(devices)]
    cross = []
    for i in range(3, devices, 4):
        after = (i + 1) % devices
        cross += [(i, after), (after, i)]
    turned = [[(i, i ^ (2 * turn)) for i in range(devices)] for turn in range(1, CHIPS)]
    send = lambda x, route: lax.ppermute(x, "seq", route)

    late = spatial // LATE
    kv_near, kv_late = pack_call(head_kind, keys, values, spatial, late, block)
    kv_cross = send(kv_near, cross)
    sums, *t_send = sums_call(head_kind, queries, keys, values, spatial, dealt)
    k_pair = send(lax.optimization_barrier((keys, kv_near))[0], pair)
    v_pair = send(lax.optimization_barrier((values, kv_near))[0], pair)
    t_got = [send(part, pair) for part in t_send]
    total = sums
    if planes & (planes - 1) == 0:
        for d in [1 << n for n in range(planes.bit_length() - 1)]:
            total = total + lax.ppermute(total, "head", [(i, i ^ d) for i in range(planes)])
    else:
        total = lax.psum(sums, "head")
    pair_total = send(total, pair)
    cross_total = lax.ppermute(
        total,
        ("seq", "head"),
        [(i * planes + p, j * planes + (p ^ 1)) for i, j in cross for p in range(planes)],
    )
    k, *t_own = own_call(
        head_kind, queries, keys, values, query_gain, key_gain, total, t_got, spatial, dealt
    )
    last = k
    if dealt:
        pieces = deal_call(
            head_kind, t_own[0], t_got[0], query_gain, key_gain, pair_total, spatial, block
        )
        arrived = [pieces[0]] + [send(p, r) for p, r in zip(pieces[1:], turned)]
        last = pieces[0]
    kp = pair_call(head_kind, k_pair, key_gain, pair_total, last, spatial)
    near = near_call(
        head_kind, queries, k, values, kp, v_pair, query_gain, total, spatial, block
    )
    operands = (queries, k, values, kp, v_pair, query_gain, key_gain, total, cross_total, kv_cross)
    half = spatial // 2
    far = far_call(head_kind, operands, near, 0, half, spatial, block)
    late_cross = send(lax.optimization_barrier((kv_late, far))[0], cross)
    last = far
    if dealt:
        results = frames_call(arrived, far)
        parts = [send(p, r) for p, r in zip(results[:0:-1], turned[::-1])]
        parts = [results[0]] + parts[::-1]
        last = results[0]
    mid = far_call(head_kind, operands, last, half, half - late, spatial, block)
    out = rest_call(
        head_kind, operands + (late_cross,), near, far, mid, spatial - late, late, spatial, block
    )
    if dealt:
        parts += [send(parts[0], pair)] + [
            send(lax.optimization_barrier((p, out))[0], pair) for p in parts[1:]
        ]
    else:
        index = lax.axis_index("seq").astype(jnp.int32)
        parts = temporal_folded(
            queries, keys, values, query_gain, key_gain, head_kind, total, spatial, index * rows
        )
    return place_call(head_kind, parts, out, spatial, block)


def solution(mesh):
    placed = (P("seq", "head"), P("seq", "head"), P("seq", "head"), P("head"), P("head"), P("head"))
    return jax.shard_map(
        per_device, mesh=mesh, in_specs=placed, out_specs=P("seq", "head"), check_vma=False
    )
```

```python
import functools
import math

import jax
import jax.numpy as jnp
from jax import lax
from jax.experimental import pallas as pl
from jax.experimental.pallas import tpu as pltpu
from jax.sharding import PartitionSpec as P

HEAD_DIM = 128
D = 5120
FRAME = 1024
OFFSET = 512
VMEM = 24 * 1024 * 1024
VMEM_PACK = 58 * 1024 * 1024
VMEM_SUMS = 32 * 1024 * 1024
LOW = -1e30
LATE = 4
FRAMES_COST = 10000000000
FACTOR = math.log2(math.e) / math.sqrt(HEAD_DIM)
F32 = jnp.float32
BF16 = jnp.bfloat16
ANY = pl.BlockSpec(memory_space=pltpu.HBM)
LOOSE = pl.BlockSpec(memory_space=pl.ANY)
IN_SMEM = pl.BlockSpec(memory_space=pltpu.SMEM)
IN_VMEM = pl.BlockSpec(memory_space=pltpu.VMEM)


def shape(dims, dtype=BF16):
    return jax.ShapeDtypeStruct(dims, dtype)


def call(kernel, name, out_shape, in_specs, out_specs, scratch, operands, aliases=None, cycles=1000, vmem=VMEM):
    return pl.pallas_call(
        kernel,
        out_shape=out_shape,
        in_specs=in_specs,
        out_specs=out_specs,
        scratch_shapes=scratch,
        input_output_aliases=aliases or {},
        compiler_params=pltpu.CompilerParams(vmem_limit_bytes=vmem),
        cost_estimate=pl.CostEstimate(flops=cycles, bytes_accessed=1000, transcendentals=0),
        name=name,
    )(*operands)


def column(ref, head, rows=None):
    lanes = pl.ds(pl.multiple_of(head * HEAD_DIM, HEAD_DIM), HEAD_DIM)
    return ref.at[:, lanes] if rows is None else ref.at[rows, lanes]


def put_order(kind_ref, order_ref, spatial):
    heads = kind_ref.shape[0]

    def step(h, count):
        s, t = count
        temporal = kind_ref[h] == 1
        order_ref[jnp.where(temporal, spatial + t, s)] = h
        return jnp.where(temporal, s, s + 1), jnp.where(temporal, t + 1, t)

    lax.fori_loop(0, heads, step, (jnp.int32(0), jnp.int32(0)))


def order_scratch(heads):
    return pltpu.SMEM((heads,), jnp.int32)


class Place:
    def __init__(self, block=1):
        index = lax.axis_index("seq").astype(jnp.int32)
        self.kind = index % 4
        self.core = index % 2
        self.chip = index // 2
        self.inner = (self.kind == 1) | (self.kind == 2)
        self.apart = jnp.where((self.kind == 0) | (self.kind == 1), 2 * block, 0)
        self.near = jnp.where(self.kind == 0, 2 * block, 0)
        self.far = jnp.where(self.kind == 0, 0, block)
        self.cross = jnp.where(self.kind == 0, 0, block)


def lanes(head):
    return pl.ds(pl.multiple_of(head * HEAD_DIM, HEAD_DIM), HEAD_DIM)


def start_all(copies):
    for copy in copies:
        copy.start()


def wait_all(copies):
    for copy in copies:
        copy.wait()


def pack_kernel(spatial, block, kind_any, k_any, v_any, early_any, late_any, kind_ref, order, held, sems, in_sems):
    place = Place(block)
    across = pl.ds(pl.multiple_of(place.cross, block), 2 * block)
    ins = [
        pltpu.make_async_copy(ref.at[across, :], held.at[i], in_sems.at[i])
        for i, ref in enumerate((k_any, v_any))
    ]
    kinds = pltpu.make_async_copy(kind_any, kind_ref, in_sems.at[2])
    kinds.start()
    start_all(ins)
    kinds.wait()
    put_order(kind_ref, order, spatial)
    early = early_any.shape[1]
    outs = []
    for i in range(2):
        ins[i].wait()
        for h in range(spatial):
            into = early_any.at[i, h] if h < early else late_any.at[i, h - early]
            outs.append(
                pltpu.make_async_copy(held.at[i, :, lanes(order[h])], into, sems.at[i, h])
            )
            outs[-1].start()
    wait_all(outs)


def pack_call(head_kind, keys, values, spatial, late, block):
    return call(
        functools.partial(pack_kernel, spatial, block),
        "pack",
        [shape((2, n, 2 * block, HEAD_DIM)) for n in (spatial - late, late)],
        [ANY] * 3,
        [ANY] * 2,
        [
            pltpu.SMEM(head_kind.shape, jnp.int32),
            order_scratch(head_kind.shape[0]),
            pltpu.VMEM((2, 2 * block, keys.shape[1]), BF16),
            pltpu.SemaphoreType.DMA((2, spatial)),
            pltpu.SemaphoreType.DMA((3,)),
        ],
        (head_kind, keys, values),
        vmem=VMEM_PACK,
    )


def row_sums(ref, squares):
    rows, width = ref.shape
    size = HEAD_DIM
    for s in range(rows // size):
        total = None
        for c in range(width // HEAD_DIM):
            x = ref[s * size : (s + 1) * size, c * HEAD_DIM : (c + 1) * HEAD_DIM].astype(F32)
            total = x * x if total is None else total + x * x
        squares[s * size : (s + 1) * size, :] = total
    return jnp.sum(jnp.transpose(squares[...]), axis=0, keepdims=True)


def key_sums_kernel(k_ref, sums_ref, squares):
    sums_ref[...] = row_sums(k_ref, squares)


def sums_kernel(spatial, dealt, kind_ref, q_ref, k_ref, v_ref, key_sums_ref, sums_ref, *refs):
    order, squares = refs[-2:]
    put_order(kind_ref, order, spatial)
    sums_ref[0:1, :] = row_sums(q_ref, squares)
    sums_ref[1:2, :] = key_sums_ref[...]
    if dealt:
        one = lanes(order[spatial + 1 - Place().core])
        for i, ref in enumerate((q_ref, k_ref, v_ref)):
            refs[0][i] = ref[:, one]


def sums_call(head_kind, queries, keys, values, spatial, dealt):
    rows, width = queries.shape
    key_sums = call(
        key_sums_kernel,
        "key_sums",
        shape((1, rows), F32),
        [IN_VMEM],
        IN_VMEM,
        [pltpu.VMEM((rows, HEAD_DIM), F32)],
        (keys,),
        vmem=VMEM_SUMS,
    )
    outs = [shape((2, rows), F32)]
    if dealt:
        outs.append(shape((3, rows, HEAD_DIM)))
    return call(
        functools.partial(sums_kernel, spatial, dealt),
        "sums",
        outs,
        [IN_SMEM] + [IN_VMEM] * 4,
        [IN_VMEM] * len(outs),
        [order_scratch(head_kind.shape[0]), pltpu.VMEM((rows, HEAD_DIM), F32)],
        (head_kind, queries, keys, values, key_sums),
        vmem=VMEM_SUMS,
    )


def row_factors(sums, which, start, size):
    total = None
    for part in sums:
        row = part[which : which + 1, pl.ds(start, size)]
        total = row if total is None else total + row
    inverse = lax.rsqrt(total / D + 1e-06)
    return jnp.transpose(jnp.broadcast_to(inverse, (HEAD_DIM, size)))


def gain_of(gain_ref, head):
    gain = gain_ref[lanes(head)]
    return jnp.broadcast_to(gain[None, :], (8, HEAD_DIM))[0:1, :]


def own_kernel(spatial, dealt, afters, kind_ref, q_ref, k_ref, v_ref, gq_ref, gk_ref, total_ref, *refs):
    ks_ref, (order, factors) = refs[afters], refs[-2:]
    rows = k_ref.shape[0]
    put_order(kind_ref, order, spatial)
    place = Place()
    factors[...] = row_factors([total_ref], 1, 0, rows)
    for h in range(spatial):
        gain = gain_of(gk_ref, order[h])
        ks_ref[h] = (k_ref[:, lanes(order[h])].astype(F32) * factors[...] * gain).astype(BF16)
    if dealt:
        t_ref = refs[afters + 1]
        head = order[spatial + place.core]
        one = lanes(head)
        scale = row_factors([total_ref], 0, 0, rows)
        t_ref[0] = (q_ref[:, one].astype(F32) * scale * (gain_of(gq_ref, head) * FACTOR)).astype(BF16)
        t_ref[1] = (k_ref[:, one].astype(F32) * factors[...] * gain_of(gk_ref, head)).astype(BF16)
        t_ref[2] = v_ref[:, one]


def own_call(head_kind, queries, keys, values, query_gain, key_gain, total, afters, spatial, dealt):
    rows = keys.shape[0]
    outs = [shape((spatial, rows, HEAD_DIM))]
    if dealt:
        outs.append(shape((3, rows, HEAD_DIM)))
    return call(
        functools.partial(own_kernel, spatial, dealt, len(afters)),
        "own",
        outs,
        [IN_SMEM] + [IN_VMEM] * 6 + [LOOSE] * len(afters),
        [IN_VMEM] * len(outs),
        [order_scratch(head_kind.shape[0]), pltpu.VMEM((rows, HEAD_DIM), F32)],
        (head_kind, queries, keys, values, query_gain, key_gain, total, *afters),
    )


def pair_kernel(spatial, kind_ref, k_ref, gain_ref, sums_ref, after_ref, kp_ref, order, factors):
    put_order(kind_ref, order, spatial)
    factors[...] = row_factors([sums_ref], 1, 0, k_ref.shape[0])
    for h in range(spatial):
        gain = gain_of(gain_ref, order[h])
        kp_ref[h] = (k_ref[:, lanes(order[h])].astype(F32) * factors[...] * gain).astype(BF16)


def pair_call(head_kind, keys, gain, sums, after, spatial):
    rows = keys.shape[0]
    return call(
        functools.partial(pair_kernel, spatial),
        "pair",
        shape((spatial, rows, HEAD_DIM)),
        [IN_SMEM] + [IN_VMEM] * 3 + [LOOSE],
        IN_VMEM,
        [order_scratch(head_kind.shape[0]), pltpu.VMEM((rows, HEAD_DIM), F32)],
        (head_kind, keys, gain, sums, after),
    )


def attend_all(work, query_of, keys_of, values_of, put):
    def scores_of(item):
        parts = [
            lax.dot_general(query_of(*item), k, (((1,), (1,)), ((), ())), preferred_element_type=F32)
            for k in keys_of(*item)
        ]
        return jnp.concatenate(parts, axis=1)

    scores = scores_of(work[0])
    for n, item in enumerate(work):
        ahead = scores_of(work[n + 1]) if n + 1 < len(work) else None
        top = jnp.max(scores, axis=1, keepdims=True)
        weights = jnp.exp2(scores - top).astype(BF16)
        value = jnp.concatenate(values_of(*item), axis=0)
        wide = jnp.concatenate([value, jnp.ones_like(value)], axis=1)
        total = jnp.dot(weights, wide, preferred_element_type=F32)
        put(item, (total[:, :HEAD_DIM] / total[:, HEAD_DIM:]).astype(BF16))
        scores = ahead


def query_part(q_ref, gain_ref, factors, head, start, size, part):
    rows = pl.ds(pl.multiple_of(start + part * size, size), size)
    gain = gain_of(gain_ref, head) * FACTOR
    scale = factors[part * size : (part + 1) * size, :]
    return (q_ref[rows, lanes(head)].astype(F32) * scale * gain).astype(BF16)


def near_kernel(spatial, block, kind_ref, q_ref, k_ref, v_ref, kp_ref, v_pair_ref, gain_ref, total_ref, out_ref, order, factors):
    put_order(kind_ref, order, spatial)
    place = Place(block)
    one = pl.ds(pl.multiple_of(place.apart, block), block)
    factors[...] = row_factors([total_ref], 0, pl.multiple_of(place.near, block), block)

    def both(own_ref, pair_ref):
        return (
            jnp.where(place.inner, own_ref[...], pair_ref[...]),
            jnp.where(place.inner, pair_ref[one, :], own_ref[one, :]),
        )

    def values_of(h):
        head = lanes(order[h])
        return both(v_ref.at[:, head], v_pair_ref.at[:, head])

    def put(item, result):
        out_ref[item[0]] = result

    attend_all(
        [(h,) for h in range(spatial)],
        lambda h: query_part(q_ref, gain_ref, factors, order[h], place.near, block, 0),
        lambda h: both(k_ref.at[h], kp_ref.at[h]),
        values_of,
        put,
    )


def near_call(head_kind, q, k, v, k_pair, v_pair, gain, total, spatial, block):
    return call(
        functools.partial(near_kernel, spatial, block),
        "near",
        shape((spatial, block, HEAD_DIM)),
        [IN_SMEM] + [IN_VMEM] * 7,
        IN_VMEM,
        [order_scratch(head_kind.shape[0]), pltpu.VMEM((block, HEAD_DIM), F32)],
        (head_kind, q, k, v, k_pair, v_pair, gain, total),
    )


def far_attention(first, count, block, place, order, refs, put):
    q_ref, k_ref, v_ref, kp_ref, v_pair_ref, gq_ref, gk_ref, total_ref, cross_ref, *refs = refs
    kvx_refs, (factors, x_factors, x_keys) = refs[:-3], refs[-3:]
    early = kvx_refs[0].shape[1]

    def crossed(i, n):
        return kvx_refs[0][i, n] if n < early else kvx_refs[1][i, n - early]

    one = pl.ds(pl.multiple_of(place.apart, block), block)
    start = jnp.where(place.inner, 0, place.far)
    two = pl.ds(pl.multiple_of(start, block), 2 * block)
    factors[...] = row_factors([total_ref], 0, pl.multiple_of(place.far, block), 2 * block)
    sent = pl.multiple_of(jnp.where(place.kind == 0, block, 0), block)
    x_factors[...] = row_factors([cross_ref], 1, sent, 2 * block)

    def three(own_ref, pair_ref, cross):
        return (
            own_ref[two, :],
            jnp.where(place.inner, own_ref[2 * block :, :], cross[:block]),
            jnp.where(place.inner, pair_ref[one, :], cross[block:]),
        )

    def keys_of(h, part):
        n = first + h
        if part == 0:
            gain = gain_of(gk_ref, order[n])
            x_keys[h % 2] = (crossed(0, n).astype(F32) * x_factors[...] * gain).astype(BF16)
        return three(k_ref.at[n], kp_ref.at[n], x_keys[h % 2])

    def values_of(h, part):
        head = lanes(order[first + h])
        return three(v_ref.at[:, head], v_pair_ref.at[:, head], crossed(1, first + h))

    attend_all(
        [(h, part) for h in range(count) for part in range(2)],
        lambda h, part: query_part(q_ref, gq_ref, factors, order[first + h], place.far, block, part),
        keys_of,
        values_of,
        put,
    )


def far_kernel(spatial, first, count, block, kind_ref, *refs):
    operands, (out_ref, order, factors, x_factors, x_keys) = refs[:-6], refs[-5:]
    put_order(kind_ref, order, spatial)
    place = Place(block)

    def put(item, result):
        h, part = item
        out_ref[h, part * block : (part + 1) * block, :] = result

    far_attention(first, count, block, place, order, operands + (factors, x_factors, x_keys), put)


def far_call(head_kind, operands, after, first, count, spatial, block):
    return call(
        functools.partial(far_kernel, spatial, first, count, block),
        "far",
        shape((count, 2 * block, HEAD_DIM)),
        [IN_SMEM] + [IN_VMEM] * len(operands) + [LOOSE],
        IN_VMEM,
        [order_scratch(head_kind.shape[0])]
        + [pltpu.VMEM((2 * block, HEAD_DIM), F32)] * 2
        + [pltpu.VMEM((2, 2 * block, HEAD_DIM), BF16)],
        (head_kind, *operands, after),
    )


def rest_kernel(spatial, first, count, block, given, kind_ref, *refs):
    operands, refs = refs[:given], refs[given:]
    near_ref, far_ref, mid_ref, out_ref, order, factors, x_factors, x_keys, done, sems = refs
    put_order(kind_ref, order, spatial)
    place = Place(block)
    near_rows = pl.ds(pl.multiple_of(place.near, block), block)
    far_rows = pl.ds(pl.multiple_of(place.far, block), 2 * block)
    copies = []

    def send(source, head, rows):
        copies.append(
            pltpu.make_async_copy(source, column(out_ref, head, rows), sems.at[len(copies)])
        )
        copies[-1].start()

    waiting = [(near_ref.at[h], order[h], near_rows) for h in range(spatial)]
    for at, ref in ((0, far_ref), (far_ref.shape[0], mid_ref)):
        waiting += [(ref.at[h], order[at + h], far_rows) for h in range(ref.shape[0])]
    some = -(-len(waiting) // (2 * count - 1))

    def put(item, result):
        h, part = item
        done[h, part * block : (part + 1) * block, :] = result
        if part == 1:
            send(done.at[h], order[first + h], far_rows)
        for _ in range(min(some, len(waiting))):
            send(*waiting.pop(0))

    far_attention(first, count, block, place, order, operands + (factors, x_factors, x_keys), put)
    wait_all(copies)


def rest_call(head_kind, operands, near, far, mid, first, count, spatial, block):
    rows, width = operands[0].shape
    heads = head_kind.shape[0]
    return call(
        functools.partial(rest_kernel, spatial, first, count, block, len(operands)),
        "rest",
        shape((rows, width)),
        [IN_SMEM] + [IN_VMEM] * (len(operands) + 3),
        ANY,
        [
            order_scratch(heads),
            pltpu.VMEM((2 * block, HEAD_DIM), F32),
            pltpu.VMEM((2 * block, HEAD_DIM), F32),
            pltpu.VMEM((2, 2 * block, HEAD_DIM), BF16),
            pltpu.VMEM((count, 2 * block, HEAD_DIM), BF16),
            pltpu.SemaphoreType.DMA((2 * spatial,)),
        ],
        (head_kind, *operands, near, far, mid),
    )


def place_kernel(spatial, block, parts, kind_ref, *refs):
    t_refs, (_, out_ref, order, held, sems) = refs[:parts], refs[parts:]
    put_order(kind_ref, order, spatial)
    place = Place(block)
    rows = 3 * block
    copies = []

    def send(source, head):
        copies.append(
            pltpu.make_async_copy(source, column(out_ref, head), sems.at[len(copies)])
        )
        copies[-1].start()

    if parts == 2 * CHIPS:
        for j in range(2):
            for turn in range(CHIPS):
                for g in range(TURNS):
                    piece = (place.chip ^ turn) + CHIPS * g
                    into = pl.ds(pl.multiple_of(piece * PIECE, PIECE), PIECE)
                    held[j, into, :] = t_refs[j * CHIPS + turn][g]
            own = pl.ds(pl.multiple_of(place.core * rows, block), rows)
            send(held.at[j, own], order[spatial + (place.core ^ j)])
    else:
        for j in range(parts):
            send(t_refs[j], order[spatial + j])
    wait_all(copies)


def place_call(head_kind, parts, have, spatial, block):
    heads = head_kind.shape[0]
    return call(
        functools.partial(place_kernel, spatial, block, len(parts)),
        "place",
        shape(have.shape),
        [IN_SMEM] + [IN_VMEM] * len(parts) + [ANY],
        ANY,
        [
            order_scratch(heads),
            pltpu.VMEM((2, 2 * have.shape[0], HEAD_DIM), BF16),
            pltpu.SemaphoreType.DMA((heads - spatial,)),
        ],
        (head_kind, *parts, have),
        aliases={1 + len(parts): 0},
    )


PIECE = 128
CHIPS = 4
TURNS = 3


def deal_kernel(spatial, block, kind_ref, own_ref, got_ref, gq_ref, gk_ref, sums_ref, *refs):
    outs, (order, held) = refs[:CHIPS], refs[CHIPS:]
    put_order(kind_ref, order, spatial)
    place = Place(block)
    rows = own_ref.shape[1]
    head = order[spatial + place.core]
    own = pl.ds(pl.multiple_of(place.core * rows, rows), rows)
    other = pl.ds(pl.multiple_of((1 - place.core) * rows, rows), rows)
    gains = (gain_of(gq_ref, head) * FACTOR, gain_of(gk_ref, head))
    for i in range(2):
        factors = row_factors([sums_ref], i, 0, rows)
        held[i, other, :] = (got_ref[i].astype(F32) * factors * gains[i]).astype(BF16)
    held[2, other, :] = got_ref[2]
    for i in range(3):
        held[i, own, :] = own_ref[i]
    for turn in range(CHIPS):
        owner = place.chip ^ turn
        for g in range(TURNS):
            at = pl.multiple_of((owner + CHIPS * g) * PIECE, PIECE)
            for i in range(3):
                outs[turn][i, g] = held[i, pl.ds(at, PIECE), :]


def deal_call(head_kind, own, got, query_gain, key_gain, sums, spatial, block):
    return call(
        functools.partial(deal_kernel, spatial, block),
        "deal",
        [shape((3, TURNS, PIECE, HEAD_DIM))] * CHIPS,
        [IN_SMEM] + [IN_VMEM] * 5,
        [IN_VMEM] * CHIPS,
        [
            order_scratch(head_kind.shape[0]),
            pltpu.VMEM((3, 2 * own.shape[1], HEAD_DIM), BF16),
        ],
        (head_kind, own, got, query_gain, key_gain, sums),
    )


GROUPS = (
    ((0, 1), (2, 1), (1, 0), (1, 2), (3, 0), (3, 2)),
    ((0, 0), (0, 2), (2, 0), (2, 2), (1, 1), (3, 1)),
)


def frames_kernel(*refs):
    ins, outs = refs[:CHIPS], refs[-CHIPS:]
    side = len(GROUPS[0]) * PIECE
    row = lax.broadcasted_iota(jnp.int32, (PIECE, PIECE), 0)
    col = lax.broadcasted_iota(jnp.int32, (PIECE, PIECE), 1)
    same = jnp.tile(row == col, (1, len(GROUPS[0])))
    half = side // 2
    work = [(n, part) for n in range(len(GROUPS)) for part in range(2)]
    query, key, value = (
        [jnp.concatenate([ins[s][i, g] for s, g in group], axis=0) for group in GROUPS]
        for i in range(3)
    )
    same = jnp.concatenate([same] * (half // PIECE), axis=0)

    def scores_of(n, part):
        return lax.dot_general(
            query[n][part * half : (part + 1) * half],
            key[n],
            (((1,), (1,)), ((), ())),
            preferred_element_type=F32,
        )

    scores = scores_of(*work[0])
    for at, (n, part) in enumerate(work):
        ahead = scores_of(*work[at + 1]) if at + 1 < len(work) else None
        scores = jnp.where(same, scores, LOW)
        top = jnp.max(scores, axis=1, keepdims=True)
        weights = jnp.exp2(scores - top).astype(BF16)
        wide = jnp.concatenate([value[n], jnp.ones_like(value[n])], axis=1)
        total = jnp.dot(weights, wide, preferred_element_type=F32)
        done = (total[:, :HEAD_DIM] / total[:, HEAD_DIM:]).astype(BF16)
        for i in range(half // PIECE):
            s, g = GROUPS[n][part * (half // PIECE) + i]
            outs[s][g] = done[i * PIECE : (i + 1) * PIECE]
        scores = ahead


def frames_call(parts, after):
    return call(
        frames_kernel,
        "frames",
        [shape((TURNS, PIECE, HEAD_DIM))] * CHIPS,
        [IN_VMEM] * CHIPS + [LOOSE],
        [IN_VMEM] * CHIPS,
        [],
        (*parts, after),
        cycles=FRAMES_COST,
    )


def temporal_folded(queries, keys, values, query_gain, key_gain, head_kind, total, spatial, first):
    rows = queries.shape[0]
    heads = head_kind.shape[0]
    count = heads - spatial
    ids = jnp.argsort(head_kind, stable=True)[spatial:]
    take = lambda x: jnp.take(x.reshape(-1, heads, HEAD_DIM), ids, axis=1)
    inverse = lax.rsqrt(total / D + 1e-06)[:, :, None, None]
    norm = lambda x, i, gain: (take(x).astype(F32) * inverse[i] * take(gain)).astype(BF16)
    query = norm(queries, 0, query_gain * FACTOR).astype(F32)
    flat = lambda x: lax.all_gather(x.reshape(rows, -1), "seq", axis=0, tiled=True)
    key_all = flat(norm(keys, 1, key_gain))
    value_all = flat(take(values))
    place = (first + jnp.arange(rows, dtype=jnp.int32)) % FRAME
    running = jnp.full((rows, count), LOW, F32)
    summed = jnp.zeros((rows, count), F32)
    result = jnp.zeros((rows, count, HEAD_DIM), F32)
    for step in range(key_all.shape[0] // FRAME):
        at = place + step * FRAME
        key = jnp.take(key_all, at, axis=0).reshape(rows, count, HEAD_DIM).astype(F32)
        value = jnp.take(value_all, at, axis=0).reshape(rows, count, HEAD_DIM).astype(F32)
        scores = jnp.sum(query * key, axis=2)
        newest = jnp.maximum(running, scores)
        shrink = jnp.exp2(running - newest)
        weight = jnp.exp2(scores - newest)
        summed = summed * shrink + weight
        result = result * shrink[:, :, None] + weight[:, :, None] * value
        running = newest
    done = (result / summed[:, :, None]).astype(BF16)
    return [done[:, j] for j in range(count)]


def per_device(queries, keys, values, query_gain, key_gain, head_kind):
    rows = queries.shape[0]
    heads = head_kind.shape[0]
    temporal = heads // 5
    spatial = heads - temporal
    block = rows // 3
    devices = lax.axis_size("seq")
    planes = lax.axis_size("head")
    dealt = temporal == 2 and devices == 2 * CHIPS and rows == 6 * PIECE
    pair = [(i, i ^ 1) for i in range(devices)]
    cross = []
    for i in range(3, devices, 4):
        after = (i + 1) % devices
        cross += [(i, after), (after, i)]
    turned = [[(i, i ^ (2 * turn)) for i in range(devices)] for turn in range(1, CHIPS)]
    send = lambda x, route: lax.ppermute(x, "seq", route)

    late = spatial // LATE
    kv_near, kv_late = pack_call(head_kind, keys, values, spatial, late, block)
    kv_cross = send(kv_near, cross)
    sums, *t_send = sums_call(head_kind, queries, keys, values, spatial, dealt)
    k_pair = send(lax.optimization_barrier((keys, kv_near))[0], pair)
    v_pair = send(lax.optimization_barrier((values, kv_near))[0], pair)
    t_got = [send(part, pair) for part in t_send]
    total = sums
    if planes & (planes - 1) == 0:
        for d in [1 << n for n in range(planes.bit_length() - 1)]:
            total = total + lax.ppermute(total, "head", [(i, i ^ d) for i in range(planes)])
    else:
        total = lax.psum(sums, "head")
    pair_total = send(total, pair)
    cross_total = lax.ppermute(
        total,
        ("seq", "head"),
        [(i * planes + p, j * planes + (p ^ 1)) for i, j in cross for p in range(planes)],
    )
    k, *t_own = own_call(
        head_kind, queries, keys, values, query_gain, key_gain, total, t_got, spatial, dealt
    )
    last = k
    if dealt:
        pieces = deal_call(
            head_kind, t_own[0], t_got[0], query_gain, key_gain, pair_total, spatial, block
        )
        arrived = [pieces[0]] + [send(p, r) for p, r in zip(pieces[1:], turned)]
        last = pieces[0]
    kp = pair_call(head_kind, k_pair, key_gain, pair_total, last, spatial)
    near = near_call(
        head_kind, queries, k, values, kp, v_pair, query_gain, total, spatial, block
    )
    operands = (queries, k, values, kp, v_pair, query_gain, key_gain, total, cross_total, kv_cross)
    ahead = (3 * spatial) // 8
    far = far_call(head_kind, operands, near, 0, ahead, spatial, block)
    late_cross = send(lax.optimization_barrier((kv_late, far))[0], cross)
    last = far
    if dealt:
        results = frames_call(arrived, far)
        parts = [send(p, r) for p, r in zip(results[:0:-1], turned[::-1])]
        parts = [results[0]] + parts[::-1]
        last = results[0]
    mid = far_call(
        head_kind, operands, last, ahead, spatial - ahead - late, spatial, block
    )
    out = rest_call(
        head_kind, operands + (late_cross,), near, far, mid, spatial - late, late, spatial, block
    )
    if dealt:
        parts += [send(parts[0], pair)] + [
            send(lax.optimization_barrier((p, out))[0], pair) for p in parts[1:]
        ]
    else:
        index = lax.axis_index("seq").astype(jnp.int32)
        parts = temporal_folded(
            queries, keys, values, query_gain, key_gain, head_kind, total, spatial, index * rows
        )
    return place_call(head_kind, parts, out, spatial, block)


def solution(mesh):
    placed = (P("seq", "head"), P("seq", "head"), P("seq", "head"), P("head"), P("head"), P("head"))
    return jax.shard_map(
        per_device, mesh=mesh, in_specs=placed, out_specs=P("seq", "head"), check_vma=False
    )
```

```python
import functools
import math

import jax
import jax.numpy as jnp
from jax import lax
from jax.experimental import pallas as pl
from jax.experimental.pallas import tpu as pltpu
from jax.sharding import PartitionSpec as P

HEAD_DIM = 128
D = 5120
FRAME = 1024
OFFSET = 512
VMEM = 24 * 1024 * 1024
VMEM_PACK = 58 * 1024 * 1024
VMEM_SUMS = 32 * 1024 * 1024
LOW = -1e30
LATE = 4
FRAMES_COST = 10000000000
FACTOR = math.log2(math.e) / math.sqrt(HEAD_DIM)
F32 = jnp.float32
BF16 = jnp.bfloat16
ANY = pl.BlockSpec(memory_space=pltpu.HBM)
LOOSE = pl.BlockSpec(memory_space=pl.ANY)
IN_SMEM = pl.BlockSpec(memory_space=pltpu.SMEM)
IN_VMEM = pl.BlockSpec(memory_space=pltpu.VMEM)


def shape(dims, dtype=BF16):
    return jax.ShapeDtypeStruct(dims, dtype)


def call(kernel, name, out_shape, in_specs, out_specs, scratch, operands, aliases=None, cycles=1000, vmem=VMEM):
    return pl.pallas_call(
        kernel,
        out_shape=out_shape,
        in_specs=in_specs,
        out_specs=out_specs,
        scratch_shapes=scratch,
        input_output_aliases=aliases or {},
        compiler_params=pltpu.CompilerParams(vmem_limit_bytes=vmem),
        cost_estimate=pl.CostEstimate(flops=cycles, bytes_accessed=1000, transcendentals=0),
        name=name,
    )(*operands)


def column(ref, head, rows=None):
    lanes = pl.ds(pl.multiple_of(head * HEAD_DIM, HEAD_DIM), HEAD_DIM)
    return ref.at[:, lanes] if rows is None else ref.at[rows, lanes]


def put_order(kind_ref, order_ref, spatial):
    heads = kind_ref.shape[0]

    def step(h, count):
        s, t = count
        temporal = kind_ref[h] == 1
        order_ref[jnp.where(temporal, spatial + t, s)] = h
        return jnp.where(temporal, s, s + 1), jnp.where(temporal, t + 1, t)

    lax.fori_loop(0, heads, step, (jnp.int32(0), jnp.int32(0)))


def order_scratch(heads):
    return pltpu.SMEM((heads,), jnp.int32)


class Place:
    def __init__(self, block=1):
        index = lax.axis_index("seq").astype(jnp.int32)
        self.kind = index % 4
        self.core = index % 2
        self.chip = index // 2
        self.inner = (self.kind == 1) | (self.kind == 2)
        self.apart = jnp.where((self.kind == 0) | (self.kind == 1), 2 * block, 0)
        self.near = jnp.where(self.kind == 0, 2 * block, 0)
        self.far = jnp.where(self.kind == 0, 0, block)
        self.cross = jnp.where(self.kind == 0, 0, block)


def lanes(head):
    return pl.ds(pl.multiple_of(head * HEAD_DIM, HEAD_DIM), HEAD_DIM)


def start_all(copies):
    for copy in copies:
        copy.start()


def wait_all(copies):
    for copy in copies:
        copy.wait()


def pack_kernel(spatial, block, kind_any, k_any, v_any, early_any, late_any, kind_ref, order, held, sems, in_sems):
    place = Place(block)
    across = pl.ds(pl.multiple_of(place.cross, block), 2 * block)
    ins = [
        pltpu.make_async_copy(ref.at[across, :], held.at[i], in_sems.at[i])
        for i, ref in enumerate((k_any, v_any))
    ]
    kinds = pltpu.make_async_copy(kind_any, kind_ref, in_sems.at[2])
    start_all(ins)
    kinds.start()
    kinds.wait()
    put_order(kind_ref, order, spatial)
    early = early_any.shape[1]
    outs = []
    for i in range(2):
        ins[i].wait()
        for h in range(spatial):
            into = early_any.at[i, h] if h < early else late_any.at[i, h - early]
            outs.append(
                pltpu.make_async_copy(held.at[i, :, lanes(order[h])], into, sems.at[i, h])
            )
            outs[-1].start()
    wait_all(outs)


def pack_call(head_kind, keys, values, spatial, late, block):
    return call(
        functools.partial(pack_kernel, spatial, block),
        "pack",
        [shape((2, n, 2 * block, HEAD_DIM)) for n in (spatial - late, late)],
        [ANY] * 3,
        [ANY] * 2,
        [
            pltpu.SMEM(head_kind.shape, jnp.int32),
            order_scratch(head_kind.shape[0]),
            pltpu.VMEM((2, 2 * block, keys.shape[1]), BF16),
            pltpu.SemaphoreType.DMA((2, spatial)),
            pltpu.SemaphoreType.DMA((3,)),
        ],
        (head_kind, keys, values),
        vmem=VMEM_PACK,
    )


def row_sums(ref, squares):
    rows, width = ref.shape
    size = HEAD_DIM
    for s in range(rows // size):
        total = None
        for c in range(width // HEAD_DIM):
            x = ref[s * size : (s + 1) * size, c * HEAD_DIM : (c + 1) * HEAD_DIM].astype(F32)
            total = x * x if total is None else total + x * x
        squares[s * size : (s + 1) * size, :] = total
    return jnp.sum(jnp.transpose(squares[...]), axis=0, keepdims=True)


def key_sums_kernel(k_ref, sums_ref, squares):
    sums_ref[...] = row_sums(k_ref, squares)


def sums_kernel(spatial, dealt, kind_ref, q_ref, k_ref, v_ref, key_sums_ref, sums_ref, *refs):
    order, squares = refs[-2:]
    put_order(kind_ref, order, spatial)
    sums_ref[0:1, :] = row_sums(q_ref, squares)
    sums_ref[1:2, :] = key_sums_ref[...]
    if dealt:
        one = lanes(order[spatial + 1 - Place().core])
        for i, ref in enumerate((q_ref, k_ref, v_ref)):
            refs[0][i] = ref[:, one]


def sums_call(head_kind, queries, keys, values, spatial, dealt):
    rows, width = queries.shape
    key_sums = call(
        key_sums_kernel,
        "key_sums",
        shape((1, rows), F32),
        [IN_VMEM],
        IN_VMEM,
        [pltpu.VMEM((rows, HEAD_DIM), F32)],
        (keys,),
        vmem=VMEM_SUMS,
    )
    outs = [shape((2, rows), F32)]
    if dealt:
        outs.append(shape((3, rows, HEAD_DIM)))
    return call(
        functools.partial(sums_kernel, spatial, dealt),
        "sums",
        outs,
        [IN_SMEM] + [IN_VMEM] * 4,
        [IN_VMEM] * len(outs),
        [order_scratch(head_kind.shape[0]), pltpu.VMEM((rows, HEAD_DIM), F32)],
        (head_kind, queries, keys, values, key_sums),
        vmem=VMEM_SUMS,
    )


def row_factors(sums, which, start, size):
    total = None
    for part in sums:
        row = part[which : which + 1, pl.ds(start, size)]
        total = row if total is None else total + row
    inverse = lax.rsqrt(total / D + 1e-06)
    return jnp.transpose(jnp.broadcast_to(inverse, (HEAD_DIM, size)))


def gain_of(gain_ref, head):
    gain = gain_ref[lanes(head)]
    return jnp.broadcast_to(gain[None, :], (8, HEAD_DIM))[0:1, :]


def own_kernel(spatial, dealt, afters, kind_ref, q_ref, k_ref, v_ref, gq_ref, gk_ref, total_ref, *refs):
    ks_ref, (order, factors) = refs[afters], refs[-2:]
    rows = k_ref.shape[0]
    put_order(kind_ref, order, spatial)
    place = Place()
    factors[...] = row_factors([total_ref], 1, 0, rows)
    for h in range(spatial):
        gain = gain_of(gk_ref, order[h])
        ks_ref[h] = (k_ref[:, lanes(order[h])].astype(F32) * factors[...] * gain).astype(BF16)
    if dealt:
        t_ref = refs[afters + 1]
        head = order[spatial + place.core]
        one = lanes(head)
        scale = row_factors([total_ref], 0, 0, rows)
        t_ref[0] = (q_ref[:, one].astype(F32) * scale * (gain_of(gq_ref, head) * FACTOR)).astype(BF16)
        t_ref[1] = (k_ref[:, one].astype(F32) * factors[...] * gain_of(gk_ref, head)).astype(BF16)
        t_ref[2] = v_ref[:, one]


def own_call(head_kind, queries, keys, values, query_gain, key_gain, total, afters, spatial, dealt):
    rows = keys.shape[0]
    outs = [shape((spatial, rows, HEAD_DIM))]
    if dealt:
        outs.append(shape((3, rows, HEAD_DIM)))
    return call(
        functools.partial(own_kernel, spatial, dealt, len(afters)),
        "own",
        outs,
        [IN_SMEM] + [IN_VMEM] * 6 + [LOOSE] * len(afters),
        [IN_VMEM] * len(outs),
        [order_scratch(head_kind.shape[0]), pltpu.VMEM((rows, HEAD_DIM), F32)],
        (head_kind, queries, keys, values, query_gain, key_gain, total, *afters),
    )


def pair_kernel(spatial, kind_ref, k_ref, gain_ref, sums_ref, after_ref, kp_ref, order, factors):
    put_order(kind_ref, order, spatial)
    factors[...] = row_factors([sums_ref], 1, 0, k_ref.shape[0])
    for h in range(spatial):
        gain = gain_of(gain_ref, order[h])
        kp_ref[h] = (k_ref[:, lanes(order[h])].astype(F32) * factors[...] * gain).astype(BF16)


def pair_call(head_kind, keys, gain, sums, after, spatial):
    rows = keys.shape[0]
    return call(
        functools.partial(pair_kernel, spatial),
        "pair",
        shape((spatial, rows, HEAD_DIM)),
        [IN_SMEM] + [IN_VMEM] * 3 + [LOOSE],
        IN_VMEM,
        [order_scratch(head_kind.shape[0]), pltpu.VMEM((rows, HEAD_DIM), F32)],
        (head_kind, keys, gain, sums, after),
    )


def attend_all(work, query_of, keys_of, values_of, put):
    def scores_of(item):
        parts = [
            lax.dot_general(query_of(*item), k, (((1,), (1,)), ((), ())), preferred_element_type=F32)
            for k in keys_of(*item)
        ]
        return jnp.concatenate(parts, axis=1)

    scores = scores_of(work[0])
    for n, item in enumerate(work):
        ahead = scores_of(work[n + 1]) if n + 1 < len(work) else None
        top = jnp.max(scores, axis=1, keepdims=True)
        weights = jnp.exp2(scores - top).astype(BF16)
        value = jnp.concatenate(values_of(*item), axis=0)
        wide = jnp.concatenate([value, jnp.ones_like(value)], axis=1)
        total = jnp.dot(weights, wide, preferred_element_type=F32)
        put(item, (total[:, :HEAD_DIM] / total[:, HEAD_DIM:]).astype(BF16))
        scores = ahead


def query_part(q_ref, gain_ref, factors, head, start, size, part):
    rows = pl.ds(pl.multiple_of(start + part * size, size), size)
    gain = gain_of(gain_ref, head) * FACTOR
    scale = factors[part * size : (part + 1) * size, :]
    return (q_ref[rows, lanes(head)].astype(F32) * scale * gain).astype(BF16)


def near_kernel(spatial, block, kind_ref, q_ref, k_ref, v_ref, kp_ref, v_pair_ref, gain_ref, total_ref, out_ref, order, factors):
    put_order(kind_ref, order, spatial)
    place = Place(block)
    one = pl.ds(pl.multiple_of(place.apart, block), block)
    factors[...] = row_factors([total_ref], 0, pl.multiple_of(place.near, block), block)

    def both(own_ref, pair_ref):
        return (
            jnp.where(place.inner, own_ref[...], pair_ref[...]),
            jnp.where(place.inner, pair_ref[one, :], own_ref[one, :]),
        )

    def values_of(h):
        head = lanes(order[h])
        return both(v_ref.at[:, head], v_pair_ref.at[:, head])

    def put(item, result):
        out_ref[item[0]] = result

    attend_all(
        [(h,) for h in range(spatial)],
        lambda h: query_part(q_ref, gain_ref, factors, order[h], place.near, block, 0),
        lambda h: both(k_ref.at[h], kp_ref.at[h]),
        values_of,
        put,
    )


def near_call(head_kind, q, k, v, k_pair, v_pair, gain, total, spatial, block):
    return call(
        functools.partial(near_kernel, spatial, block),
        "near",
        shape((spatial, block, HEAD_DIM)),
        [IN_SMEM] + [IN_VMEM] * 7,
        IN_VMEM,
        [order_scratch(head_kind.shape[0]), pltpu.VMEM((block, HEAD_DIM), F32)],
        (head_kind, q, k, v, k_pair, v_pair, gain, total),
    )


def far_attention(first, count, block, place, order, refs, put):
    q_ref, k_ref, v_ref, kp_ref, v_pair_ref, gq_ref, gk_ref, total_ref, cross_ref, *refs = refs
    kvx_refs, (factors, x_factors, x_keys) = refs[:-3], refs[-3:]
    early = kvx_refs[0].shape[1]

    def crossed(i, n):
        return kvx_refs[0][i, n] if n < early else kvx_refs[1][i, n - early]

    one = pl.ds(pl.multiple_of(place.apart, block), block)
    start = jnp.where(place.inner, 0, place.far)
    two = pl.ds(pl.multiple_of(start, block), 2 * block)
    factors[...] = row_factors([total_ref], 0, pl.multiple_of(place.far, block), 2 * block)
    sent = pl.multiple_of(jnp.where(place.kind == 0, block, 0), block)
    x_factors[...] = row_factors([cross_ref], 1, sent, 2 * block)

    def three(own_ref, pair_ref, cross):
        return (
            own_ref[two, :],
            jnp.where(place.inner, own_ref[2 * block :, :], cross[:block]),
            jnp.where(place.inner, pair_ref[one, :], cross[block:]),
        )

    def keys_of(h, part):
        n = first + h
        if part == 0:
            gain = gain_of(gk_ref, order[n])
            x_keys[h % 2] = (crossed(0, n).astype(F32) * x_factors[...] * gain).astype(BF16)
        return three(k_ref.at[n], kp_ref.at[n], x_keys[h % 2])

    def values_of(h, part):
        head = lanes(order[first + h])
        return three(v_ref.at[:, head], v_pair_ref.at[:, head], crossed(1, first + h))

    attend_all(
        [(h, part) for h in range(count) for part in range(2)],
        lambda h, part: query_part(q_ref, gq_ref, factors, order[first + h], place.far, block, part),
        keys_of,
        values_of,
        put,
    )


def far_kernel(spatial, first, count, block, kind_ref, *refs):
    operands, (out_ref, order, factors, x_factors, x_keys) = refs[:-6], refs[-5:]
    put_order(kind_ref, order, spatial)
    place = Place(block)

    def put(item, result):
        h, part = item
        out_ref[h, part * block : (part + 1) * block, :] = result

    far_attention(first, count, block, place, order, operands + (factors, x_factors, x_keys), put)


def far_call(head_kind, operands, after, first, count, spatial, block):
    return call(
        functools.partial(far_kernel, spatial, first, count, block),
        "far",
        shape((count, 2 * block, HEAD_DIM)),
        [IN_SMEM] + [IN_VMEM] * len(operands) + [LOOSE],
        IN_VMEM,
        [order_scratch(head_kind.shape[0])]
        + [pltpu.VMEM((2 * block, HEAD_DIM), F32)] * 2
        + [pltpu.VMEM((2, 2 * block, HEAD_DIM), BF16)],
        (head_kind, *operands, after),
    )


def rest_kernel(spatial, first, count, block, given, kind_ref, *refs):
    operands, refs = refs[:given], refs[given:]
    near_ref, far_ref, mid_ref, out_ref, order, factors, x_factors, x_keys, done, sems = refs
    put_order(kind_ref, order, spatial)
    place = Place(block)
    near_rows = pl.ds(pl.multiple_of(place.near, block), block)
    far_rows = pl.ds(pl.multiple_of(place.far, block), 2 * block)
    copies = []

    def send(source, head, rows):
        copies.append(
            pltpu.make_async_copy(source, column(out_ref, head, rows), sems.at[len(copies)])
        )
        copies[-1].start()

    waiting = [(near_ref.at[h], order[h], near_rows) for h in range(spatial)]
    for at, ref in ((0, far_ref), (far_ref.shape[0], mid_ref)):
        waiting += [(ref.at[h], order[at + h], far_rows) for h in range(ref.shape[0])]
    some = -(-len(waiting) // (2 * count - 1))

    def put(item, result):
        h, part = item
        done[h, part * block : (part + 1) * block, :] = result
        if part == 1:
            send(done.at[h], order[first + h], far_rows)
        for _ in range(min(some, len(waiting))):
            send(*waiting.pop(0))

    far_attention(first, count, block, place, order, operands + (factors, x_factors, x_keys), put)
    wait_all(copies)


def rest_call(head_kind, operands, near, far, mid, first, count, spatial, block):
    rows, width = operands[0].shape
    heads = head_kind.shape[0]
    return call(
        functools.partial(rest_kernel, spatial, first, count, block, len(operands)),
        "rest",
        shape((rows, width)),
        [IN_SMEM] + [IN_VMEM] * (len(operands) + 3),
        ANY,
        [
            order_scratch(heads),
            pltpu.VMEM((2 * block, HEAD_DIM), F32),
            pltpu.VMEM((2 * block, HEAD_DIM), F32),
            pltpu.VMEM((2, 2 * block, HEAD_DIM), BF16),
            pltpu.VMEM((count, 2 * block, HEAD_DIM), BF16),
            pltpu.SemaphoreType.DMA((2 * spatial,)),
        ],
        (head_kind, *operands, near, far, mid),
    )


def place_kernel(spatial, block, parts, kind_ref, *refs):
    t_refs, (_, out_ref, order, held, sems) = refs[:parts], refs[parts:]
    put_order(kind_ref, order, spatial)
    place = Place(block)
    rows = 3 * block
    copies = []

    def send(source, head):
        copies.append(
            pltpu.make_async_copy(source, column(out_ref, head), sems.at[len(copies)])
        )
        copies[-1].start()

    if parts == 2 * CHIPS:
        for j in range(2):
            for turn in range(CHIPS):
                for g in range(TURNS):
                    piece = (place.chip ^ turn) + CHIPS * g
                    into = pl.ds(pl.multiple_of(piece * PIECE, PIECE), PIECE)
                    held[j, into, :] = t_refs[j * CHIPS + turn][g]
            own = pl.ds(pl.multiple_of(place.core * rows, block), rows)
            send(held.at[j, own], order[spatial + (place.core ^ j)])
    else:
        for j in range(parts):
            send(t_refs[j], order[spatial + j])
    wait_all(copies)


def place_call(head_kind, parts, have, spatial, block):
    heads = head_kind.shape[0]
    return call(
        functools.partial(place_kernel, spatial, block, len(parts)),
        "place",
        shape(have.shape),
        [IN_SMEM] + [IN_VMEM] * len(parts) + [ANY],
        ANY,
        [
            order_scratch(heads),
            pltpu.VMEM((2, 2 * have.shape[0], HEAD_DIM), BF16),
            pltpu.SemaphoreType.DMA((heads - spatial,)),
        ],
        (head_kind, *parts, have),
        aliases={1 + len(parts): 0},
    )


PIECE = 128
CHIPS = 4
TURNS = 3


def deal_kernel(spatial, block, kind_ref, own_ref, got_ref, gq_ref, gk_ref, sums_ref, *refs):
    outs, (order, held) = refs[:CHIPS], refs[CHIPS:]
    put_order(kind_ref, order, spatial)
    place = Place(block)
    rows = own_ref.shape[1]
    head = order[spatial + place.core]
    own = pl.ds(pl.multiple_of(place.core * rows, rows), rows)
    other = pl.ds(pl.multiple_of((1 - place.core) * rows, rows), rows)
    gains = (gain_of(gq_ref, head) * FACTOR, gain_of(gk_ref, head))
    for i in range(2):
        factors = row_factors([sums_ref], i, 0, rows)
        held[i, other, :] = (got_ref[i].astype(F32) * factors * gains[i]).astype(BF16)
    held[2, other, :] = got_ref[2]
    for i in range(3):
        held[i, own, :] = own_ref[i]
    for turn in range(CHIPS):
        owner = place.chip ^ turn
        for g in range(TURNS):
            at = pl.multiple_of((owner + CHIPS * g) * PIECE, PIECE)
            for i in range(3):
                outs[turn][i, g] = held[i, pl.ds(at, PIECE), :]


def deal_call(head_kind, own, got, query_gain, key_gain, sums, spatial, block):
    return call(
        functools.partial(deal_kernel, spatial, block),
        "deal",
        [shape((3, TURNS, PIECE, HEAD_DIM))] * CHIPS,
        [IN_SMEM] + [IN_VMEM] * 5,
        [IN_VMEM] * CHIPS,
        [
            order_scratch(head_kind.shape[0]),
            pltpu.VMEM((3, 2 * own.shape[1], HEAD_DIM), BF16),
        ],
        (head_kind, own, got, query_gain, key_gain, sums),
    )


GROUPS = (
    ((0, 1), (2, 1), (1, 0), (1, 2), (3, 0), (3, 2)),
    ((0, 0), (0, 2), (2, 0), (2, 2), (1, 1), (3, 1)),
)


def frames_kernel(*refs):
    ins, outs = refs[:CHIPS], refs[-CHIPS:]
    side = len(GROUPS[0]) * PIECE
    row = lax.broadcasted_iota(jnp.int32, (PIECE, PIECE), 0)
    col = lax.broadcasted_iota(jnp.int32, (PIECE, PIECE), 1)
    same = jnp.tile(row == col, (1, len(GROUPS[0])))
    half = side // 2
    work = [(n, part) for n in range(len(GROUPS)) for part in range(2)]
    query, key, value = (
        [jnp.concatenate([ins[s][i, g] for s, g in group], axis=0) for group in GROUPS]
        for i in range(3)
    )
    same = jnp.concatenate([same] * (half // PIECE), axis=0)

    def scores_of(n, part):
        return lax.dot_general(
            query[n][part * half : (part + 1) * half],
            key[n],
            (((1,), (1,)), ((), ())),
            preferred_element_type=F32,
        )

    scores = scores_of(*work[0])
    for at, (n, part) in enumerate(work):
        ahead = scores_of(*work[at + 1]) if at + 1 < len(work) else None
        scores = jnp.where(same, scores, LOW)
        top = jnp.max(scores, axis=1, keepdims=True)
        weights = jnp.exp2(scores - top).astype(BF16)
        wide = jnp.concatenate([value[n], jnp.ones_like(value[n])], axis=1)
        total = jnp.dot(weights, wide, preferred_element_type=F32)
        done = (total[:, :HEAD_DIM] / total[:, HEAD_DIM:]).astype(BF16)
        for i in range(half // PIECE):
            s, g = GROUPS[n][part * (half // PIECE) + i]
            outs[s][g] = done[i * PIECE : (i + 1) * PIECE]
        scores = ahead


def frames_call(parts, after):
    return call(
        frames_kernel,
        "frames",
        [shape((TURNS, PIECE, HEAD_DIM))] * CHIPS,
        [IN_VMEM] * CHIPS + [LOOSE],
        [IN_VMEM] * CHIPS,
        [],
        (*parts, after),
        cycles=FRAMES_COST,
    )


def temporal_folded(queries, keys, values, query_gain, key_gain, head_kind, total, spatial, first):
    rows = queries.shape[0]
    heads = head_kind.shape[0]
    count = heads - spatial
    ids = jnp.argsort(head_kind, stable=True)[spatial:]
    take = lambda x: jnp.take(x.reshape(-1, heads, HEAD_DIM), ids, axis=1)
    inverse = lax.rsqrt(total / D + 1e-06)[:, :, None, None]
    norm = lambda x, i, gain: (take(x).astype(F32) * inverse[i] * take(gain)).astype(BF16)
    query = norm(queries, 0, query_gain * FACTOR).astype(F32)
    flat = lambda x: lax.all_gather(x.reshape(rows, -1), "seq", axis=0, tiled=True)
    key_all = flat(norm(keys, 1, key_gain))
    value_all = flat(take(values))
    place = (first + jnp.arange(rows, dtype=jnp.int32)) % FRAME
    running = jnp.full((rows, count), LOW, F32)
    summed = jnp.zeros((rows, count), F32)
    result = jnp.zeros((rows, count, HEAD_DIM), F32)
    for step in range(key_all.shape[0] // FRAME):
        at = place + step * FRAME
        key = jnp.take(key_all, at, axis=0).reshape(rows, count, HEAD_DIM).astype(F32)
        value = jnp.take(value_all, at, axis=0).reshape(rows, count, HEAD_DIM).astype(F32)
        scores = jnp.sum(query * key, axis=2)
        newest = jnp.maximum(running, scores)
        shrink = jnp.exp2(running - newest)
        weight = jnp.exp2(scores - newest)
        summed = summed * shrink + weight
        result = result * shrink[:, :, None] + weight[:, :, None] * value
        running = newest
    done = (result / summed[:, :, None]).astype(BF16)
    return [done[:, j] for j in range(count)]


def per_device(queries, keys, values, query_gain, key_gain, head_kind):
    rows = queries.shape[0]
    heads = head_kind.shape[0]
    temporal = heads // 5
    spatial = heads - temporal
    block = rows // 3
    devices = lax.axis_size("seq")
    planes = lax.axis_size("head")
    dealt = temporal == 2 and devices == 2 * CHIPS and rows == 6 * PIECE
    pair = [(i, i ^ 1) for i in range(devices)]
    cross = []
    for i in range(3, devices, 4):
        after = (i + 1) % devices
        cross += [(i, after), (after, i)]
    turned = [[(i, i ^ (2 * turn)) for i in range(devices)] for turn in range(1, CHIPS)]
    send = lambda x, route: lax.ppermute(x, "seq", route)

    late = spatial // LATE
    kv_near, kv_late = pack_call(head_kind, keys, values, spatial, late, block)
    kv_cross = send(kv_near, cross)
    sums, *t_send = sums_call(head_kind, queries, keys, values, spatial, dealt)
    k_pair = send(lax.optimization_barrier((keys, kv_near))[0], pair)
    v_pair = send(lax.optimization_barrier((values, kv_near))[0], pair)
    t_got = [send(part, pair) for part in t_send]
    total = sums
    if planes & (planes - 1) == 0:
        for d in [1 << n for n in range(planes.bit_length() - 1)]:
            total = total + lax.ppermute(total, "head", [(i, i ^ d) for i in range(planes)])
    else:
        total = lax.psum(sums, "head")
    pair_total = send(total, pair)
    cross_total = lax.ppermute(
        total,
        ("seq", "head"),
        [(i * planes + p, j * planes + (p ^ 1)) for i, j in cross for p in range(planes)],
    )
    k, *t_own = own_call(
        head_kind, queries, keys, values, query_gain, key_gain, total, t_got, spatial, dealt
    )
    last = k
    if dealt:
        pieces = deal_call(
            head_kind, t_own[0], t_got[0], query_gain, key_gain, pair_total, spatial, block
        )
        arrived = [pieces[0]] + [send(p, r) for p, r in zip(pieces[1:], turned)]
        last = pieces[0]
    kp = pair_call(head_kind, k_pair, key_gain, pair_total, last, spatial)
    near = near_call(
        head_kind, queries, k, values, kp, v_pair, query_gain, total, spatial, block
    )
    operands = (queries, k, values, kp, v_pair, query_gain, key_gain, total, cross_total, kv_cross)
    ahead = (3 * spatial) // 8
    far = far_call(head_kind, operands, near, 0, ahead, spatial, block)
    late_cross = send(lax.optimization_barrier((kv_late, far))[0], cross)
    last = far
    if dealt:
        results = frames_call(arrived, far)
        parts = [results[0]] + [send(p, r) for p, r in zip(results[1:], turned)]
        last = results[0]
    mid = far_call(
        head_kind, operands, last, ahead, spatial - ahead - late, spatial, block
    )
    out = rest_call(
        head_kind, operands + (late_cross,), near, far, mid, spatial - late, late, spatial, block
    )
    if dealt:
        parts += [send(parts[0], pair)] + [
            send(lax.optimization_barrier((p, out))[0], pair) for p in parts[1:]
        ]
    else:
        index = lax.axis_index("seq").astype(jnp.int32)
        parts = temporal_folded(
            queries, keys, values, query_gain, key_gain, head_kind, total, spatial, index * rows
        )
    return place_call(head_kind, parts, out, spatial, block)


def solution(mesh):
    placed = (P("seq", "head"), P("seq", "head"), P("seq", "head"), P("head"), P("head"), P("head"))
    return jax.shard_map(
        per_device, mesh=mesh, in_specs=placed, out_specs=P("seq", "head"), check_vma=False
    )
```
